128 devices in a mesh: lon: 16 (over y, z_lo, core), lat: 8 (over x, z_hi).
Axes of the slice: x: 4, y: 4, z: 4 (z_hi: 2, z_lo: 2; z = z_hi * 2 + z_lo), core: 2. Of those that a mesh axis runs over, the one named last changes fastest.
Arguments:
- ocean_state: float32 [4, 4, 1024, 16384], P(None, None, 'lat', 'lon'), may hold values from -3 to 3
- depth_levels: int32 [1024, 16384], P('lat', 'lon'), may hold values from 0 to 4
- vert_mix: float32 [4, 1024, 16384], P(None, 'lat', 'lon'), may hold values from 0.1 to 4
- partner: int32 [16384], P('lon'), may hold values from 0 to 16383, as said below
- ice_velocity: float32 [2, 1024, 16384], P(None, 'lat', 'lon'), may hold values from -4 to 4
- ice_mass: float32 [1024, 16384], P('lat', 'lon'), may hold values from 0.2 to 2
- ice_strength: float32 [1024, 16384], P('lat', 'lon'), may hold values from 0.2 to 2
- ice_mask: int32 [1024, 16384], P('lat', 'lon'), may hold values 0 or 1
- ice_owned: int32 [8, 16, 3], P('lat', 'lon'), may hold values from -1 to 127, as said below
Outputs:
- new_tracers: float32 [2, 4, 1024, 16384], P(None, None, 'lat', 'lon')
- new_ice_velocity: float32 [2, 1024, 16384], P(None, 'lat', 'lon')
The draws below stay inside these ranges and needn't reach their ends.
Inputs may be any that keep to these rules, and one draw needn't show every extreme that they name: partner[i] = (s - i) mod 16384 for one s drawn afresh; the partner of a column's partner is the column itself. `ice_owned`: entry [r, d, k] is -1 or a tile column of tile row r that lies on lon index (d - k) mod 16, that is, one of the 8 tile columns from ((d - k) mod 16) * 8 on; each tile column appears at most once in a row; in every row some lon index has all 3 slots filled and some lon index has none.
All inputs are finite; a program needn't handle non-finite values. No bound on the sum of `ice_mask` on one device may be relied on, other than what follows from the above.
Results may differ from the reference program's by a relative error of at most 0.0003.
Values sent between devices are 32-bit elements; how exact they have to be, the bound alone decides.
A program may use at most 192 MiB of HBM per device.

```python
import math
import jax
import jax.numpy as jnp
from jax import lax

LEV = 4
TILE = 128
CX = 1024
OWN_MOST = 3
SUBCYCLES = 32
NY = 1024
NX = 16384
N_LON = 16


def draw_partner(key, part):
    offset = jax.random.randint(key, (), 0, NX)
    return jnp.mod(offset - jnp.arange(NX, dtype=jnp.int32), NX).astype(jnp.int32)


def draw_ice_owned(key, part):
    tile_rows = NY // TILE
    tiles_dev = CX // TILE

    def one_row(row_key):
        sub_keys = jax.random.split(row_key, 4)
        start = jax.random.randint(sub_keys[0], (), 0, N_LON)
        run_length = jax.random.randint(sub_keys[1], (), OWN_MOST, N_LON // 2 + 1)
        orders = jax.vmap(lambda one_key: jax.random.permutation(one_key, tiles_dev).astype(jnp.int32))(jax.random.split(sub_keys[2], N_LON))
        owner_ids = jnp.arange(N_LON, dtype=jnp.int32)[:, None]
        slot_ids = jnp.arange(OWN_MOST, dtype=jnp.int32)[None, :]
        source = jnp.mod(owner_ids - slot_ids, N_LON)
        picked = jnp.take_along_axis(orders[:, :OWN_MOST], jnp.broadcast_to(slot_ids, (N_LON, OWN_MOST)), axis=1)
        local_pick = jnp.stack([picked[source[:, slot_id], slot_id] for slot_id in range(OWN_MOST)], axis=1)
        columns = source * tiles_dev + local_pick
        in_run = jnp.mod(source - start, N_LON) < run_length
        kept = in_run & (jax.random.randint(sub_keys[3], (N_LON, OWN_MOST), 0, 4) < 3)
        forced = jnp.mod(start + OWN_MOST - 1, N_LON)
        kept = kept | (owner_ids == forced) & in_run
        return jnp.where(kept, columns, -1).astype(jnp.int32)
    return jax.vmap(one_row)(jax.random.split(key, tile_rows)).astype(jnp.int32)


def place_ends(values, rng, least, top_value):
    shape = values.shape
    index_at = [jax.random.randint(jax.random.fold_in(rng, axis), (), 0, shape[axis]) for axis in range(len(shape))]
    values = values.at[tuple(index_at)].set(least)
    longest = shape.index(max(shape))
    index_at[longest] = (index_at[longest] + 1) % shape[longest]
    return values.at[tuple(index_at)].set(top_value)


def block_scale(own_key, dims, pieces, smallest, largest):
    level, own = 1.0, jax.random.fold_in(own_key, 6)
    for axis_at, parts in pieces:
        heights = jnp.exp(jax.random.uniform(jax.random.fold_in(own, axis_at), (parts,), jnp.float32, smallest / len(pieces), largest / len(pieces)))
        level = level * jnp.repeat(heights, dims[axis_at] // parts).reshape([-1 if axis == axis_at else 1 for axis in range(len(dims))])
    return level


def noise(key, dims, deviation, bound, pieces=(), kind=jnp.bfloat16):
    drawn = deviation * jax.random.normal(key, dims, jnp.float32)
    if pieces:
        drawn = drawn * block_scale(key, dims, pieces, -0.22, 0.18)
    return jnp.clip(drawn, -bound, bound).astype(kind)


def setup_inputs(seed: int = 0) -> dict:
    seeds = jax.random.split(jax.random.key(seed), 10)
    return {
        "ocean_state": noise(seeds[0], (4, LEV, NY, NX), 1.0, 3.0, ((2, 8), (3, 16)), jnp.float32),
        "depth_levels": place_ends(jax.random.randint(seeds[1], (NY, NX), 0, LEV + 1), jax.random.fold_in(seeds[1], 1), 0, LEV).astype(jnp.int32),
        "vert_mix": jnp.clip(jnp.exp(math.log(4.0) - 3.6888794 * jax.random.uniform(seeds[2], (LEV, NY, NX), jnp.float32) ** block_scale(seeds[2], (LEV, NY, NX), ((1, 8), (2, 16)), -0.2, 0.2)), 0.1, 4.0),
        "partner": draw_partner(jax.random.fold_in(seeds[9], 71), 0),
        "ice_velocity": noise(seeds[4], (2, NY, NX), 1.0, 4.0, ((1, 8), (2, 16)), jnp.float32),
        "ice_mass": jnp.clip(jnp.exp(math.log(2.0) - 2.3025851 * jax.random.uniform(seeds[5], (NY, NX), jnp.float32) ** block_scale(seeds[5], (NY, NX), ((0, 8), (1, 16)), -0.2, 0.2)), 0.2, 2.0),
        "ice_strength": jnp.clip(jnp.exp(math.log(2.0) - 2.3025851 * jax.random.uniform(seeds[6], (NY, NX), jnp.float32) ** block_scale(seeds[6], (NY, NX), ((0, 8), (1, 16)), -0.2, 0.2)), 0.2, 2.0),
        "ice_mask": place_ends((jax.random.randint(seeds[7], (NY, NX), 0, 4) < 3).astype(jnp.int32), jax.random.fold_in(seeds[7], 1), 0, 1),
        "ice_owned": draw_ice_owned(jax.random.fold_in(seeds[9], 71), 0),
    }


TIME_STEP = 0.25
MIX_HORIZ = 0.5
RELAX_RATE = 0.5
ECC_FACTOR = 0.25
DELTA_FLOOR_SQ = 0.25
INV_ICE_STEP = 2.0
WATER_DRAG = 1.0
CORIOLIS_PARAM = 0.5

def shift_ahead(values, which_dim):
    if which_dim == -1:
        return jnp.concatenate([values[..., 1:], jnp.zeros_like(values[..., :1])], axis=-1)
    return jnp.concatenate([values[..., 1:, :], jnp.zeros_like(values[..., :1, :])], axis=-2)

def shift_behind(values, which_dim):
    if which_dim == -1:
        return jnp.concatenate([jnp.zeros_like(values[..., :1]), values[..., :-1]], axis=-1)
    return jnp.concatenate([jnp.zeros_like(values[..., :1, :]), values[..., :-1, :]], axis=-2)

def ice_subcycles(vel_east, vel_north, mass_ice, strength, ocean_east, ocean_north):
    inertia = mass_ice * INV_ICE_STEP
    diag_coef = inertia + WATER_DRAG
    turning = CORIOLIS_PARAM * mass_ice
    denominator = diag_coef * diag_coef + turning * turning

    def one_cycle(cycle_id, carry):
        vel_east, vel_north, stress_sum, stress_diff, stress_shear = carry
        grad_east_u = shift_ahead(vel_east, -1) - vel_east
        grad_north_v = shift_ahead(vel_north, -2) - vel_north
        grad_north_u = shift_ahead(vel_east, -2) - vel_east
        grad_east_v = shift_ahead(vel_north, -1) - vel_north
        divergence = grad_east_u + grad_north_v
        tension = grad_east_u - grad_north_v
        shearing = grad_north_u + grad_east_v
        deform = jnp.sqrt(divergence * divergence + ECC_FACTOR * (tension * tension + shearing * shearing) + DELTA_FLOOR_SQ)
        pressure_ratio = strength / deform
        stress_sum = (stress_sum + RELAX_RATE * (pressure_ratio * divergence - strength)) / (1.0 + RELAX_RATE)
        stress_diff = (stress_diff + RELAX_RATE * ECC_FACTOR * pressure_ratio * tension) / (1.0 + RELAX_RATE)
        stress_shear = (stress_shear + RELAX_RATE * ECC_FACTOR * pressure_ratio * shearing) / (1.0 + RELAX_RATE)
        stress_xx = 0.5 * (stress_sum + stress_diff)
        stress_yy = 0.5 * (stress_sum - stress_diff)
        force_east = stress_xx - shift_behind(stress_xx, -1) + stress_shear - shift_behind(stress_shear, -2)
        force_north = stress_shear - shift_behind(stress_shear, -1) + stress_yy - shift_behind(stress_yy, -2)
        rhs_east = inertia * vel_east + force_east + WATER_DRAG * ocean_east
        rhs_north = inertia * vel_north + force_north + WATER_DRAG * ocean_north
        new_east = (diag_coef * rhs_east + turning * rhs_north) / denominator
        new_north = (diag_coef * rhs_north - turning * rhs_east) / denominator
        return (new_east, new_north, stress_sum, stress_diff, stress_shear)
    zeros = jnp.zeros_like(vel_east)
    result = lax.fori_loop(0, SUBCYCLES, one_cycle, (vel_east, vel_north, zeros, zeros, zeros))
    return (result[0], result[1])

def ocean_update(tracer_pad, east_pad, north_pad, depth_pad, vert_mix):
    level_count = vert_mix.shape[0]
    level_ids = jnp.arange(level_count, dtype=jnp.float32)[:, None, None]
    wet_pad = (level_ids < depth_pad[None]).astype(jnp.float32)
    wet_here = wet_pad[:, 1:-1, 1:-1]
    open_east = wet_here * wet_pad[:, 1:-1, 2:]
    open_west = wet_here * wet_pad[:, 1:-1, :-2]
    open_north = wet_here * wet_pad[:, 2:, 1:-1]
    open_south = wet_here * wet_pad[:, :-2, 1:-1]
    centre = tracer_pad[:, :, 1:-1, 1:-1]
    east_val = tracer_pad[:, :, 1:-1, 2:]
    west_val = tracer_pad[:, :, 1:-1, :-2]
    north_val = tracer_pad[:, :, 2:, 1:-1]
    south_val = tracer_pad[:, :, :-2, 1:-1]
    vel_east = east_pad[:, 1:-1, 1:-1]
    vel_west_face = east_pad[:, 1:-1, :-2]
    vel_north = north_pad[:, 1:-1, 1:-1]
    vel_south_face = north_pad[:, :-2, 1:-1]
    flux_east = (jnp.maximum(vel_east, 0.0) * centre + jnp.minimum(vel_east, 0.0) * east_val) * open_east
    flux_west = (jnp.maximum(vel_west_face, 0.0) * west_val + jnp.minimum(vel_west_face, 0.0) * centre) * open_west
    flux_north = (jnp.maximum(vel_north, 0.0) * centre + jnp.minimum(vel_north, 0.0) * north_val) * open_north
    flux_south = (jnp.maximum(vel_south_face, 0.0) * south_val + jnp.minimum(vel_south_face, 0.0) * centre) * open_south
    laplace = open_east * (east_val - centre) + open_west * (west_val - centre) + open_north * (north_val - centre) + open_south * (south_val - centre)
    interim = centre + TIME_STEP * (MIX_HORIZ * laplace - (flux_east - flux_west + flux_north - flux_south))
    coupling = [None] + [TIME_STEP * vert_mix[level_id] * wet_here[level_id] for level_id in range(1, level_count)]
    surface = TIME_STEP * vert_mix[0] * wet_here[0]
    upper_mod = []
    rhs_mod = []
    for level_id in range(level_count):
        diagonal = 1.0 + (surface if level_id == 0 else coupling[level_id])
        if level_id + 1 < level_count:
            diagonal = diagonal + coupling[level_id + 1]
        rhs_now = interim[:, level_id]
        if level_id > 0:
            lower_coef = -coupling[level_id]
            diagonal = diagonal - lower_coef * upper_mod[level_id - 1]
            rhs_now = rhs_now - lower_coef * rhs_mod[level_id - 1]
        if level_id + 1 < level_count:
            upper_mod.append(-coupling[level_id + 1] / diagonal)
        else:
            upper_mod.append(None)
        rhs_mod.append(rhs_now / diagonal)
    solved = [None] * level_count
    solved[level_count - 1] = rhs_mod[level_count - 1]
    for level_id in range(level_count - 2, -1, -1):
        solved[level_id] = rhs_mod[level_id] - upper_mod[level_id] * solved[level_id + 1]
    return jnp.stack(solved, axis=1)

def pad_grid(values, partner):
    north_row = jnp.take(values[..., -1:, :], partner, axis=-1)
    south_row = jnp.zeros_like(values[..., :1, :])
    extended = jnp.concatenate([south_row, values, north_row], axis=-2)
    return jnp.concatenate([extended[..., -1:], extended, extended[..., :1]], axis=-1)

def reference(ocean_state, depth_levels, vert_mix, partner, ice_velocity, ice_mass, ice_strength, ice_mask, ice_owned):
    depths = depth_levels.astype(jnp.float32)
    padded_state = pad_grid(ocean_state, partner)
    depth_pad = pad_grid(depths, partner)
    new_tracers = ocean_update(padded_state[0:2], padded_state[2], padded_state[3], depth_pad, vert_mix)
    ice_cover = ice_mask.astype(jnp.float32) * (depth_levels > 0).astype(jnp.float32)
    tile_rows = NY // TILE
    tile_cols = NX // TILE

    def to_tiles(values):
        return values.reshape(tile_rows, TILE, tile_cols, TILE).transpose(0, 2, 1, 3)

    def from_tiles(values):
        return values.transpose(0, 2, 1, 3).reshape(NY, NX)
    old_east = to_tiles(ice_velocity[0])
    old_north = to_tiles(ice_velocity[1])
    new_east, new_north = ice_subcycles(old_east, old_north, to_tiles(ice_mass * ice_cover), to_tiles(ice_strength * ice_cover), to_tiles(ocean_state[2, 0]), to_tiles(ocean_state[3, 0]))
    listed = jnp.any(ice_owned[:, :, :, None] == jnp.arange(tile_cols, dtype=jnp.int32)[None, None, None, :], axis=(1, 2))
    east_out = jnp.where(listed[:, :, None, None], new_east, old_east)
    north_out = jnp.where(listed[:, :, None, None], new_north, old_north)
    return (new_tracers, jnp.stack([from_tiles(east_out), from_tiles(north_out)]))
```

```python
import jax
import jax.numpy as jnp
from jax import lax
from jax.experimental import pallas as pl
from jax.experimental.pallas import tpu as pltpu
from jax.sharding import PartitionSpec as P

MESH = pl.DeviceIdType.MESH
LEV = 4
TILE = 128
ROWS = 128
COLS = 1024
LT = COLS // TILE
SLOTS = 3
SUBCYCLES = 32
NB = ROWS // 8
F32 = jnp.float32
I32 = jnp.int32


def iotas():
    lane = lax.broadcasted_iota(I32, (8, 128), 1)
    row = lax.broadcasted_iota(I32, (8, 128), 0)
    return lane, row


def ice_tile(pos, slot, ue_v, un_v, mass_v, str_v, mask_v, depth_v, uo_v, vo_v, stage, con, st, res_ref):
    lane, row = iotas()
    for b in range(NB):
        rows = slice(b * 8, b * 8 + 8)
        mass, strength = mass_v[pos, rows, :], str_v[pos, rows, :]
        ice = jnp.logical_and(mask_v[pos, rows, :] > 0, depth_v[pos, rows, :] > 0)
        stage[0, rows, :] = ue_v[pos, rows, :]
        stage[1, rows, :] = un_v[pos, rows, :]
        stage[2, rows, :] = jnp.where(ice, mass, 0.0)
        stage[3, rows, :] = jnp.where(ice, strength, 0.0)
        stage[4, rows, :] = uo_v[pos, rows, :]
        stage[5, rows, :] = vo_v[pos, rows, :]

    def strided(f, k):
        return stage[f, pl.ds(k, 8, stride=NB), :]

    p_south = None
    for k in range(NB):
        m = strided(2, k)
        strength = strided(3, k)
        inertia = m * 2.0
        a = inertia + 1.0
        b = m * 0.5
        inv = 1.0 / (a * a + b * b)
        p4 = strength * 0.25
        if k == 0:
            p_south = jnp.where(row == 0, 0.0, pltpu.roll(strided(3, NB - 1) * 0.25, 1, 0))
        p_west = jnp.where(lane == 0, 0.0, pltpu.roll(p4, 1, 1))
        con[0, k] = inertia
        con[1, k] = a * inv
        con[2, k] = b * inv
        con[3, k] = strength * (1.0 / 12.0)
        con[4, k] = strided(4, k) * 0.5 - (p4 - p_west)
        con[5, k] = strided(5, k) * 0.5 - (p4 - p_south)
        st[0, k] = strided(0, k) * 0.5
        st[1, k] = strided(1, k) * 0.5
        st[2, k] = p4
        st[3, k] = p4
        st[4, k] = jnp.zeros((8, 128), F32)
        p_south = p4

    keep = 1.0 / 1.5

    def momentum(k, u, v, sx, sy, sh, sy_s, sh_s):
        sx_w = jnp.where(lane == 0, 0.0, pltpu.roll(sx, 1, 1))
        sh_w = jnp.where(lane == 0, 0.0, pltpu.roll(sh, 1, 1))
        rx = (con[0, k] * u + con[4, k]) + ((sx - sx_w) + (sh - sh_s))
        ry = (con[0, k] * v + con[5, k]) + ((sh - sh_w) + (sy - sy_s))
        al, be = con[1, k], con[2, k]
        st[0, k] = al * rx + be * ry
        st[1, k] = al * ry - be * rx

    def cycle(_, carry):
        un, vn = st[0, 0], st[1, 0]
        u0, v0 = un, vn
        first = None
        sy_s = sh_s = None
        for k in range(NB):
            u, v = un, vn
            if k < NB - 1:
                un, vn = st[0, k + 1], st[1, k + 1]
            else:
                un = jnp.where(row == 7, 0.0, pltpu.roll(u0, 7, 0))
                vn = jnp.where(row == 7, 0.0, pltpu.roll(v0, 7, 0))
            ue = jnp.where(lane == 127, 0.0, pltpu.roll(u, 127, 1))
            ve = jnp.where(lane == 127, 0.0, pltpu.roll(v, 127, 1))
            d1 = ue - u
            d2 = vn - v
            h = (un - u) + (ve - v)
            div = d1 + d2
            ten = d1 - d2
            p = div + div
            r = ten * 0.5
            x = (p * p + ten * ten) + (h * h + 0.25)
            q = con[3, k] * lax.rsqrt(x)
            sx = st[2, k] * keep + q * (p + r)
            sy = st[3, k] * keep + q * (p - r)
            sh = st[4, k] * keep + q * h
            st[2, k] = sx
            st[3, k] = sy
            st[4, k] = sh
            if k == 0:
                first = (u, v, sx, sy, sh)
            else:
                momentum(k, u, v, sx, sy, sh, sy_s, sh_s)
            sy_s, sh_s = sy, sh
        sy_s = jnp.where(row == 0, 0.0, pltpu.roll(sy_s, 1, 0))
        sh_s = jnp.where(row == 0, 0.0, pltpu.roll(sh_s, 1, 0))
        momentum(0, *first, sy_s, sh_s)
        return carry

    lax.fori_loop(0, SUBCYCLES, cycle, 0)
    for k in range(NB):
        res_ref[slot, 0, pl.ds(k, 8, stride=NB), :] = st[0, k] * 2.0
        res_ref[slot, 1, pl.ds(k, 8, stride=NB), :] = st[1, k] * 2.0


def exchange_kernel(
    n_lon,
    n_lat,
    owned,
    state,
    depth,
    ivel,
    mass,
    strength,
    mask,
    he,
    hw,
    hs,
    hn,
    fold,
    res,
    info,
    depth_v,
    uo_v,
    vo_v,
    ue_v,
    un_v,
    mass_v,
    str_v,
    mask_v,
    col_first,
    col_last,
    blk_first,
    blk_last,
    pack_first,
    pack_last,
    pack_n,
    pack_s,
    pack_f,
    my_list,
    lists,
    lists_s,
    stage,
    con,
    st,
    load_sem,
    send_sem,
    recv_sem,
    fsend_sem,
    frecv_sem,
    local_sem,
    plane_sem,
):
    x = lax.axis_index("lon")
    y = lax.axis_index("lat")
    lane, row = iotas()
    top = y == n_lat - 1
    bottom = y == 0

    def lon(step):
        return {"lon": lax.rem(x + step + n_lon, n_lon), "lat": y}

    def lat(step):
        return {"lon": x, "lat": y + step}

    barrier = pltpu.get_barrier_semaphore()

    def greet(device):
        pl.semaphore_signal(barrier, inc=1, device_id=device, device_id_type=MESH)

    for step in (1, -1, 2, -2):
        greet(lon(step))

    @pl.when(top)
    def _():
        for step in range(3, n_lon - 2):
            greet(lon(step))

    @pl.when(jnp.logical_not(top))
    def _():
        greet(lat(1))

    @pl.when(jnp.logical_not(bottom))
    def _():
        greet(lat(-1))

    loads = [
        (state.at[0:2, :, :, pl.ds(0, 128)], col_first),
        (state.at[0:3, :, :, pl.ds(COLS - 128, 128)], col_last),
        (state.at[0:2, :, pl.ds(0, 8), :], blk_first),
        (state.at[0:2, :, pl.ds(ROWS - 8, 8), :], blk_last.at[0:2]),
        (state.at[3, :, pl.ds(ROWS - 8, 8), :], blk_last.at[2]),
    ]
    planes = [
        (depth, depth_v),
        (ivel.at[0], ue_v),
        (ivel.at[1], un_v),
        (mass, mass_v),
        (strength, str_v),
        (mask, mask_v),
        (state.at[2, 0], uo_v),
        (state.at[3, 0], vo_v),
    ]
    copies = [pltpu.make_async_copy(s, d, load_sem.at[i]) for i, (s, d) in enumerate(loads)]
    for i, (s, d) in enumerate(planes):
        if i == 1:
            for c in copies:
                c.start()
        for j in range(LT):
            pltpu.make_async_copy(s.at[:, j * 128 : j * 128 + 128], d.at[j], plane_sem.at[i]).start()

    def plane_wait(i):
        pltpu.make_async_copy(planes[i][1], planes[i][1], plane_sem.at[i]).wait()

    my_list[...] = jnp.where(
        lane == 0, owned[0, 0, 0], jnp.where(lane == 1, owned[0, 0, 1], owned[0, 0, 2])
    )

    plane_wait(0)
    for c in copies:
        c.wait()

    def pack_cols(b, carry):
        rows = pl.ds(pl.multiple_of(b * 8, 8), 8)
        first = jnp.zeros((8, 128), F32)
        last = jnp.zeros((8, 128), F32)
        for t in range(2):
            for k in range(LEV):
                n = t * LEV + k
                value = col_first[t, k, rows, :]
                first = jnp.where(lane == n, value if n == 0 else pltpu.roll(value, n, 1), first)
                last = jnp.where(lane == n, pltpu.roll(col_last[t, k, rows, :], n + 1, 1), last)
        d_first = depth_v[0, rows, :].astype(F32)
        d_last = depth_v[LT - 1, rows, :].astype(F32)
        first = jnp.where(lane == 8, pltpu.roll(d_first, 8, 1), first)
        last = jnp.where(lane == 8, pltpu.roll(d_last, 9, 1), last)
        for k in range(LEV):
            last = jnp.where(lane == 9 + k, pltpu.roll(col_last[2, k, rows, :], 10 + k, 1), last)
        pack_first[rows, :] = first
        pack_last[rows, :] = last
        return carry

    lax.fori_loop(0, NB, pack_cols, 0)
    pack_n[...] = jnp.zeros((16, COLS), F32)
    pack_s[...] = jnp.zeros((16, COLS), F32)
    for t in range(2):
        for k in range(LEV):
            n = t * LEV + k
            pack_n[n : n + 1, :] = blk_first[t, k, 0:1, :]
            pack_s[n : n + 1, :] = blk_last[t, k, 7:8, :]
    for k in range(LEV):
        pack_s[9 + k : 10 + k, :] = blk_last[2, k, 7:8, :]
    for j in range(LT):
        cols = slice(j * 128, j * 128 + 128)
        pack_n[8:9, cols] = depth_v[j, 0:8, :].astype(F32)[0:1, :]
        pack_s[8:9, cols] = depth_v[j, ROWS - 8 : ROWS, :].astype(F32)[7:8, :]
        pack_f[j] = pack_s[0:8, j * 128 : j * 128 + 128]
        pack_f[LT, j : j + 1, :] = pack_s[8:9, j * 128 : j * 128 + 128]

    @pl.when(jnp.logical_and(top, jnp.logical_not(bottom)))
    def _():
        pl.semaphore_wait(barrier, n_lon)

    @pl.when(jnp.logical_and(bottom, jnp.logical_not(top)))
    def _():
        pl.semaphore_wait(barrier, 5)

    @pl.when(jnp.logical_not(jnp.logical_or(bottom, top)))
    def _():
        pl.semaphore_wait(barrier, 6)

    def remote(src, dst, i, device):
        return pltpu.make_async_remote_copy(
            src_ref=src,
            dst_ref=dst,
            send_sem=send_sem.at[i],
            recv_sem=recv_sem.at[i],
            device_id=device,
            device_id_type=MESH,
        )

    list_1 = remote(my_list, lists.at[0], 0, lon(-1))
    list_2 = remote(my_list, lists.at[1], 1, lon(-2))
    to_west = remote(pack_first, he, 2, lon(-1))
    to_east = remote(pack_last, hw, 3, lon(1))
    to_south = remote(pack_n, hn, 4, lat(-1))
    to_north = remote(pack_s, hs, 5, lat(1))
    always = (list_1, list_2, to_west, to_east)
    for c in always:
        c.start()

    @pl.when(jnp.logical_not(bottom))
    def _():
        to_south.start()

    @pl.when(jnp.logical_not(top))
    def _():
        to_north.start()

    def fold_copy(step):
        return pltpu.make_async_remote_copy(
            src_ref=pack_f,
            dst_ref=fold.at[x],
            send_sem=fsend_sem.at[step],
            recv_sem=frecv_sem.at[x],
            device_id=lon(step),
            device_id_type=MESH,
        )

    def fold_arrival(step):
        source = lax.rem(x - step + n_lon, n_lon)
        return pltpu.make_async_remote_copy(
            src_ref=pack_f,
            dst_ref=fold.at[source],
            send_sem=fsend_sem.at[step],
            recv_sem=frecv_sem.at[source],
            device_id=lon(step),
            device_id_type=MESH,
        )

    own_fold = pltpu.make_async_copy(pack_f, fold.at[x], local_sem.at[0])

    @pl.when(top)
    def _():
        own_fold.start()
        for step in range(1, n_lon):
            fold_copy(step).start()

    for i in range(1, len(planes)):
        plane_wait(i)

    def work(column, slot):
        info[slot] = jnp.where(column >= 0, column - x * LT, -1)
        pos = jnp.clip(column - x * LT, 0, LT - 1)
        ice_tile(pos, slot, ue_v, un_v, mass_v, str_v, mask_v, depth_v, uo_v, vo_v, stage, con, st, res)

    work(owned[0, 0, 0], 0)
    list_1.wait_recv()
    list_2.wait_recv()
    to_smem = pltpu.make_async_copy(lists, lists_s, local_sem.at[1])
    to_smem.start()
    to_smem.wait()
    work(lists_s[0, 0, 1], 1)
    work(lists_s[1, 0, 2], 2)

    list_1.wait_send()
    list_2.wait_send()
    to_west.wait()
    to_east.wait()

    @pl.when(jnp.logical_not(bottom))
    def _():
        to_south.wait_send()
        to_north.wait_recv()

    @pl.when(jnp.logical_not(top))
    def _():
        to_north.wait_send()
        to_south.wait_recv()

    @pl.when(top)
    def _():
        own_fold.wait()
        for step in range(1, n_lon):
            fold_copy(step).wait_send()
        for step in range(1, n_lon):
            fold_arrival(step).wait_recv()


def exchange_and_ice(n_lon, n_lat, owned, state, depth, ivel, mass, strength, mask):
    anywhere = pl.BlockSpec(memory_space=pl.ANY)
    plane = pltpu.VMEM((LT, ROWS, 128), F32)
    plane_i = pltpu.VMEM((LT, ROWS, 128), I32)

    def body(*refs):
        exchange_kernel(n_lon, n_lat, *refs)

    return pl.pallas_call(
        body,
        name="exchange_and_ice",
        out_shape=(
            jax.ShapeDtypeStruct((ROWS, 128), F32),
            jax.ShapeDtypeStruct((ROWS, 128), F32),
            jax.ShapeDtypeStruct((16, COLS), F32),
            jax.ShapeDtypeStruct((16, COLS), F32),
            jax.ShapeDtypeStruct((n_lon, LT + 1, 8, 128), F32),
            jax.ShapeDtypeStruct((SLOTS, 2, TILE, TILE), F32),
            jax.ShapeDtypeStruct((SLOTS,), I32),
        ),
        in_specs=[pl.BlockSpec(memory_space=pltpu.SMEM)] + [anywhere] * 6,
        out_specs=(anywhere,) * 5
        + (pl.BlockSpec(memory_space=pltpu.VMEM), pl.BlockSpec(memory_space=pltpu.SMEM)),
        scratch_shapes=[
            plane_i,
            plane,
            plane,
            plane,
            plane,
            plane,
            plane,
            plane_i,
            pltpu.VMEM((2, LEV, ROWS, 128), F32),
            pltpu.VMEM((3, LEV, ROWS, 128), F32),
            pltpu.VMEM((2, LEV, 8, COLS), F32),
            pltpu.VMEM((3, LEV, 8, COLS), F32),
            pltpu.VMEM((ROWS, 128), F32),
            pltpu.VMEM((ROWS, 128), F32),
            pltpu.VMEM((16, COLS), F32),
            pltpu.VMEM((16, COLS), F32),
            pltpu.VMEM((LT + 1, 8, 128), F32),
            pltpu.VMEM((8, 128), I32),
            pltpu.VMEM((2, 8, 128), I32),
            pltpu.SMEM((2, 8, 128), I32),
            pltpu.VMEM((6, TILE, TILE), F32),
            pltpu.VMEM((6, NB, 8, 128), F32),
            pltpu.VMEM((5, NB, 8, 128), F32),
            pltpu.SemaphoreType.DMA((5,)),
            pltpu.SemaphoreType.DMA((6,)),
            pltpu.SemaphoreType.DMA((6,)),
            pltpu.SemaphoreType.DMA((n_lon,)),
            pltpu.SemaphoreType.DMA((n_lon,)),
            pltpu.SemaphoreType.DMA((2,)),
            pltpu.SemaphoreType.DMA((8,)),
        ],
        compiler_params=pltpu.CompilerParams(
            collective_id=0, has_side_effects=True, vmem_limit_bytes=40 * 2**20
        ),
    )(owned, state, depth, ivel, mass, strength, mask)


def recip(value):
    r = pl.reciprocal(value, approx=True)
    return r * (2.0 - value * r)


def face(open_depth, level, velocity):
    is_open = open_depth > level
    z = jnp.where(is_open, velocity * 0.25, 0.0)
    e = jnp.where(is_open, 0.125, 0.0)
    far = e - jnp.minimum(z, 0.0)
    return far, far + z


def ocean_kernel(
    n_lon,
    n_lat,
    partner,
    info,
    state,
    depth,
    vmix,
    ivel,
    he,
    hw,
    hs,
    hn,
    fold,
    res,
    out,
    out_ice,
    c_v,
    u_v,
    v_v,
    d_v,
    vm_v,
    o_v,
    ice_v,
    he_v,
    hw_v,
    hs_v,
    hn_v,
    fold_v,
    win,
    prev,
    in_sem,
    out_sem,
    sem,
):
    y = lax.axis_index("lat")
    top = y == n_lat - 1
    bottom = y == 0
    lane, row = iotas()
    lane16 = lax.broadcasted_iota(I32, (16, 128), 1)

    small = [
        pltpu.make_async_copy(he, he_v, sem.at[0]),
        pltpu.make_async_copy(hw, hw_v, sem.at[1]),
        pltpu.make_async_copy(hs, hs_v, sem.at[2]),
        pltpu.make_async_copy(hn, hn_v, sem.at[3]),
    ]
    get_fold = pltpu.make_async_copy(fold, fold_v, sem.at[4])
    get_ice = pltpu.make_async_copy(ivel, ice_v, sem.at[5])
    put_ice = pltpu.make_async_copy(ice_v, out_ice, sem.at[6])

    def fetch(i):
        rows = pl.ds(pl.multiple_of(i * 8, 8), 8)
        return [
            pltpu.make_async_copy(state.at[0:2, :, rows, :], c_v.at[:, :, rows, :], in_sem.at[0, i]),
            pltpu.make_async_copy(state.at[2, :, rows, :], u_v.at[:, rows, :], in_sem.at[1, i]),
            pltpu.make_async_copy(state.at[3, :, rows, :], v_v.at[:, rows, :], in_sem.at[2, i]),
            pltpu.make_async_copy(depth.at[rows, :], d_v.at[rows, :], in_sem.at[3, i]),
            pltpu.make_async_copy(vmix.at[:, rows, :], vm_v.at[:, rows, :], in_sem.at[4, i]),
        ]

    def put(i):
        rows = pl.ds(pl.multiple_of(i * 8, 8), 8)
        return pltpu.make_async_copy(o_v.at[:, :, rows, :], out.at[:, :, rows, :], out_sem.at[i])

    @pl.when(top)
    def _():
        get_fold.start()

    for c in small:
        c.start()

    def start_fetch(i, carry):
        for c in fetch(i):
            c.start()
        return carry

    lax.fori_loop(0, NB, start_fetch, 0)
    get_ice.start()
    for c in small:
        c.wait()

    @pl.when(top)
    def _():
        get_fold.wait()
        base = partner[COLS - 1]
        tile0 = lax.div(base, 128)
        shift = lax.rem(base, 128)
        for m in range(LT + 1):
            t = lax.rem(tile0 + m, n_lon * LT)
            dev = lax.div(t, LT)
            j = lax.rem(t, LT)
            win[m, 0:8, :] = fold_v[dev, j]
            win[m, 8:9, :] = fold_v[dev, LT, pl.ds(j, 1), :]
        back = lax.rem(128 - shift, 128)
        for m in range(LT):
            near = pltpu.roll(win[m], back, 1)
            far = pltpu.roll(win[m + 1], back, 1)
            value = jnp.where(lane16 < 128 - shift, near, far)
            for bit in (1, 2, 4, 8, 16, 32, 64):
                value = jnp.where(
                    (lane16 & bit) != 0, pltpu.roll(value, bit, 1), pltpu.roll(value, 128 - bit, 1)
                )
            at = (LT - 1 - m) * 128
            hn_v[:, at : at + 128] = value

    @pl.when(bottom)
    def _():
        hs_v[...] = jnp.zeros((16, COLS), F32)

    for t in range(2):
        for k in range(LEV):
            n = t * LEV + k
            c_v[t, k, ROWS : ROWS + 1, :] = hn_v[n : n + 1, :]
    d_v[ROWS : ROWS + 1, :] = hn_v[8:9, :].astype(I32)

    for c in fetch(0):
        c.wait()

    for j in range(LT):
        cols = slice(j * 128, j * 128 + 128)
        d_s = jnp.broadcast_to(hs_v[8:9, cols], (8, 128))
        open_s = jnp.minimum(d_v[0:8, cols].astype(F32), d_s)
        for k in range(LEV):
            far, near = face(open_s, k, jnp.broadcast_to(hs_v[9 + k : 10 + k, cols], (8, 128)))
            for t in range(2):
                n = t * LEV + k
                south = jnp.broadcast_to(hs_v[n : n + 1, cols], (8, 128))
                prev[n, :, cols] = c_v[t, k, 0:8, cols] * far - south * near

    def block(i, carry):
        @pl.when(i < NB - 1)
        def _():
            for c in fetch(i + 1):
                c.wait()

        rows = pl.ds(pl.multiple_of(i * 8, 8), 8)
        rows_n = pl.ds(pl.multiple_of(i * 8 + 8, 8), 8)

        west_pack = hw_v[rows, :]
        east_pack = he_v[rows, :]
        d0 = d_v[rows, 0:128].astype(F32)
        open_w = jnp.minimum(d0, pltpu.roll(west_pack, 128 - 8, 1))
        west = [None] * 8
        for k in range(LEV):
            far, near = face(open_w, k, pltpu.roll(west_pack, 128 - 9 - k, 1))
            for t in range(2):
                n = t * LEV + k
                c_w = west_pack if n == 0 else pltpu.roll(west_pack, 128 - n, 1)
                west[n] = c_v[t, k, rows, 0:128] * far - c_w * near

        c_own = [c_v[n // LEV, n % LEV, rows, 0:128] for n in range(8)]
        c_roll = [pltpu.roll(value, 127, 1) for value in c_own]
        d_own = d0
        d_roll = pltpu.roll(d0, 127, 1)
        for j in range(LT):
            cols = slice(j * 128, j * 128 + 128)
            nxt = slice(j * 128 + 128, j * 128 + 256)
            if j < LT - 1:
                d_next = d_v[rows, nxt].astype(F32)
                d_next_roll = pltpu.roll(d_next, 127, 1)
                c_next = [c_v[n // LEV, n % LEV, rows, nxt] for n in range(8)]
                c_next_roll = [pltpu.roll(value, 127, 1) for value in c_next]
            else:
                d_next = None
                d_next_roll = pltpu.roll(east_pack, 127 - 8, 1)
                c_next = None
                c_next_roll = [pltpu.roll(east_pack, 127 - n, 1) for n in range(8)]
            d_e = jnp.where(lane == 127, d_next_roll, d_roll)
            d_n = jnp.where(
                row == 7,
                pltpu.roll(d_v[rows_n, cols].astype(F32), 7, 0),
                pltpu.roll(d_own, 7, 0),
            )
            open_e = jnp.minimum(d_own, d_e)
            open_n = jnp.minimum(d_own, d_n)
            rhs = [None] * 8
            for k in range(LEV):
                e_far, e_near = face(open_e, k, u_v[k, rows, cols])
                n_far, n_near = face(open_n, k, v_v[k, rows, cols])
                for t in range(2):
                    n = t * LEV + k
                    c = c_own[n]
                    c_e = jnp.where(lane == 127, c_next_roll[n], c_roll[n])
                    c_n = jnp.where(
                        row == 7, pltpu.roll(c_v[t, k, rows_n, cols], 7, 0), pltpu.roll(c, 7, 0)
                    )
                    east = c_e * e_far - c * e_near
                    north = c_n * n_far - c * n_near
                    east_roll = pltpu.roll(east, 1, 1)
                    north_roll = pltpu.roll(north, 1, 0)
                    from_west = jnp.where(lane == 0, west[n], east_roll)
                    from_south = jnp.where(row == 0, prev[n, :, cols], north_roll)
                    west[n] = east_roll
                    prev[n, :, cols] = north_roll
                    rhs[n] = c + ((east - from_west) + (north - from_south))
            g = [jnp.where(d_own > k, vm_v[k, rows, cols] * 0.25, 0.0) for k in range(LEV)]
            i0 = recip((1.0 + g[0]) + g[1])
            u0 = g[1] * i0
            i1 = recip((1.0 + g[1]) + g[2] - g[1] * u0)
            u1 = g[2] * i1
            i2 = recip((1.0 + g[2]) + g[3] - g[2] * u1)
            u2 = g[3] * i2
            i3 = recip((1.0 + g[3]) - g[3] * u2)
            for t in range(2):
                f = rhs[t * LEV : t * LEV + LEV]
                r0 = f[0] * i0
                r1 = (f[1] + g[1] * r0) * i1
                r2 = (f[2] + g[2] * r1) * i2
                x3 = (f[3] + g[3] * r2) * i3
                x2 = r2 + u2 * x3
                x1 = r1 + u1 * x2
                x0 = r0 + u0 * x1
                for k, value in enumerate((x0, x1, x2, x3)):
                    o_v[t, k, rows, cols] = value
            c_own, c_roll, d_own, d_roll = c_next, c_next_roll, d_next, d_next_roll
        put(i).start()
        return carry

    lax.fori_loop(0, NB // 2, block, 0)

    get_ice.wait()
    for slot in range(SLOTS):
        pos = info[slot]

        @pl.when(pos >= 0)
        def _(slot=slot, pos=pos):
            at = pl.multiple_of(jnp.clip(pos, 0, LT - 1) * 128, 128)
            copy = pltpu.make_async_copy(
                res.at[slot], ice_v.at[:, :, pl.ds(at, 128)], sem.at[7 + slot]
            )
            copy.start()

    for slot in range(SLOTS):
        pos = info[slot]

        @pl.when(pos >= 0)
        def _(slot=slot, pos=pos):
            at = pl.multiple_of(jnp.clip(pos, 0, LT - 1) * 128, 128)
            copy = pltpu.make_async_copy(
                res.at[slot], ice_v.at[:, :, pl.ds(at, 128)], sem.at[7 + slot]
            )
            copy.wait()

    put_ice.start()
    lax.fori_loop(NB // 2, NB, block, 0)

    def drain(i, carry):
        put(i).wait()
        return carry

    lax.fori_loop(0, NB, drain, 0)
    put_ice.wait()


def ocean(n_lon, n_lat, partner, info, state, depth, vmix, ivel, he, hw, hs, hn, fold, res):
    anywhere = pl.BlockSpec(memory_space=pl.ANY)
    smem = pl.BlockSpec(memory_space=pltpu.SMEM)

    def body(*refs):
        ocean_kernel(n_lon, n_lat, *refs)

    return pl.pallas_call(
        body,
        name="ocean",
        out_shape=(
            jax.ShapeDtypeStruct((2, LEV, ROWS, COLS), F32),
            jax.ShapeDtypeStruct((2, ROWS, COLS), F32),
        ),
        in_specs=[smem, smem] + [anywhere] * 10,
        out_specs=(anywhere, anywhere),
        scratch_shapes=[
            pltpu.VMEM((2, LEV, ROWS + 8, COLS), F32),
            pltpu.VMEM((LEV, ROWS, COLS), F32),
            pltpu.VMEM((LEV, ROWS, COLS), F32),
            pltpu.VMEM((ROWS + 8, COLS), I32),
            pltpu.VMEM((LEV, ROWS, COLS), F32),
            pltpu.VMEM((2, LEV, ROWS, COLS), F32),
            pltpu.VMEM((2, ROWS, COLS), F32),
            pltpu.VMEM((ROWS, 128), F32),
            pltpu.VMEM((ROWS, 128), F32),
            pltpu.VMEM((16, COLS), F32),
            pltpu.VMEM((16, COLS), F32),
            pltpu.VMEM((n_lon, LT + 1, 8, 128), F32),
            pltpu.VMEM((LT + 1, 16, 128), F32),
            pltpu.VMEM((8, 8, COLS), F32),
            pltpu.SemaphoreType.DMA((5, NB)),
            pltpu.SemaphoreType.DMA((NB,)),
            pltpu.SemaphoreType.DMA((7 + SLOTS,)),
        ],
        compiler_params=pltpu.CompilerParams(vmem_limit_bytes=48 * 2**20),
    )(partner, info, state, depth, vmix, ivel, he, hw, hs, hn, fold, res)


def on_device(state, depth, vmix, partner, ivel, mass, strength, mask, owned):
    n_lon, n_lat = lax.axis_size("lon"), lax.axis_size("lat")
    he, hw, hs, hn, fold, res, info = exchange_and_ice(
        n_lon, n_lat, owned, state, depth, ivel, mass, strength, mask
    )
    return ocean(n_lon, n_lat, partner, info, state, depth, vmix, ivel, he, hw, hs, hn, fold, res)


def solution(mesh):
    return jax.shard_map(
        on_device,
        mesh=mesh,
        in_specs=(
            P(None, None, "lat", "lon"),
            P("lat", "lon"),
            P(None, "lat", "lon"),
            P("lon"),
            P(None, "lat", "lon"),
            P("lat", "lon"),
            P("lat", "lon"),
            P("lat", "lon"),
            P("lat", "lon", None),
        ),
        out_specs=(P(None, None, "lat", "lon"), P(None, "lat", "lon")),
        check_vma=False,
    )
```

```python
import jax
import jax.numpy as jnp
from jax import lax
from jax.experimental import pallas as pl
from jax.experimental.pallas import tpu as pltpu
from jax.sharding import PartitionSpec as P

MESH = pl.DeviceIdType.MESH
LEV = 4
TILE = 128
ROWS = 128
COLS = 1024
LT = COLS // TILE
SLOTS = 3
SUBCYCLES = 32
NB = ROWS // 8
F32 = jnp.float32
I32 = jnp.int32


def iotas():
    lane = lax.broadcasted_iota(I32, (8, 128), 1)
    row = lax.broadcasted_iota(I32, (8, 128), 0)
    return lane, row


def ice_tiles(places, planes, con, st, rolled, res_ref):
    lane, row = iotas()
    not_first, not_last = lane != 0, lane != 127
    tiles = range(len(places))
    ue_v, un_v, mass_v, str_v, mask_v, depth_v, uo_v, vo_v = planes
    zeros = jnp.zeros((8, 128), F32)

    def at(k):
        return slice(k * 8, k * 8 + 8)

    def north(value):
        return jnp.where(row == 7, 0.0, pltpu.roll(value, 7, 0))

    def south(value):
        return jnp.where(row == 0, 0.0, pltpu.roll(value, 1, 0))

    def keep_east(t, f, k, value):
        pltpu.store(rolled.at[t, f, at(k), :], pltpu.roll(value, 127, 1), mask=not_last)

    def keep_west(t, f, k, value):
        pltpu.store(rolled.at[t, f, at(k), :], pltpu.roll(value, 1, 1), mask=not_first)

    for t in tiles:
        pos = places[t]
        for b in range(NB):
            rows = slice(b * 8, b * 8 + 8)
            spread = pl.ds((b % 2) * 64 + b // 2, 8, stride=8)
            mass, strength = mass_v[pos, rows, :], str_v[pos, rows, :]
            ice = jnp.logical_and(mask_v[pos, rows, :] > 0, depth_v[pos, rows, :] > 0)
            mass = jnp.where(ice, mass, 0.0)
            strength = jnp.where(ice, strength, 0.0)
            inertia = mass * 2.0
            diag = inertia + 1.0
            turn = mass * 0.5
            inv = 1.0 / (diag * diag + turn * turn)
            con[t, 0, spread, :] = inertia
            con[t, 1, spread, :] = diag * inv
            con[t, 2, spread, :] = turn * inv
            con[t, 3, spread, :] = strength * (1.0 / 12.0)
            con[t, 4, spread, :] = uo_v[pos, rows, :] * 0.5
            con[t, 5, spread, :] = vo_v[pos, rows, :] * 0.5
            st[t, 0, spread, :] = ue_v[pos, rows, :] * 0.5
            st[t, 1, spread, :] = un_v[pos, rows, :] * 0.5
            st[t, 2, spread, :] = strength * 0.25
    for t in tiles:
        for k in range(NB):
            for f in range(4):
                rolled[t, f, at(k), :] = zeros
    for t in tiles:
        for k in range(NB):
            p4 = st[t, 2, at(k), :]
            p_south = st[t, 2, at(k - 1), :] if k else south(st[t, 2, at(NB - 1), :])
            p_west = jnp.where(lane == 0, 0.0, pltpu.roll(p4, 1, 1))
            con[t, 4, at(k), :] = con[t, 4, at(k), :] - (p4 - p_west)
            con[t, 5, at(k), :] = con[t, 5, at(k), :] - (p4 - p_south)
            st[t, 3, at(k), :] = p4
            st[t, 4, at(k), :] = zeros
            keep_east(t, 0, k, st[t, 0, at(k), :])
            keep_east(t, 1, k, st[t, 1, at(k), :])

    keep = 1.0 / 1.5

    def stress(t, k):
        u, v = st[t, 0, at(k), :], st[t, 1, at(k), :]
        if k < NB - 1:
            un, vn = st[t, 0, at(k + 1), :], st[t, 1, at(k + 1), :]
        else:
            un, vn = north(st[t, 0, at(0), :]), north(st[t, 1, at(0), :])
        d1 = rolled[t, 0, at(k), :] - u
        d2 = vn - v
        h = (un - u) + (rolled[t, 1, at(k), :] - v)
        div = d1 + d2
        ten = d1 - d2
        p = div + div
        r = ten * 0.5
        q = con[t, 3, at(k), :] * lax.rsqrt((p * p + ten * ten) + (h * h + 0.25))
        sx = st[t, 2, at(k), :] * keep + q * (p + r)
        sy = st[t, 3, at(k), :] * keep + q * (p - r)
        sh = st[t, 4, at(k), :] * keep + q * h
        st[t, 2, at(k), :] = sx
        st[t, 3, at(k), :] = sy
        st[t, 4, at(k), :] = sh
        keep_west(t, 2, k, sx)
        keep_west(t, 3, k, sh)

    def momentum(t, k):
        u, v, sx, sy, sh = [st[t, f, at(k), :] for f in range(5)]
        if k:
            sy_s, sh_s = st[t, 3, at(k - 1), :], st[t, 4, at(k - 1), :]
        else:
            sy_s, sh_s = south(st[t, 3, at(NB - 1), :]), south(st[t, 4, at(NB - 1), :])
        inertia, al, be, kx, ky = [con[t, f, at(k), :] for f in (0, 1, 2, 4, 5)]
        rx = (inertia * u + kx) + ((sx - rolled[t, 2, at(k), :]) + (sh - sh_s))
        ry = (inertia * v + ky) + ((sh - rolled[t, 3, at(k), :]) + (sy - sy_s))
        u = al * rx + be * ry
        v = al * ry - be * rx
        st[t, 0, at(k), :] = u
        st[t, 1, at(k), :] = v
        keep_east(t, 0, k, u)
        keep_east(t, 1, k, v)

    def cycle(_, carry):
        for t in tiles:
            for k in range(NB):
                stress(t, k)
        for t in tiles:
            for k in range(NB):
                momentum(t, k)
        return carry

    lax.fori_loop(0, SUBCYCLES, cycle, 0, unroll=4)
    for t in tiles:
        for k in range(NB):
            res_ref[t, 0, pl.ds(k, 8, stride=NB), :] = st[t, 0, at(k), :] * 2.0
            res_ref[t, 1, pl.ds(k, 8, stride=NB), :] = st[t, 1, at(k), :] * 2.0


def exchange_kernel(
    n_lon,
    n_lat,
    owned_hbm,
    state,
    depth,
    ivel,
    mass,
    strength,
    mask,
    he,
    hw,
    hs,
    hn,
    fold,
    res,
    info,
    depth_v,
    uo_v,
    vo_v,
    ue_v,
    un_v,
    mass_v,
    str_v,
    mask_v,
    col_first,
    col_last,
    blk_first,
    blk_last,
    pack_first,
    pack_last,
    pack_n,
    pack_s,
    pack_f,
    my_list,
    lists,
    lists_s,
    con,
    st,
    rolled,
    load_sem,
    send_sem,
    recv_sem,
    fsend_sem,
    frecv_sem,
    local_sem,
    plane_sem,
    owned,
):
    x = lax.axis_index("lon")
    y = lax.axis_index("lat")
    lane, row = iotas()
    top = y == n_lat - 1
    bottom = y == 0

    def lon(step):
        return {"lon": lax.rem(x + step + n_lon, n_lon), "lat": y}

    def lat(step):
        return {"lon": x, "lat": y + step}

    get_owned = pltpu.make_async_copy(owned_hbm, owned, local_sem.at[2])
    get_owned.start()
    barrier = pltpu.get_barrier_semaphore()

    def greet(device):
        pl.semaphore_signal(barrier, inc=1, device_id=device, device_id_type=MESH)

    for step in (1, -1, 2, -2):
        greet(lon(step))

    @pl.when(top)
    def _():
        for step in range(3, n_lon - 2):
            greet(lon(step))

    @pl.when(jnp.logical_not(top))
    def _():
        greet(lat(1))

    @pl.when(jnp.logical_not(bottom))
    def _():
        greet(lat(-1))

    loads = [
        (state.at[0:2, :, :, pl.ds(0, 128)], col_first),
        (state.at[0:3, :, :, pl.ds(COLS - 128, 128)], col_last),
        (state.at[0:2, :, pl.ds(0, 8), :], blk_first),
        (state.at[0:2, :, pl.ds(ROWS - 8, 8), :], blk_last.at[0:2]),
        (state.at[3, :, pl.ds(ROWS - 8, 8), :], blk_last.at[2]),
    ]
    planes = [
        (depth, depth_v),
        (ivel.at[0], ue_v),
        (ivel.at[1], un_v),
        (mass, mass_v),
        (strength, str_v),
        (mask, mask_v),
        (state.at[2, 0], uo_v),
        (state.at[3, 0], vo_v),
    ]
    copies = [pltpu.make_async_copy(s, d, load_sem.at[i]) for i, (s, d) in enumerate(loads)]
    for i, (s, d) in enumerate(planes):
        if i == 1:
            for c in copies:
                c.start()
        for j in range(LT):
            pltpu.make_async_copy(s.at[:, j * 128 : j * 128 + 128], d.at[j], plane_sem.at[i]).start()

    def plane_wait(i):
        pltpu.make_async_copy(planes[i][1], planes[i][1], plane_sem.at[i]).wait()

    get_owned.wait()
    my_list[...] = jnp.where(
        lane == 0, owned[0, 0, 0], jnp.where(lane == 1, owned[0, 0, 1], owned[0, 0, 2])
    )

    @pl.when(jnp.logical_and(top, jnp.logical_not(bottom)))
    def _():
        pl.semaphore_wait(barrier, n_lon)

    @pl.when(jnp.logical_and(bottom, jnp.logical_not(top)))
    def _():
        pl.semaphore_wait(barrier, 5)

    @pl.when(jnp.logical_not(jnp.logical_or(bottom, top)))
    def _():
        pl.semaphore_wait(barrier, 6)

    def remote(src, dst, i, device):
        return pltpu.make_async_remote_copy(
            src_ref=src,
            dst_ref=dst,
            send_sem=send_sem.at[i],
            recv_sem=recv_sem.at[i],
            device_id=device,
            device_id_type=MESH,
        )

    list_1 = remote(my_list, lists.at[0], 0, lon(-1))
    list_2 = remote(my_list, lists.at[1], 1, lon(-2))
    to_west = remote(pack_first, he, 2, lon(-1))
    to_east = remote(pack_last, hw, 3, lon(1))
    to_south = remote(pack_n, hn, 4, lat(-1))
    to_north = remote(pack_s, hs, 5, lat(1))
    list_1.start()
    list_2.start()

    plane_wait(0)
    for c in copies:
        c.wait()

    for b in range(NB):
        rows = slice(b * 8, b * 8 + 8)
        first = jnp.zeros((8, 128), F32)
        last = jnp.zeros((8, 128), F32)
        for t in range(2):
            for k in range(LEV):
                n = t * LEV + k
                value = col_first[t, k, rows, :]
                first = jnp.where(lane == n, value if n == 0 else pltpu.roll(value, n, 1), first)
                last = jnp.where(lane == n, pltpu.roll(col_last[t, k, rows, :], n + 1, 1), last)
        d_first = depth_v[0, rows, :].astype(F32)
        d_last = depth_v[LT - 1, rows, :].astype(F32)
        first = jnp.where(lane == 8, pltpu.roll(d_first, 8, 1), first)
        last = jnp.where(lane == 8, pltpu.roll(d_last, 9, 1), last)
        for k in range(LEV):
            last = jnp.where(lane == 9 + k, pltpu.roll(col_last[2, k, rows, :], 10 + k, 1), last)
        pack_first[rows, :] = first
        pack_last[rows, :] = last

    pack_n[...] = jnp.zeros((16, COLS), F32)
    pack_s[...] = jnp.zeros((16, COLS), F32)
    for t in range(2):
        for k in range(LEV):
            n = t * LEV + k
            pack_n[n : n + 1, :] = blk_first[t, k, 0:1, :]
            pack_s[n : n + 1, :] = blk_last[t, k, 7:8, :]
    for k in range(LEV):
        pack_s[9 + k : 10 + k, :] = blk_last[2, k, 7:8, :]
    for j in range(LT):
        cols = slice(j * 128, j * 128 + 128)
        pack_n[8:9, cols] = depth_v[j, 0:8, :].astype(F32)[0:1, :]
        pack_s[8:9, cols] = depth_v[j, ROWS - 8 : ROWS, :].astype(F32)[7:8, :]
        pack_f[j] = pack_s[0:8, j * 128 : j * 128 + 128]
        pack_f[LT, j : j + 1, :] = pack_s[8:9, j * 128 : j * 128 + 128]

    to_west.start()
    to_east.start()

    @pl.when(jnp.logical_not(bottom))
    def _():
        to_south.start()

    @pl.when(jnp.logical_not(top))
    def _():
        to_north.start()

    def fold_copy(step):
        return pltpu.make_async_remote_copy(
            src_ref=pack_f,
            dst_ref=fold.at[x],
            send_sem=fsend_sem.at[step],
            recv_sem=frecv_sem.at[x],
            device_id=lon(step),
            device_id_type=MESH,
        )

    def fold_arrival(step):
        source = lax.rem(x - step + n_lon, n_lon)
        return pltpu.make_async_remote_copy(
            src_ref=pack_f,
            dst_ref=fold.at[source],
            send_sem=fsend_sem.at[step],
            recv_sem=frecv_sem.at[source],
            device_id=lon(step),
            device_id_type=MESH,
        )

    own_fold = pltpu.make_async_copy(pack_f, fold.at[x], local_sem.at[0])

    @pl.when(top)
    def _():
        own_fold.start()
        for step in range(1, n_lon):
            fold_copy(step).start()

    for i in range(1, len(planes)):
        plane_wait(i)

    list_1.wait_recv()
    list_2.wait_recv()
    to_smem = pltpu.make_async_copy(lists, lists_s, local_sem.at[1])
    to_smem.start()
    to_smem.wait()
    places = []
    for slot, column in enumerate((owned[0, 0, 0], lists_s[0, 0, 1], lists_s[1, 0, 2])):
        info[slot] = jnp.where(column >= 0, column - x * LT, -1)
        places.append(jnp.clip(column - x * LT, 0, LT - 1))
    ice_tiles(
        places, (ue_v, un_v, mass_v, str_v, mask_v, depth_v, uo_v, vo_v), con, st, rolled, res
    )

    list_1.wait_send()
    list_2.wait_send()
    to_west.wait()
    to_east.wait()

    @pl.when(jnp.logical_not(bottom))
    def _():
        to_south.wait_send()
        to_north.wait_recv()

    @pl.when(jnp.logical_not(top))
    def _():
        to_north.wait_send()
        to_south.wait_recv()

    @pl.when(top)
    def _():
        own_fold.wait()
        for step in range(1, n_lon):
            fold_copy(step).wait_send()
        for step in range(1, n_lon):
            fold_arrival(step).wait_recv()


def exchange_and_ice(n_lon, n_lat, owned, state, depth, ivel, mass, strength, mask):
    anywhere = pl.BlockSpec(memory_space=pl.ANY)
    plane = pltpu.VMEM((LT, ROWS, 128), F32)
    plane_i = pltpu.VMEM((LT, ROWS, 128), I32)

    def body(*refs):
        exchange_kernel(n_lon, n_lat, *refs)

    return pl.pallas_call(
        body,
        name="exchange_and_ice",
        out_shape=(
            jax.ShapeDtypeStruct((ROWS, 128), F32),
            jax.ShapeDtypeStruct((ROWS, 128), F32),
            jax.ShapeDtypeStruct((16, COLS), F32),
            jax.ShapeDtypeStruct((16, COLS), F32),
            jax.ShapeDtypeStruct((n_lon, LT + 1, 8, 128), F32),
            jax.ShapeDtypeStruct((SLOTS, 2, TILE, TILE), F32),
            jax.ShapeDtypeStruct((SLOTS,), I32),
        ),
        in_specs=[pl.BlockSpec(memory_space=pltpu.HBM)] * 7,
        out_specs=(anywhere,) * 5
        + (pl.BlockSpec(memory_space=pltpu.VMEM), pl.BlockSpec(memory_space=pltpu.SMEM)),
        scratch_shapes=[
            plane_i,
            plane,
            plane,
            plane,
            plane,
            plane,
            plane,
            plane_i,
            pltpu.VMEM((2, LEV, ROWS, 128), F32),
            pltpu.VMEM((3, LEV, ROWS, 128), F32),
            pltpu.VMEM((2, LEV, 8, COLS), F32),
            pltpu.VMEM((3, LEV, 8, COLS), F32),
            pltpu.VMEM((ROWS, 128), F32),
            pltpu.VMEM((ROWS, 128), F32),
            pltpu.VMEM((16, COLS), F32),
            pltpu.VMEM((16, COLS), F32),
            pltpu.VMEM((LT + 1, 8, 128), F32),
            pltpu.VMEM((8, 128), I32),
            pltpu.VMEM((2, 8, 128), I32),
            pltpu.SMEM((2, 8, 128), I32),
            pltpu.VMEM((SLOTS, 6, TILE, TILE), F32),
            pltpu.VMEM((SLOTS, 5, TILE, TILE), F32),
            pltpu.VMEM((SLOTS, 4, TILE, TILE), F32),
            pltpu.SemaphoreType.DMA((5,)),
            pltpu.SemaphoreType.DMA((6,)),
            pltpu.SemaphoreType.DMA((6,)),
            pltpu.SemaphoreType.DMA((n_lon,)),
            pltpu.SemaphoreType.DMA((n_lon,)),
            pltpu.SemaphoreType.DMA((3,)),
            pltpu.SemaphoreType.DMA((8,)),
            pltpu.SMEM((1, 1, SLOTS), I32),
        ],
        compiler_params=pltpu.CompilerParams(
            collective_id=0, has_side_effects=True, vmem_limit_bytes=16 * 2**20
        ),
    )(owned, state, depth, ivel, mass, strength, mask)


def recip(value):
    r = pltpu.reciprocal(value, approx=True)
    return r * (2.0 - value * r)


def face(open_depth, level, velocity):
    is_open = open_depth > level
    z = jnp.where(is_open, velocity * 0.25, 0.0)
    e = jnp.where(is_open, 0.125, 0.0)
    far = e - jnp.minimum(z, 0.0)
    return far, far + z


def ocean_kernel(
    n_lon,
    n_lat,
    partner,
    info,
    state,
    depth,
    vmix,
    ivel,
    he,
    hw,
    hs,
    hn,
    fold,
    res,
    out,
    out_ice,
    c_v,
    u_v,
    v_v,
    d_v,
    vm_v,
    o_v,
    ice_v,
    he_v,
    hw_v,
    hs_v,
    hn_v,
    fold_v,
    win,
    c_rolled,
    d_rolled,
    h_west,
    h_north,
    in_sem,
    out_sem,
    sem,
):
    y = lax.axis_index("lat")
    top = y == n_lat - 1
    bottom = y == 0
    lane, _ = iotas()
    lane16 = lax.broadcasted_iota(I32, (16, 128), 1)

    small = [
        pltpu.make_async_copy(he, he_v, sem.at[0]),
        pltpu.make_async_copy(hw, hw_v, sem.at[1]),
        pltpu.make_async_copy(hs, hs_v, sem.at[2]),
        pltpu.make_async_copy(hn, hn_v, sem.at[3]),
    ]
    get_fold = pltpu.make_async_copy(fold, fold_v, sem.at[4])
    get_ice = pltpu.make_async_copy(ivel, ice_v, sem.at[5])
    put_ice = pltpu.make_async_copy(ice_v, out_ice, sem.at[6])

    def fetch(j):
        cols = pl.ds(pl.multiple_of(j * 128, 128), 128)
        rows = pl.ds(0, ROWS)
        return [
            pltpu.make_async_copy(state.at[0:2, :, :, cols], c_v.at[j, :, :, rows, :], in_sem.at[0, j]),
            pltpu.make_async_copy(depth.at[:, cols], d_v.at[j, rows, :], in_sem.at[1, j]),
            pltpu.make_async_copy(state.at[2, :, :, cols], u_v.at[j], in_sem.at[2, j]),
            pltpu.make_async_copy(state.at[3, :, :, cols], v_v.at[j], in_sem.at[3, j]),
            pltpu.make_async_copy(vmix.at[:, :, cols], vm_v.at[j], in_sem.at[4, j]),
        ]

    def put(j):
        cols = pl.ds(pl.multiple_of(j * 128, 128), 128)
        return pltpu.make_async_copy(o_v.at[j], out.at[:, :, :, cols], out_sem.at[j])

    def patch(slot):
        at = pl.multiple_of(jnp.clip(info[slot], 0, LT - 1) * 128, 128)
        return pltpu.make_async_copy(res.at[slot], ice_v.at[:, :, pl.ds(at, 128)], sem.at[7 + slot])

    @pl.when(top)
    def _():
        get_fold.start()

    for c in small:
        c.start()
    for j in range(LT):
        for c in fetch(j):
            c.start()
    get_ice.start()
    for c in small:
        c.wait()

    @pl.when(top)
    def _():
        get_fold.wait()
        base = partner[COLS - 1]
        tile0 = lax.div(base, 128)
        shift = lax.rem(base, 128)
        for m in range(LT + 1):
            t = lax.rem(tile0 + m, n_lon * LT)
            dev = lax.div(t, LT)
            j = lax.rem(t, LT)
            win[m, 0:8, :] = fold_v[dev, j]
            win[m, 8:9, :] = fold_v[dev, LT, pl.ds(j, 1), :]
        back = lax.rem(128 - shift, 128)
        values = []
        for m in range(LT):
            near = pltpu.roll(win[m], back, 1)
            far = pltpu.roll(win[m + 1], back, 1)
            values.append(jnp.where(lane16 < 128 - shift, near, far))
        for bit in (1, 2, 4, 8, 16, 32, 64):
            odd = (lane16 & bit) != 0
            values = [
                jnp.where(odd, pltpu.roll(value, bit, 1), pltpu.roll(value, 128 - bit, 1))
                for value in values
            ]
        for m in range(LT):
            at = (LT - 1 - m) * 128
            hn_v[:, at : at + 128] = values[m]

    @pl.when(bottom)
    def _():
        hs_v[...] = jnp.zeros((16, COLS), F32)

    for j in range(LT):
        cols = slice(j * 128, j * 128 + 128)
        for n in range(8):
            c_v[j, n // LEV, n % LEV, ROWS : ROWS + 1, :] = hn_v[n : n + 1, cols]
        d_v[j, ROWS : ROWS + 1, :] = hn_v[8:9, cols].astype(I32)
    for b in range(NB):
        rows = slice(b * 8, b * 8 + 8)
        pack = he_v[rows, :]
        for n in range(8):
            c_v[LT, n // LEV, n % LEV, rows, :] = pack if n == 0 else pltpu.roll(pack, 128 - n, 1)
        d_v[LT, rows, :] = pltpu.roll(pack, 120, 1).astype(I32)

    for c in fetch(0):
        c.wait()

    for b in range(NB):
        rows = slice(b * 8, b * 8 + 8)
        pack = hw_v[rows, :]
        own = d_v[0, rows, :].astype(F32)
        d_rolled[rows, :] = pltpu.roll(own, 127, 1)
        open_w = jnp.minimum(own, pltpu.roll(pack, 120, 1))
        for k in range(LEV):
            far, near = face(open_w, k, pltpu.roll(pack, 119 - k, 1))
            for t in range(2):
                n = t * LEV + k
                c_w = pack if n == 0 else pltpu.roll(pack, 128 - n, 1)
                c = c_v[0, t, k, rows, :]
                h_west[n, rows, :] = c * far - c_w * near
                c_rolled[n, rows, :] = pltpu.roll(c, 127, 1)

    def column(j, carry):
        @pl.when(j < LT - 1)
        def _():
            for c in fetch(j + 1):
                c.wait()

        @pl.when(j == 2)
        def _():
            get_ice.wait()
            for slot in range(SLOTS):

                @pl.when(info[slot] >= 0)
                def _(slot=slot):
                    patch(slot).start()

        @pl.when(j == 4)
        def _():
            for slot in range(SLOTS):

                @pl.when(info[slot] >= 0)
                def _(slot=slot):
                    patch(slot).wait()

            put_ice.start()

        cols = pl.ds(pl.multiple_of(j * 128, 128), 128)
        own = jnp.broadcast_to(d_v[j, 0:8, :].astype(F32)[0:1, :], (8, 128))
        open_s = jnp.minimum(own, jnp.broadcast_to(hs_v[8:9, cols], (8, 128)))
        for k in range(LEV):
            far, near = face(open_s, k, jnp.broadcast_to(hs_v[9 + k : 10 + k, cols], (8, 128)))
            for t in range(2):
                n = t * LEV + k
                c_s = jnp.broadcast_to(hs_v[n : n + 1, cols], (8, 128))
                c = jnp.broadcast_to(c_v[j, t, k, 0:1, :], (8, 128))
                h_north[n, 0:8, :] = c * far - c_s * near

        for b in range(NB):
            rows = slice(b * 8, b * 8 + 8)
            ahead = slice(b * 8 + 1, b * 8 + 9)
            store = slice(b * 8 + 8, b * 8 + 16)
            behind = slice(b * 8 + 7, b * 8 + 15)
            own = d_v[j, rows, :].astype(F32)
            d_next = pltpu.roll(d_v[j + 1, rows, :].astype(F32), 127, 1)
            open_e = jnp.minimum(own, jnp.where(lane == 127, d_next, d_rolled[rows, :]))
            open_n = jnp.minimum(own, d_v[j, ahead, :].astype(F32))
            d_rolled[rows, :] = d_next
            rhs = [None] * 8
            for k in range(LEV):
                e_far, e_near = face(open_e, k, u_v[j, k, rows, :])
                n_far, n_near = face(open_n, k, v_v[j, k, rows, :])
                for t in range(2):
                    n = t * LEV + k
                    c = c_v[j, t, k, rows, :]
                    c_next = pltpu.roll(c_v[j + 1, t, k, rows, :], 127, 1)
                    c_e = jnp.where(lane == 127, c_next, c_rolled[n, rows, :])
                    c_rolled[n, rows, :] = c_next
                    east = c_e * e_far - c * e_near
                    north = c_v[j, t, k, ahead, :] * n_far - c * n_near
                    h_north[n, store, :] = north
                    east_rolled = pltpu.roll(east, 1, 1)
                    from_west = jnp.where(lane == 0, h_west[n, rows, :], east_rolled)
                    h_west[n, rows, :] = east_rolled
                    rhs[n] = c + ((east - from_west) + (north - h_north[n, behind, :]))
            g = [jnp.where(own > k, vm_v[j, k, rows, :] * 0.25, 0.0) for k in range(LEV)]
            i0 = recip((1.0 + g[0]) + g[1])
            u0 = g[1] * i0
            i1 = recip((1.0 + g[1]) + g[2] - g[1] * u0)
            u1 = g[2] * i1
            i2 = recip((1.0 + g[2]) + g[3] - g[2] * u1)
            u2 = g[3] * i2
            i3 = recip((1.0 + g[3]) - g[3] * u2)
            for t in range(2):
                f = rhs[t * LEV : t * LEV + LEV]
                r0 = f[0] * i0
                r1 = (f[1] + g[1] * r0) * i1
                r2 = (f[2] + g[2] * r1) * i2
                x3 = (f[3] + g[3] * r2) * i3
                x2 = r2 + u2 * x3
                x1 = r1 + u1 * x2
                x0 = r0 + u0 * x1
                for k, value in enumerate((x0, x1, x2, x3)):
                    o_v[j, t, k, rows, :] = value
        put(j).start()
        return carry

    lax.fori_loop(0, LT, column, 0)
    for j in range(LT):
        put(j).wait()
    put_ice.wait()


def ocean(n_lon, n_lat, partner, info, state, depth, vmix, ivel, he, hw, hs, hn, fold, res):
    anywhere = pl.BlockSpec(memory_space=pl.ANY)
    smem = pl.BlockSpec(memory_space=pltpu.SMEM)

    def body(*refs):
        ocean_kernel(n_lon, n_lat, *refs)

    return pl.pallas_call(
        body,
        name="ocean",
        out_shape=(
            jax.ShapeDtypeStruct((2, LEV, ROWS, COLS), F32),
            jax.ShapeDtypeStruct((2, ROWS, COLS), F32),
        ),
        in_specs=[smem, smem] + [anywhere] * 10,
        out_specs=(anywhere, anywhere),
        scratch_shapes=[
            pltpu.VMEM((LT + 1, 2, LEV, ROWS + 8, 128), F32),
            pltpu.VMEM((LT, LEV, ROWS, 128), F32),
            pltpu.VMEM((LT, LEV, ROWS, 128), F32),
            pltpu.VMEM((LT + 1, ROWS + 8, 128), I32),
            pltpu.VMEM((LT, LEV, ROWS, 128), F32),
            pltpu.VMEM((LT, 2, LEV, ROWS, 128), F32),
            pltpu.VMEM((2, ROWS, COLS), F32),
            pltpu.VMEM((ROWS, 128), F32),
            pltpu.VMEM((ROWS, 128), F32),
            pltpu.VMEM((16, COLS), F32),
            pltpu.VMEM((16, COLS), F32),
            pltpu.VMEM((n_lon, LT + 1, 8, 128), F32),
            pltpu.VMEM((LT + 1, 16, 128), F32),
            pltpu.VMEM((8, ROWS, 128), F32),
            pltpu.VMEM((ROWS, 128), F32),
            pltpu.VMEM((8, ROWS, 128), F32),
            pltpu.VMEM((8, ROWS + 8, 128), F32),
            pltpu.SemaphoreType.DMA((5, LT)),
            pltpu.SemaphoreType.DMA((LT,)),
            pltpu.SemaphoreType.DMA((7 + SLOTS,)),
        ],
        compiler_params=pltpu.CompilerParams(vmem_limit_bytes=28 * 2**20),
    )(partner, info, state, depth, vmix, ivel, he, hw, hs, hn, fold, res)


def on_device(state, depth, vmix, partner, ivel, mass, strength, mask, owned):
    n_lon, n_lat = lax.axis_size("lon"), lax.axis_size("lat")
    in_hbm = [
        pltpu.with_memory_space_constraint(value, pltpu.HBM)
        for value in (owned, state, depth, ivel, mass, strength, mask)
    ]
    he, hw, hs, hn, fold, res, info = exchange_and_ice(n_lon, n_lat, *in_hbm)
    depth = in_hbm[2]
    return ocean(n_lon, n_lat, partner, info, state, depth, vmix, ivel, he, hw, hs, hn, fold, res)


def solution(mesh):
    return jax.shard_map(
        on_device,
        mesh=mesh,
        in_specs=(
            P(None, None, "lat", "lon"),
            P("lat", "lon"),
            P(None, "lat", "lon"),
            P("lon"),
            P(None, "lat", "lon"),
            P("lat", "lon"),
            P("lat", "lon"),
            P("lat", "lon"),
            P("lat", "lon", None),
        ),
        out_specs=(P(None, None, "lat", "lon"), P(None, "lat", "lon")),
        check_vma=False,
    )
```

```python
import jax
import jax.numpy as jnp
from jax import lax
from jax.experimental import pallas as pl
from jax.experimental.pallas import tpu as pltpu
from jax.sharding import PartitionSpec as P

MESH = pl.DeviceIdType.MESH
LEV = 4
TILE = 128
ROWS = 128
COLS = 1024
LT = COLS // TILE
SLOTS = 3
SUBCYCLES = 32
NB = ROWS // 8
F32 = jnp.float32
I32 = jnp.int32


def iotas():
    lane = lax.broadcasted_iota(I32, (8, 128), 1)
    row = lax.broadcasted_iota(I32, (8, 128), 0)
    return lane, row


def recip(value):
    r = pltpu.reciprocal(value, approx=True)
    return r * (2.0 - value * r)


def face(open_depth, level, velocity):
    is_open = open_depth > level
    z = jnp.where(is_open, velocity * 0.25, 0.0)
    e = jnp.where(is_open, 0.125, 0.0)
    far = e - jnp.minimum(z, 0.0)
    return far, far + z


def ice_tiles(places, planes, con, st, rolled, res_ref, hook):
    lane, row = iotas()
    not_first, not_last = lane != 0, lane != 127
    tiles = range(len(places))
    ue_v, un_v, mass_v, str_v, mask_v, depth_v, uo_v, vo_v = planes
    zeros = jnp.zeros((8, 128), F32)

    def at(k):
        return slice(k * 8, k * 8 + 8)

    def north(value):
        return jnp.where(row == 7, 0.0, pltpu.roll(value, 7, 0))

    def south(value):
        return jnp.where(row == 0, 0.0, pltpu.roll(value, 1, 0))

    def keep_east(t, f, k, value):
        pltpu.store(rolled.at[t, f, at(k), :], pltpu.roll(value, 127, 1), mask=not_last)

    def keep_west(t, f, k, value):
        pltpu.store(rolled.at[t, f, at(k), :], pltpu.roll(value, 1, 1), mask=not_first)

    for t in tiles:
        pos = places[t]
        for b in range(NB):
            rows = slice(b * 8, b * 8 + 8)
            spread = pl.ds((b % 2) * 64 + b // 2, 8, stride=8)
            mass, strength = mass_v[pos, rows, :], str_v[pos, rows, :]
            ice = jnp.logical_and(mask_v[pos, rows, :] > 0, depth_v[pos, rows, :] > 0)
            mass = jnp.where(ice, mass, 0.0)
            strength = jnp.where(ice, strength, 0.0)
            inertia = mass * 2.0
            diag = inertia + 1.0
            turn = mass * 0.5
            inv = 1.0 / (diag * diag + turn * turn)
            con[t, 0, spread, :] = inertia
            con[t, 1, spread, :] = diag * inv
            con[t, 2, spread, :] = turn * inv
            con[t, 3, spread, :] = strength * (1.0 / 12.0)
            con[t, 4, spread, :] = uo_v[pos, 0, rows, :] * 0.5
            con[t, 5, spread, :] = vo_v[pos, 0, rows, :] * 0.5
            st[t, 0, spread, :] = ue_v[pos, rows, :] * 0.5
            st[t, 1, spread, :] = un_v[pos, rows, :] * 0.5
            st[t, 2, spread, :] = strength * 0.25
    for t in tiles:
        for k in range(NB):
            for f in range(4):
                rolled[t, f, at(k), :] = zeros
    for t in tiles:
        for k in range(NB):
            p4 = st[t, 2, at(k), :]
            p_south = st[t, 2, at(k - 1), :] if k else south(st[t, 2, at(NB - 1), :])
            p_west = jnp.where(lane == 0, 0.0, pltpu.roll(p4, 1, 1))
            con[t, 4, at(k), :] = con[t, 4, at(k), :] - (p4 - p_west)
            con[t, 5, at(k), :] = con[t, 5, at(k), :] - (p4 - p_south)
            st[t, 3, at(k), :] = p4
            st[t, 4, at(k), :] = zeros
            keep_east(t, 0, k, st[t, 0, at(k), :])
            keep_east(t, 1, k, st[t, 1, at(k), :])

    keep = 1.0 / 1.5

    def stress(t, k):
        u, v = st[t, 0, at(k), :], st[t, 1, at(k), :]
        if k < NB - 1:
            un, vn = st[t, 0, at(k + 1), :], st[t, 1, at(k + 1), :]
        else:
            un, vn = north(st[t, 0, at(0), :]), north(st[t, 1, at(0), :])
        d1 = rolled[t, 0, at(k), :] - u
        d2 = vn - v
        h = (un - u) + (rolled[t, 1, at(k), :] - v)
        div = d1 + d2
        ten = d1 - d2
        p = div + div
        r = ten * 0.5
        q = con[t, 3, at(k), :] * lax.rsqrt((p * p + ten * ten) + (h * h + 0.25))
        sx = st[t, 2, at(k), :] * keep + q * (p + r)
        sy = st[t, 3, at(k), :] * keep + q * (p - r)
        sh = st[t, 4, at(k), :] * keep + q * h
        st[t, 2, at(k), :] = sx
        st[t, 3, at(k), :] = sy
        st[t, 4, at(k), :] = sh
        keep_west(t, 2, k, sx)
        keep_west(t, 3, k, sh)

    def momentum(t, k):
        u, v, sx, sy, sh = [st[t, f, at(k), :] for f in range(5)]
        if k:
            sy_s, sh_s = st[t, 3, at(k - 1), :], st[t, 4, at(k - 1), :]
        else:
            sy_s, sh_s = south(st[t, 3, at(NB - 1), :]), south(st[t, 4, at(NB - 1), :])
        inertia, al, be, kx, ky = [con[t, f, at(k), :] for f in (0, 1, 2, 4, 5)]
        rx = (inertia * u + kx) + ((sx - rolled[t, 2, at(k), :]) + (sh - sh_s))
        ry = (inertia * v + ky) + ((sh - rolled[t, 3, at(k), :]) + (sy - sy_s))
        u = al * rx + be * ry
        v = al * ry - be * rx
        st[t, 0, at(k), :] = u
        st[t, 1, at(k), :] = v
        keep_east(t, 0, k, u)
        keep_east(t, 1, k, v)

    def cycle(_, carry):
        for t in tiles:
            for k in range(NB):
                stress(t, k)
        for t in tiles:
            for k in range(NB):
                momentum(t, k)
        return carry

    def four(i, carry):
        hook(i)
        for _ in range(4):
            cycle(i, carry)
        return carry

    lax.fori_loop(0, SUBCYCLES // 4, four, 0)
    for t in tiles:
        for k in range(NB):
            res_ref[t, 0, pl.ds(k, 8, stride=NB), :] = st[t, 0, at(k), :] * 2.0
            res_ref[t, 1, pl.ds(k, 8, stride=NB), :] = st[t, 1, at(k), :] * 2.0


def exchange_kernel(
    n_lon,
    n_lat,
    owned_hbm,
    state,
    depth,
    ivel,
    mass,
    strength,
    mask,
    he,
    hw,
    hs,
    hn,
    own_first,
    own_last,
    own_n,
    own_s,
    fold,
    interim,
    res,
    info,
    c_v,
    u_v,
    v_v,
    d_v,
    ue_v,
    un_v,
    mass_v,
    str_v,
    mask_v,
    c_rolled,
    d_rolled,
    h_west,
    h_north,
    part,
    p_v,
    pack_first,
    pack_last,
    pack_n,
    pack_s,
    pack_f,
    my_list,
    lists,
    lists_s,
    owned,
    con,
    st,
    rolled,
    in_sem,
    plane_sem,
    p_sem,
    send_sem,
    recv_sem,
    fsend_sem,
    frecv_sem,
    local_sem,
):
    x = lax.axis_index("lon")
    y = lax.axis_index("lat")
    lane, row = iotas()
    is_last, not_last = lane == 127, lane != 127
    is_first, not_first = lane == 0, lane != 0
    top = y == n_lat - 1
    bottom = y == 0
    half = lax.rem(x, 2)
    chip = lax.div(x, 2)

    def lon(step):
        return {"lon": lax.rem(x + step + n_lon, n_lon), "lat": y}

    def lat(step):
        return {"lon": x, "lat": y + step}

    get_owned = pltpu.make_async_copy(owned_hbm, owned, local_sem.at[0])
    get_owned.start()
    barrier = pltpu.get_barrier_semaphore()

    def greet(device):
        pl.semaphore_signal(barrier, inc=1, device_id=device, device_id_type=MESH)

    for step in (1, -1, 2, -2):
        greet(lon(step))

    fold_extra = range(4, n_lon - 2, 2)

    @pl.when(top)
    def _():
        for step in fold_extra:
            greet(lon(step))

    @pl.when(jnp.logical_not(top))
    def _():
        greet(lat(1))

    @pl.when(jnp.logical_not(bottom))
    def _():
        greet(lat(-1))

    def barrier_wait():
        @pl.when(jnp.logical_and(top, jnp.logical_not(bottom)))
        def _():
            pl.semaphore_wait(barrier, 5 + len(fold_extra))

        @pl.when(jnp.logical_and(bottom, jnp.logical_not(top)))
        def _():
            pl.semaphore_wait(barrier, 5)

        @pl.when(jnp.logical_not(jnp.logical_or(bottom, top)))
        def _():
            pl.semaphore_wait(barrier, 6)

    def fetch(j):
        cols = pl.ds(pl.multiple_of(j * 128, 128), 128)
        rows = pl.ds(0, ROWS)
        return [
            pltpu.make_async_copy(state.at[0:2, :, :, cols], c_v.at[j, :, :, rows, :], in_sem.at[0, j]),
            pltpu.make_async_copy(depth.at[:, cols], d_v.at[j, rows, :], in_sem.at[1, j]),
            pltpu.make_async_copy(state.at[2, :, :, cols], u_v.at[j], in_sem.at[2, j]),
            pltpu.make_async_copy(state.at[3, :, :, cols], v_v.at[j], in_sem.at[3, j]),
        ]

    for j in range(LT):
        for c in fetch(j):
            c.start()
    planes = [(ivel.at[0], ue_v), (ivel.at[1], un_v), (mass, mass_v), (strength, str_v), (mask, mask_v)]
    for i, (src, dst) in enumerate(planes):
        for j in range(LT):
            pltpu.make_async_copy(
                src.at[:, j * 128 : j * 128 + 128], dst.at[j], plane_sem.at[i]
            ).start()

    get_owned.wait()
    my_list[...] = jnp.where(
        lane == 0, owned[0, 0, 0], jnp.where(lane == 1, owned[0, 0, 1], owned[0, 0, 2])
    )

    def remote(src, dst, i, device):
        return pltpu.make_async_remote_copy(
            src_ref=src,
            dst_ref=dst,
            send_sem=send_sem.at[i],
            recv_sem=recv_sem.at[i],
            device_id=device,
            device_id_type=MESH,
        )

    list_1 = remote(my_list, lists.at[0], 0, lon(-1))
    list_2 = remote(my_list, lists.at[1], 1, lon(-2))
    to_west = remote(pack_first, he, 2, lon(-1))
    to_east = remote(pack_last, hw, 3, lon(1))
    to_south = remote(pack_n, hn, 4, lat(-1))
    to_north = remote(pack_s, hs, 5, lat(1))

    zeros = jnp.zeros((8, 128), F32)
    beyond = slice(ROWS, ROWS + 8)
    for j in range(LT):
        d_v[j, beyond, :] = jnp.zeros((8, 128), I32)
        for n in range(8):
            c_v[j, n // LEV, n % LEV, beyond, :] = zeros
    for n in range(8):
        h_north[n, 0:8, :] = zeros
        for b in range(NB):
            h_west[0, n, b * 8 : b * 8 + 8, :] = zeros
    for c in fetch(0):
        c.wait()
    for b in range(NB):
        rows = slice(b * 8, b * 8 + 8)
        pltpu.store(
            d_rolled.at[0, rows, :], pltpu.roll(d_v[0, rows, :].astype(F32), 127, 1), mask=not_last
        )
        for n in range(8):
            value = pltpu.roll(c_v[0, n // LEV, n % LEV, rows, :], 127, 1)
            pltpu.store(c_rolled.at[0, n, rows, :], value, mask=not_last)

    def put(j):
        return pltpu.make_async_copy(p_v.at[j], interim.at[j], p_sem.at[j])

    def column(j, carry):
        @pl.when(j < LT - 1)
        def _():
            for c in fetch(j + 1):
                c.wait()

        @pl.when(j == 3)
        def _():
            barrier_wait()
            list_1.start()
            list_2.start()

        cur = lax.rem(j, 2)
        nxt = 1 - cur
        after = jnp.minimum(j + 1, LT - 1)
        inside = jnp.where(j < LT - 1, 1.0, 0.0)

        def roll_next(b):
            rows = slice(b * 8, b * 8 + 8)
            value = pltpu.roll(d_v[after, rows, :].astype(F32) * inside, 127, 1)
            pltpu.store(d_rolled.at[cur, rows, :], value, mask=is_last)
            pltpu.store(d_rolled.at[nxt, rows, :], value, mask=not_last)
            for n in range(8):
                value = pltpu.roll(c_v[after, n // LEV, n % LEV, rows, :], 127, 1)
                pltpu.store(c_rolled.at[cur, n, rows, :], value, mask=is_last)
                pltpu.store(c_rolled.at[nxt, n, rows, :], value, mask=not_last)

        def fluxes(b):
            rows = slice(b * 8, b * 8 + 8)
            ahead = slice(b * 8 + 1, b * 8 + 9)
            store = slice(b * 8 + 8, b * 8 + 16)
            behind = slice(b * 8 + 7, b * 8 + 15)
            own = d_v[j, rows, :].astype(F32)
            open_e = jnp.minimum(own, d_rolled[cur, rows, :])
            open_n = jnp.minimum(own, d_v[j, ahead, :].astype(F32))
            for k in range(LEV):
                e_far, e_near = face(open_e, k, u_v[j, k, rows, :])
                n_far, n_near = face(open_n, k, v_v[j, k, rows, :])
                for t in range(2):
                    n = t * LEV + k
                    c = c_v[j, t, k, rows, :]
                    east = c_rolled[cur, n, rows, :] * e_far - c * e_near
                    east_rolled = pltpu.roll(east, 1, 1)
                    pltpu.store(h_west.at[cur, n, rows, :], east_rolled, mask=not_first)
                    pltpu.store(h_west.at[nxt, n, rows, :], east_rolled, mask=is_first)
                    north = c_v[j, t, k, ahead, :] * n_far - c * n_near
                    h_north[n, store, :] = north
                    part[n, rows, :] = (c + east) + (north - h_north[n, behind, :])

        def finish(b):
            rows = slice(b * 8, b * 8 + 8)
            for n in range(8):
                p_v[j, n, rows, :] = part[n, rows, :] - h_west[cur, n, rows, :]

        for b in range(NB + 6):
            if b < NB:
                roll_next(b)
            if 0 <= b - 3 < NB:
                fluxes(b - 3)
            if 0 <= b - 6 < NB:
                finish(b - 6)
        put(j).start()
        return carry

    lax.fori_loop(0, LT, column, 0)

    for b in range(NB):
        rows = slice(b * 8, b * 8 + 8)
        d_first = jnp.broadcast_to(d_v[0, rows, :].astype(F32)[:, 0:1], (8, 128))
        d_last = jnp.broadcast_to(d_v[LT - 1, rows, :].astype(F32)[:, 127:128], (8, 128))
        first, last = d_first, d_last
        for n in range(8):
            t, k = n // LEV, n % LEV
            value = c_v[0, t, k, rows, :]
            first = jnp.where(lane == n, value if n == 0 else pltpu.roll(value, n, 1), first)
            last = jnp.where(lane == n, pltpu.roll(c_v[LT - 1, t, k, rows, :], n + 1, 1), last)
        for k in range(LEV):
            value = pltpu.roll(u_v[LT - 1, k, rows, :], 9 + k, 1)
            last = jnp.where(lane == 8 + k, value, last)
        last = jnp.where(jnp.logical_and(lane >= 12, lane < 16), pltpu.roll(last, 4, 1), last)
        pack_first[rows, :] = first
        pack_last[rows, :] = last
    for j in range(LT):
        cols = slice(j * 128, j * 128 + 128)
        d_n = d_v[j, 0:8, :].astype(F32)[0:1, :]
        d_s = d_v[j, ROWS - 8 : ROWS, :].astype(F32)[7:8, :]
        for n in range(8):
            t, k = n // LEV, n % LEV
            pack_n[n : n + 1, cols] = c_v[j, t, k, 0:1, :]
            pack_s[n : n + 1, cols] = c_v[j, t, k, ROWS - 1 : ROWS, :]
            pack_s[8 + n : 9 + n, cols] = v_v[j, k, ROWS - 1 : ROWS, :]
        pack_n[8:16, cols] = zeros
        pack_n[16:24, cols] = jnp.broadcast_to(d_n, (8, 128))
        pack_s[16:24, cols] = jnp.broadcast_to(d_s, (8, 128))
        pack_f[j] = pack_s[0:8, cols]
        pack_f[LT, j : j + 1, :] = d_s

    to_west.start()
    to_east.start()

    @pl.when(jnp.logical_not(bottom))
    def _():
        to_south.start()

    @pl.when(jnp.logical_not(top))
    def _():
        to_north.start()

    steps = range(1, n_lon // 2)

    def fold_copy(step):
        return pltpu.make_async_remote_copy(
            src_ref=pack_f,
            dst_ref=fold.at[half, chip],
            send_sem=fsend_sem.at[step],
            recv_sem=frecv_sem.at[chip],
            device_id=lon(2 * step),
            device_id_type=MESH,
        )

    def fold_arrival(step):
        source = lax.rem(chip - step + n_lon // 2, n_lon // 2)
        return pltpu.make_async_remote_copy(
            src_ref=pack_f,
            dst_ref=fold.at[half, source],
            send_sem=fsend_sem.at[step],
            recv_sem=frecv_sem.at[source],
            device_id=lon(2 * step),
            device_id_type=MESH,
        )

    def fold_sibling(which):
        return pltpu.make_async_remote_copy(
            src_ref=fold.at[which],
            dst_ref=fold.at[which],
            send_sem=fsend_sem.at[0],
            recv_sem=frecv_sem.at[n_lon // 2],
            device_id=lon(1 - 2 * half),
            device_id_type=MESH,
        )

    own_fold = pltpu.make_async_copy(pack_f, fold.at[half, chip], local_sem.at[1])

    @pl.when(top)
    def _():
        own_fold.start()
        for step in steps:
            fold_copy(step).start()

    own_packs = [
        pltpu.make_async_copy(src, dst, local_sem.at[3 + i])
        for i, (src, dst) in enumerate(
            ((pack_first, own_first), (pack_last, own_last), (pack_n, own_n), (pack_s, own_s))
        )
    ]
    for c in own_packs:
        c.start()
    for i, (_, dst) in enumerate(planes):
        pltpu.make_async_copy(dst, dst, plane_sem.at[i]).wait()
    list_1.wait_recv()
    list_2.wait_recv()
    to_smem = pltpu.make_async_copy(lists, lists_s, local_sem.at[2])
    to_smem.start()
    to_smem.wait()
    places = []
    for slot, column_id in enumerate((owned[0, 0, 0], lists_s[0, 0, 1], lists_s[1, 0, 2])):
        info[slot] = jnp.where(column_id >= 0, column_id - x * LT, -1)
        places.append(jnp.clip(column_id - x * LT, 0, LT - 1))

    def hook(i):
        @pl.when(jnp.logical_and(top, i == 5))
        def _():
            own_fold.wait()
            for step in steps:
                fold_arrival(step).wait_recv()
            fold_sibling(half).start()

    ice_tiles(
        places, (ue_v, un_v, mass_v, str_v, mask_v, d_v, u_v, v_v), con, st, rolled, res, hook
    )

    list_1.wait_send()
    list_2.wait_send()
    to_west.wait()
    to_east.wait()
    for c in own_packs:
        c.wait()
    for j in range(LT):
        put(j).wait()

    @pl.when(jnp.logical_not(bottom))
    def _():
        to_south.wait_send()
        to_north.wait_recv()

    @pl.when(jnp.logical_not(top))
    def _():
        to_north.wait_send()
        to_south.wait_recv()

    @pl.when(top)
    def _():
        for step in steps:
            fold_copy(step).wait_send()
        fold_sibling(half).wait_send()
        fold_sibling(1 - half).wait_recv()


def exchange_and_ice(n_lon, n_lat, owned, state, depth, ivel, mass, strength, mask):
    anywhere = pl.BlockSpec(memory_space=pl.ANY)
    plane = pltpu.VMEM((LT, ROWS, 128), F32)
    column = jax.ShapeDtypeStruct((ROWS, 128), F32)
    rows = jax.ShapeDtypeStruct((24, COLS), F32)

    def body(*refs):
        exchange_kernel(n_lon, n_lat, *refs)

    return pl.pallas_call(
        body,
        name="exchange_and_ice",
        out_shape=(
            column,
            column,
            rows,
            rows,
            column,
            column,
            rows,
            rows,
            jax.ShapeDtypeStruct((2, n_lon // 2, LT + 1, 8, 128), F32),
            jax.ShapeDtypeStruct((LT, 8, ROWS, 128), F32),
            jax.ShapeDtypeStruct((SLOTS, 2, TILE, TILE), F32),
            jax.ShapeDtypeStruct((SLOTS,), I32),
        ),
        in_specs=[pl.BlockSpec(memory_space=pltpu.HBM)] * 7,
        out_specs=(anywhere,) * 10
        + (pl.BlockSpec(memory_space=pltpu.VMEM), pl.BlockSpec(memory_space=pltpu.SMEM)),
        scratch_shapes=[
            pltpu.VMEM((LT, 2, LEV, ROWS + 8, 128), F32),
            pltpu.VMEM((LT, LEV, ROWS, 128), F32),
            pltpu.VMEM((LT, LEV, ROWS, 128), F32),
            pltpu.VMEM((LT, ROWS + 8, 128), I32),
            plane,
            plane,
            plane,
            plane,
            pltpu.VMEM((LT, ROWS, 128), I32),
            pltpu.VMEM((2, 8, ROWS, 128), F32),
            pltpu.VMEM((2, ROWS, 128), F32),
            pltpu.VMEM((2, 8, ROWS, 128), F32),
            pltpu.VMEM((8, ROWS + 8, 128), F32),
            pltpu.VMEM((8, ROWS, 128), F32),
            pltpu.VMEM((LT, 8, ROWS, 128), F32),
            pltpu.VMEM((ROWS, 128), F32),
            pltpu.VMEM((ROWS, 128), F32),
            pltpu.VMEM((24, COLS), F32),
            pltpu.VMEM((24, COLS), F32),
            pltpu.VMEM((LT + 1, 8, 128), F32),
            pltpu.VMEM((8, 128), I32),
            pltpu.VMEM((2, 8, 128), I32),
            pltpu.SMEM((2, 8, 128), I32),
            pltpu.SMEM((1, 1, SLOTS), I32),
            pltpu.VMEM((SLOTS, 6, TILE, TILE), F32),
            pltpu.VMEM((SLOTS, 5, TILE, TILE), F32),
            pltpu.VMEM((SLOTS, 4, TILE, TILE), F32),
            pltpu.SemaphoreType.DMA((4, LT)),
            pltpu.SemaphoreType.DMA((5,)),
            pltpu.SemaphoreType.DMA((LT,)),
            pltpu.SemaphoreType.DMA((6,)),
            pltpu.SemaphoreType.DMA((6,)),
            pltpu.SemaphoreType.DMA((n_lon // 2,)),
            pltpu.SemaphoreType.DMA((n_lon // 2 + 1,)),
            pltpu.SemaphoreType.DMA((7,)),
        ],
        compiler_params=pltpu.CompilerParams(
            collective_id=0, has_side_effects=True, vmem_limit_bytes=28 * 2**20
        ),
    )(owned, state, depth, ivel, mass, strength, mask)


def ocean_kernel(
    n_lon,
    n_lat,
    partner,
    info,
    interim,
    depth,
    vmix,
    ivel,
    he,
    hw,
    hs,
    hn,
    own_first,
    own_last,
    own_n,
    own_s,
    fold,
    res,
    out,
    out_ice,
    p_v,
    d_v,
    vm_v,
    o_v,
    ice_v,
    he_v,
    hw_v,
    hs_v,
    hn_v,
    first_v,
    last_v,
    n_v,
    s_v,
    fold_v,
    win,
    west_h,
    east_h,
    south_h,
    north_h,
    in_sem,
    out_sem,
    sem,
):
    y = lax.axis_index("lat")
    top = y == n_lat - 1
    bottom = y == 0
    lane, row = iotas()
    lane16 = lax.broadcasted_iota(I32, (16, 128), 1)

    small = [
        pltpu.make_async_copy(src, dst, sem.at[i])
        for i, (src, dst) in enumerate(
            (
                (he, he_v),
                (hw, hw_v),
                (hs, hs_v),
                (hn, hn_v),
                (own_first, first_v),
                (own_last, last_v),
                (own_n, n_v),
                (own_s, s_v),
            )
        )
    ]
    get_fold = pltpu.make_async_copy(fold, fold_v, sem.at[8])
    get_ice = pltpu.make_async_copy(ivel, ice_v, sem.at[9])
    put_ice = pltpu.make_async_copy(ice_v, out_ice, sem.at[10])

    def fetch(j):
        cols = slice(j * 128, j * 128 + 128)
        return [
            pltpu.make_async_copy(interim.at[j], p_v.at[j], in_sem.at[0, j]),
            pltpu.make_async_copy(depth.at[:, cols], d_v.at[j], in_sem.at[1, j]),
            pltpu.make_async_copy(vmix.at[:, :, cols], vm_v.at[j], in_sem.at[2, j]),
        ]

    def put(j):
        cols = slice(j * 128, j * 128 + 128)
        return pltpu.make_async_copy(o_v.at[j], out.at[:, :, :, cols], out_sem.at[j])

    def patch(slot):
        at = pl.multiple_of(jnp.clip(info[slot], 0, LT - 1) * 128, 128)
        return pltpu.make_async_copy(res.at[slot], ice_v.at[:, :, pl.ds(at, 128)], sem.at[11 + slot])

    @pl.when(top)
    def _():
        get_fold.start()

    for c in small:
        c.start()
    get_ice.start()
    for j in range(LT):
        for c in fetch(j):
            c.start()
    for c in small:
        c.wait()

    @pl.when(top)
    def _():
        get_fold.wait()
        base = partner[COLS - 1]
        tile0 = lax.div(base, 128)
        shift = lax.rem(base, 128)
        for m in range(LT + 1):
            t = lax.rem(tile0 + m, n_lon * LT)
            dev = lax.div(t, LT)
            j = lax.rem(t, LT)
            half, chip = lax.rem(dev, 2), lax.div(dev, 2)
            win[m, 0:8, :] = fold_v[half, chip, j]
            win[m, 8:9, :] = fold_v[half, chip, LT, pl.ds(j, 1), :]
        back = lax.rem(128 - shift, 128)
        values = []
        for m in range(LT):
            near = pltpu.roll(win[m], back, 1)
            far = pltpu.roll(win[m + 1], back, 1)
            values.append(jnp.where(lane16 < 128 - shift, near, far))
        for bit in (1, 2, 4, 8, 16, 32, 64):
            odd = (lane16 & bit) != 0
            values = [
                jnp.where(odd, pltpu.roll(value, bit, 1), pltpu.roll(value, 128 - bit, 1))
                for value in values
            ]
        for m in range(LT):
            at = (LT - 1 - m) * 128
            hn_v[0:8, at : at + 128] = values[m][0:8, :]
            hn_v[16:24, at : at + 128] = jnp.broadcast_to(values[m][8:9, :], (8, 128))

    @pl.when(bottom)
    def _():
        hs_v[...] = jnp.zeros((24, COLS), F32)

    level = (lane & 3).astype(F32)
    for b in range(NB):
        rows = slice(b * 8, b * 8 + 8)
        pack, own = hw_v[rows, :], first_v[rows, :]
        both = jnp.minimum(pltpu.roll(pack, 112, 1), pltpu.roll(own, 112, 1))
        far, near = face(both, level, pltpu.roll(pack, 120, 1))
        west_h[rows, :] = pack * near - own * far
        pack, own = he_v[rows, :], last_v[rows, :]
        both = jnp.minimum(pltpu.roll(pack, 112, 1), pltpu.roll(own, 112, 1))
        far, near = face(both, level, pltpu.roll(own, 120, 1))
        east_h[rows, :] = pack * far - own * near
    level = (row & 3).astype(F32)
    for j in range(LT):
        cols = slice(j * 128, j * 128 + 128)
        far, near = face(jnp.minimum(s_v[16:24, cols], hn_v[16:24, cols]), level, s_v[8:16, cols])
        north_h[:, cols] = hn_v[0:8, cols] * far - s_v[0:8, cols] * near
        far, near = face(jnp.minimum(n_v[16:24, cols], hs_v[16:24, cols]), level, hs_v[8:16, cols])
        south_h[:, cols] = hs_v[0:8, cols] * near - n_v[0:8, cols] * far

    def rhs(j, n, b):
        rows = slice(b * 8, b * 8 + 8)
        value = p_v[j, n, rows, :]
        if j == 0:
            west = west_h[rows, :] if n == 0 else pltpu.roll(west_h[rows, :], 128 - n, 1)
            value = value + jnp.where(lane == 0, west, 0.0)
        if j == LT - 1:
            value = value + jnp.where(lane == 127, pltpu.roll(east_h[rows, :], 127 - n, 1), 0.0)
        cols = slice(j * 128, j * 128 + 128)
        if b == 0:
            rim = jnp.broadcast_to(south_h[n : n + 1, cols], (8, 128))
            value = value + jnp.where(row == 0, rim, 0.0)
        if b == NB - 1:
            rim = jnp.broadcast_to(north_h[n : n + 1, cols], (8, 128))
            value = value + jnp.where(row == 7, rim, 0.0)
        return value

    for j in range(LT):
        for c in fetch(j):
            c.wait()
        if j == 2:
            get_ice.wait()
            for slot in range(SLOTS):

                @pl.when(info[slot] >= 0)
                def _(slot=slot):
                    patch(slot).start()

        if j == 4:
            for slot in range(SLOTS):

                @pl.when(info[slot] >= 0)
                def _(slot=slot):
                    patch(slot).wait()

            put_ice.start()
        for b in range(NB):
            rows = slice(b * 8, b * 8 + 8)
            own = d_v[j, rows, :]
            g = [jnp.where(own > k, vm_v[j, k, rows, :] * 0.25, 0.0) for k in range(LEV)]
            i0 = recip((1.0 + g[0]) + g[1])
            u0 = g[1] * i0
            i1 = recip((1.0 + g[1]) + g[2] - g[1] * u0)
            u1 = g[2] * i1
            i2 = recip((1.0 + g[2]) + g[3] - g[2] * u1)
            u2 = g[3] * i2
            i3 = recip((1.0 + g[3]) - g[3] * u2)
            for t in range(2):
                f = [rhs(j, t * LEV + k, b) for k in range(LEV)]
                r0 = f[0] * i0
                r1 = (f[1] + g[1] * r0) * i1
                r2 = (f[2] + g[2] * r1) * i2
                x3 = (f[3] + g[3] * r2) * i3
                x2 = r2 + u2 * x3
                x1 = r1 + u1 * x2
                x0 = r0 + u0 * x1
                for k, value in enumerate((x0, x1, x2, x3)):
                    o_v[j, t, k, rows, :] = value
        put(j).start()

    for j in range(LT):
        put(j).wait()
    put_ice.wait()


def ocean(n_lon, n_lat, *operands):
    anywhere = pl.BlockSpec(memory_space=pl.ANY)
    smem = pl.BlockSpec(memory_space=pltpu.SMEM)
    column = pltpu.VMEM((ROWS, 128), F32)
    rows = pltpu.VMEM((24, COLS), F32)

    def body(*refs):
        ocean_kernel(n_lon, n_lat, *refs)

    return pl.pallas_call(
        body,
        name="ocean",
        out_shape=(
            jax.ShapeDtypeStruct((2, LEV, ROWS, COLS), F32),
            jax.ShapeDtypeStruct((2, ROWS, COLS), F32),
        ),
        in_specs=[smem, smem] + [anywhere] * (len(operands) - 2),
        out_specs=(anywhere, anywhere),
        scratch_shapes=[
            pltpu.VMEM((LT, 8, ROWS, 128), F32),
            pltpu.VMEM((LT, ROWS, 128), I32),
            pltpu.VMEM((LT, LEV, ROWS, 128), F32),
            pltpu.VMEM((LT, 2, LEV, ROWS, 128), F32),
            pltpu.VMEM((2, ROWS, COLS), F32),
            column,
            column,
            rows,
            rows,
            column,
            column,
            rows,
            rows,
            pltpu.VMEM((2, n_lon // 2, LT + 1, 8, 128), F32),
            pltpu.VMEM((LT + 1, 16, 128), F32),
            column,
            column,
            pltpu.VMEM((8, COLS), F32),
            pltpu.VMEM((8, COLS), F32),
            pltpu.SemaphoreType.DMA((3, LT)),
            pltpu.SemaphoreType.DMA((LT,)),
            pltpu.SemaphoreType.DMA((11 + SLOTS,)),
        ],
        compiler_params=pltpu.CompilerParams(vmem_limit_bytes=20 * 2**20),
    )(*operands)


def on_device(state, depth, vmix, partner, ivel, mass, strength, mask, owned):
    n_lon, n_lat = lax.axis_size("lon"), lax.axis_size("lat")
    in_hbm = [
        pltpu.with_memory_space_constraint(value, pltpu.HBM)
        for value in (owned, state, depth, ivel, mass, strength, mask)
    ]
    *rims, interim, res, info = exchange_and_ice(n_lon, n_lat, *in_hbm)
    return ocean(n_lon, n_lat, partner, info, interim, depth, vmix, ivel, *rims, res)


def solution(mesh):
    return jax.shard_map(
        on_device,
        mesh=mesh,
        in_specs=(
            P(None, None, "lat", "lon"),
            P("lat", "lon"),
            P(None, "lat", "lon"),
            P("lon"),
            P(None, "lat", "lon"),
            P("lat", "lon"),
            P("lat", "lon"),
            P("lat", "lon"),
            P("lat", "lon", None),
        ),
        out_specs=(P(None, None, "lat", "lon"), P(None, "lat", "lon")),
        check_vma=False,
    )
```

```python
import jax
import jax.numpy as jnp
from jax import lax
from jax.experimental import pallas as pl
from jax.experimental.pallas import tpu as pltpu
from jax.sharding import PartitionSpec as P

MESH = pl.DeviceIdType.MESH
LEV = 4
TILE = 128
ROWS = 128
COLS = 1024
LT = COLS // TILE
SLOTS = 3
SUBCYCLES = 32
NB = ROWS // 8
F32 = jnp.float32
I32 = jnp.int32


def iotas():
    lane = lax.broadcasted_iota(I32, (8, 128), 1)
    row = lax.broadcasted_iota(I32, (8, 128), 0)
    return lane, row


def recip(value):
    r = pltpu.reciprocal(value, approx=True)
    return r * (2.0 - value * r)


def face(open_depth, level, velocity):
    is_open = open_depth > level
    z = jnp.where(is_open, velocity * 0.25, 0.0)
    e = jnp.where(is_open, 0.125, 0.0)
    far = e - jnp.minimum(z, 0.0)
    return far, far + z


def ice_tiles(places, planes, con, st, rolled, res_ref, hook):
    lane, row = iotas()
    not_first, not_last = lane != 0, lane != 127
    tiles = range(len(places))
    ue_v, un_v, mass_v, str_v, mask_v, depth_v, uo_v, vo_v = planes
    zeros = jnp.zeros((8, 128), F32)

    def at(k):
        return slice(k * 8, k * 8 + 8)

    def north(value):
        return jnp.where(row == 7, 0.0, pltpu.roll(value, 7, 0))

    def south(value):
        return jnp.where(row == 0, 0.0, pltpu.roll(value, 1, 0))

    def keep_east(t, f, k, value):
        pltpu.store(rolled.at[t, f, at(k), :], pltpu.roll(value, 127, 1), mask=not_last)

    def keep_west(t, f, k, value):
        pltpu.store(rolled.at[t, f, at(k), :], pltpu.roll(value, 1, 1), mask=not_first)

    for t in tiles:
        pos = places[t]
        for b in range(NB):
            rows = slice(b * 8, b * 8 + 8)
            spread = pl.ds((b % 2) * 64 + b // 2, 8, stride=8)
            mass, strength = mass_v[pos, rows, :], str_v[pos, rows, :]
            ice = jnp.logical_and(mask_v[pos, rows, :] > 0, depth_v[pos, rows, :] > 0)
            mass = jnp.where(ice, mass, 0.0)
            strength = jnp.where(ice, strength, 0.0)
            inertia = mass * 2.0
            diag = inertia + 1.0
            turn = mass * 0.5
            inv = 1.0 / (diag * diag + turn * turn)
            con[t, 0, spread, :] = inertia
            con[t, 1, spread, :] = diag * inv
            con[t, 2, spread, :] = turn * inv
            con[t, 3, spread, :] = strength * (1.0 / 12.0)
            con[t, 4, spread, :] = uo_v[pos, 0, rows, :] * 0.5
            con[t, 5, spread, :] = vo_v[pos, 0, rows, :] * 0.5
            st[t, 0, spread, :] = ue_v[pos, rows, :] * 0.5
            st[t, 1, spread, :] = un_v[pos, rows, :] * 0.5
            st[t, 2, spread, :] = strength * 0.25
    for t in tiles:
        for k in range(NB):
            for f in range(4):
                rolled[t, f, at(k), :] = zeros
    for t in tiles:
        for k in range(NB):
            p4 = st[t, 2, at(k), :]
            p_south = st[t, 2, at(k - 1), :] if k else south(st[t, 2, at(NB - 1), :])
            p_west = jnp.where(lane == 0, 0.0, pltpu.roll(p4, 1, 1))
            con[t, 4, at(k), :] = con[t, 4, at(k), :] - (p4 - p_west)
            con[t, 5, at(k), :] = con[t, 5, at(k), :] - (p4 - p_south)
            st[t, 3, at(k), :] = p4
            st[t, 4, at(k), :] = zeros
            keep_east(t, 0, k, st[t, 0, at(k), :])
            keep_east(t, 1, k, st[t, 1, at(k), :])

    keep = 1.0 / 1.5

    def stress(t, k):
        u, v = st[t, 0, at(k), :], st[t, 1, at(k), :]
        if k < NB - 1:
            un, vn = st[t, 0, at(k + 1), :], st[t, 1, at(k + 1), :]
        else:
            un, vn = north(st[t, 0, at(0), :]), north(st[t, 1, at(0), :])
        d1 = rolled[t, 0, at(k), :] - u
        d2 = vn - v
        h = (un - u) + (rolled[t, 1, at(k), :] - v)
        div = d1 + d2
        ten = d1 - d2
        p = div + div
        r = ten * 0.5
        q = con[t, 3, at(k), :] * lax.rsqrt((p * p + ten * ten) + (h * h + 0.25))
        sx = st[t, 2, at(k), :] * keep + q * (p + r)
        sy = st[t, 3, at(k), :] * keep + q * (p - r)
        sh = st[t, 4, at(k), :] * keep + q * h
        st[t, 2, at(k), :] = sx
        st[t, 3, at(k), :] = sy
        st[t, 4, at(k), :] = sh
        keep_west(t, 2, k, sx)
        keep_west(t, 3, k, sh)

    def momentum(t, k):
        u, v, sx, sy, sh = [st[t, f, at(k), :] for f in range(5)]
        if k:
            sy_s, sh_s = st[t, 3, at(k - 1), :], st[t, 4, at(k - 1), :]
        else:
            sy_s, sh_s = south(st[t, 3, at(NB - 1), :]), south(st[t, 4, at(NB - 1), :])
        inertia, al, be, kx, ky = [con[t, f, at(k), :] for f in (0, 1, 2, 4, 5)]
        rx = (inertia * u + kx) + ((sx - rolled[t, 2, at(k), :]) + (sh - sh_s))
        ry = (inertia * v + ky) + ((sh - rolled[t, 3, at(k), :]) + (sy - sy_s))
        u = al * rx + be * ry
        v = al * ry - be * rx
        st[t, 0, at(k), :] = u
        st[t, 1, at(k), :] = v
        keep_east(t, 0, k, u)
        keep_east(t, 1, k, v)

    def cycle(_, carry):
        for t in tiles:
            for k in range(NB):
                stress(t, k)
        for t in tiles:
            for k in range(NB):
                momentum(t, k)
        return carry

    def four(i, carry):
        hook(i)
        for _ in range(4):
            cycle(i, carry)
        return carry

    lax.fori_loop(0, SUBCYCLES // 4, four, 0)
    for t in tiles:
        for k in range(NB):
            res_ref[t, 0, pl.ds(k, 8, stride=NB), :] = st[t, 0, at(k), :] * 2.0
            res_ref[t, 1, pl.ds(k, 8, stride=NB), :] = st[t, 1, at(k), :] * 2.0


def exchange_kernel(
    n_lon,
    n_lat,
    owned_hbm,
    state,
    depth,
    ivel,
    mass,
    strength,
    mask,
    vmix,
    he,
    hw,
    hs,
    hn,
    own_first,
    own_last,
    own_n,
    own_s,
    fold,
    interim,
    vmix_out,
    depth_out,
    ivel_out,
    res,
    info,
    c_v,
    u_v,
    v_v,
    d_v,
    ue_v,
    un_v,
    mass_v,
    str_v,
    mask_v,
    blk_first,
    blk_last,
    d_rim,
    c_rolled,
    d_rolled,
    h_west,
    h_north,
    part,
    pack_first,
    pack_last,
    pack_n,
    pack_s,
    pack_f,
    my_list,
    lists,
    lists_s,
    owned,
    con,
    st,
    rolled,
    in_sem,
    plane_sem,
    send_sem,
    recv_sem,
    fsend_sem,
    frecv_sem,
    local_sem,
    rim_sem,
    out_sem,
):
    x = lax.axis_index("lon")
    y = lax.axis_index("lat")
    lane, row = iotas()
    is_last, not_last = lane == 127, lane != 127
    is_first, not_first = lane == 0, lane != 0
    top = y == n_lat - 1
    bottom = y == 0
    half = lax.rem(x, 2)
    chip = lax.div(x, 2)

    def lon(step):
        return {"lon": lax.rem(x + step + n_lon, n_lon), "lat": y}

    def lat(step):
        return {"lon": x, "lat": y + step}

    get_owned = pltpu.make_async_copy(owned_hbm, owned, local_sem.at[0])
    get_owned.start()
    barrier = pltpu.get_barrier_semaphore()

    def greet(device):
        pl.semaphore_signal(barrier, inc=1, device_id=device, device_id_type=MESH)

    for step in (1, -1, 2, -2):
        greet(lon(step))

    fold_extra = range(4, n_lon - 2, 2)

    @pl.when(top)
    def _():
        for step in fold_extra:
            greet(lon(step))

    @pl.when(jnp.logical_not(top))
    def _():
        greet(lat(1))

    @pl.when(jnp.logical_not(bottom))
    def _():
        greet(lat(-1))

    def barrier_wait():
        @pl.when(jnp.logical_and(top, jnp.logical_not(bottom)))
        def _():
            pl.semaphore_wait(barrier, 5 + len(fold_extra))

        @pl.when(jnp.logical_and(bottom, jnp.logical_not(top)))
        def _():
            pl.semaphore_wait(barrier, 5)

        @pl.when(jnp.logical_not(jnp.logical_or(bottom, top)))
        def _():
            pl.semaphore_wait(barrier, 6)

    def fetch(j):
        cols = pl.ds(pl.multiple_of(j * 128, 128), 128)
        rows = pl.ds(0, ROWS)
        return [
            pltpu.make_async_copy(state.at[0:2, :, :, cols], c_v.at[j, :, :, rows, :], in_sem.at[0, j]),
            pltpu.make_async_copy(depth.at[:, cols], d_v.at[j, rows, :], in_sem.at[1, j]),
            pltpu.make_async_copy(state.at[2, :, :, cols], u_v.at[j], in_sem.at[2, j]),
            pltpu.make_async_copy(state.at[3, :, :, cols], v_v.at[j], in_sem.at[3, j]),
        ]

    rims = [
        pltpu.make_async_copy(state.at[0:2, :, pl.ds(0, 8), :], blk_first, rim_sem.at[0]),
        pltpu.make_async_copy(state.at[0:2, :, pl.ds(ROWS - 8, 8), :], blk_last.at[0:2], rim_sem.at[1]),
        pltpu.make_async_copy(state.at[3, :, pl.ds(ROWS - 8, 8), :], blk_last.at[2], rim_sem.at[2]),
        pltpu.make_async_copy(depth.at[pl.ds(0, 8), :], d_rim.at[0], rim_sem.at[3]),
        pltpu.make_async_copy(depth.at[pl.ds(ROWS - 8, 8), :], d_rim.at[1], rim_sem.at[4]),
    ]
    for c in rims:
        c.start()
    for j in range(LT):
        for c in fetch(j):
            c.start()
    planes = [(ivel.at[0], ue_v), (ivel.at[1], un_v), (mass, mass_v), (strength, str_v), (mask, mask_v)]
    for i, (src, dst) in enumerate(planes):
        for j in range(LT):
            pltpu.make_async_copy(
                src.at[:, j * 128 : j * 128 + 128], dst.at[j], plane_sem.at[i]
            ).start()

    passed = [pltpu.make_async_copy(ivel, ivel_out, out_sem.at[LT])] + [
        pltpu.make_async_copy(vmix.at[:, :, j * 128 : j * 128 + 128], vmix_out.at[j], out_sem.at[j])
        for j in range(LT)
    ]
    for c in passed:
        c.start()

    get_owned.wait()
    my_list[...] = jnp.where(
        lane == 0, owned[0, 0, 0], jnp.where(lane == 1, owned[0, 0, 1], owned[0, 0, 2])
    )

    def remote(src, dst, i, device):
        return pltpu.make_async_remote_copy(
            src_ref=src,
            dst_ref=dst,
            send_sem=send_sem.at[i],
            recv_sem=recv_sem.at[i],
            device_id=device,
            device_id_type=MESH,
        )

    list_1 = remote(my_list, lists.at[0], 0, lon(-1))
    list_2 = remote(my_list, lists.at[1], 1, lon(-2))
    to_smem = pltpu.make_async_copy(lists, lists_s, local_sem.at[2])
    to_west = remote(pack_first, he, 2, lon(-1))
    to_east = remote(pack_last, hw, 3, lon(1))
    to_south = remote(pack_n, hn, 4, lat(-1))
    to_north = remote(pack_s, hs, 5, lat(1))

    zeros = jnp.zeros((8, 128), F32)
    beyond = slice(ROWS, ROWS + 8)
    for j in range(LT):
        d_v[j, beyond, :] = jnp.zeros((8, 128), I32)
        for n in range(8):
            c_v[j, n // LEV, n % LEV, beyond, :] = zeros
    for n in range(8):
        h_north[n, 0:8, :] = zeros
        for b in range(NB):
            h_west[0, n, b * 8 : b * 8 + 8, :] = zeros
    for c in rims:
        c.wait()
    for j in range(LT):
        cols = slice(j * 128, j * 128 + 128)
        d_n = d_rim[0, :, cols].astype(F32)[0:1, :]
        d_s = d_rim[1, :, cols].astype(F32)[7:8, :]
        for n in range(8):
            t, k = n // LEV, n % LEV
            pack_n[n : n + 1, cols] = blk_first[t, k, 0:1, cols]
            pack_s[n : n + 1, cols] = blk_last[t, k, 7:8, cols]
            pack_s[8 + n : 9 + n, cols] = blk_last[2, k, 7:8, cols]
        pack_n[8:16, cols] = zeros
        pack_n[16:24, cols] = jnp.broadcast_to(d_n, (8, 128))
        pack_s[16:24, cols] = jnp.broadcast_to(d_s, (8, 128))
        pack_f[j] = pack_s[0:8, cols]
        pack_f[LT, j : j + 1, :] = d_s

    steps = range(1, n_lon // 2)

    def fold_copy(step):
        return pltpu.make_async_remote_copy(
            src_ref=pack_f,
            dst_ref=fold.at[half, chip],
            send_sem=fsend_sem.at[step],
            recv_sem=frecv_sem.at[chip],
            device_id=lon(2 * step),
            device_id_type=MESH,
        )

    def fold_arrival(step):
        source = lax.rem(chip - step + n_lon // 2, n_lon // 2)
        return pltpu.make_async_remote_copy(
            src_ref=pack_f,
            dst_ref=fold.at[half, source],
            send_sem=fsend_sem.at[step],
            recv_sem=frecv_sem.at[source],
            device_id=lon(2 * step),
            device_id_type=MESH,
        )

    def fold_sibling(which):
        return pltpu.make_async_remote_copy(
            src_ref=fold.at[which],
            dst_ref=fold.at[which],
            send_sem=fsend_sem.at[0],
            recv_sem=frecv_sem.at[n_lon // 2],
            device_id=lon(1 - 2 * half),
            device_id_type=MESH,
        )

    own_fold = pltpu.make_async_copy(pack_f, fold.at[half, chip], local_sem.at[1])

    for c in fetch(0):
        c.wait()
    for b in range(NB):
        rows = slice(b * 8, b * 8 + 8)
        pltpu.store(
            d_rolled.at[0, rows, :], pltpu.roll(d_v[0, rows, :].astype(F32), 127, 1), mask=not_last
        )
        for n in range(8):
            value = pltpu.roll(c_v[0, n // LEV, n % LEV, rows, :], 127, 1)
            pltpu.store(c_rolled.at[0, n, rows, :], value, mask=not_last)

    def column(j, carry):
        @pl.when(j < LT - 1)
        def _():
            for c in fetch(j + 1):
                c.wait()

        @pl.when(j == 2)
        def _():
            barrier_wait()
            list_1.start()
            list_2.start()

            @pl.when(jnp.logical_not(bottom))
            def _():
                to_south.start()

            @pl.when(jnp.logical_not(top))
            def _():
                to_north.start()

            @pl.when(top)
            def _():
                own_fold.start()
                for step in steps:
                    fold_copy(step).start()

        @pl.when(j == LT - 1)
        def _():
            list_1.wait_recv()
            list_2.wait_recv()
            to_smem.start()

        cur = lax.rem(j, 2)
        nxt = 1 - cur
        after = jnp.minimum(j + 1, LT - 1)
        inside = jnp.where(j < LT - 1, 1.0, 0.0)

        def roll_next(b):
            rows = slice(b * 8, b * 8 + 8)
            value = pltpu.roll(d_v[after, rows, :].astype(F32) * inside, 127, 1)
            pltpu.store(d_rolled.at[cur, rows, :], value, mask=is_last)
            pltpu.store(d_rolled.at[nxt, rows, :], value, mask=not_last)
            for n in range(8):
                value = pltpu.roll(c_v[after, n // LEV, n % LEV, rows, :], 127, 1)
                pltpu.store(c_rolled.at[cur, n, rows, :], value, mask=is_last)
                pltpu.store(c_rolled.at[nxt, n, rows, :], value, mask=not_last)

        def fluxes(b):
            rows = slice(b * 8, b * 8 + 8)
            ahead = slice(b * 8 + 1, b * 8 + 9)
            store = slice(b * 8 + 8, b * 8 + 16)
            behind = slice(b * 8 + 7, b * 8 + 15)
            own = d_v[j, rows, :].astype(F32)
            open_e = jnp.minimum(own, d_rolled[cur, rows, :])
            open_n = jnp.minimum(own, d_v[j, ahead, :].astype(F32))
            for k in range(LEV):
                e_far, e_near = face(open_e, k, u_v[j, k, rows, :])
                n_far, n_near = face(open_n, k, v_v[j, k, rows, :])
                for t in range(2):
                    n = t * LEV + k
                    c = c_v[j, t, k, rows, :]
                    east = c_rolled[cur, n, rows, :] * e_far - c * e_near
                    east_rolled = pltpu.roll(east, 1, 1)
                    pltpu.store(h_west.at[cur, n, rows, :], east_rolled, mask=not_first)
                    pltpu.store(h_west.at[nxt, n, rows, :], east_rolled, mask=is_first)
                    north = c_v[j, t, k, ahead, :] * n_far - c * n_near
                    h_north[n, store, :] = north
                    part[n, rows, :] = (c + east) + (north - h_north[n, behind, :])

        def finish(b):
            rows = slice(b * 8, b * 8 + 8)
            for n in range(8):
                interim[j, n, rows, :] = part[n, rows, :] - h_west[cur, n, rows, :]

        for b in range(NB + 6):
            if b < NB:
                roll_next(b)
            if 0 <= b - 3 < NB:
                fluxes(b - 3)
            if 0 <= b - 6 < NB:
                finish(b - 6)
        return carry

    lax.fori_loop(0, LT, column, 0)

    for b in range(NB):
        rows = slice(b * 8, b * 8 + 8)
        d_first = jnp.broadcast_to(d_v[0, rows, :].astype(F32)[:, 0:1], (8, 128))
        d_last = jnp.broadcast_to(d_v[LT - 1, rows, :].astype(F32)[:, 127:128], (8, 128))
        first, last = d_first, d_last
        for n in range(8):
            t, k = n // LEV, n % LEV
            value = c_v[0, t, k, rows, :]
            first = jnp.where(lane == n, value if n == 0 else pltpu.roll(value, n, 1), first)
            last = jnp.where(lane == n, pltpu.roll(c_v[LT - 1, t, k, rows, :], n + 1, 1), last)
        for k in range(LEV):
            value = pltpu.roll(u_v[LT - 1, k, rows, :], 9 + k, 1)
            last = jnp.where(lane == 8 + k, value, last)
        last = jnp.where(jnp.logical_and(lane >= 12, lane < 16), pltpu.roll(last, 4, 1), last)
        pack_first[rows, :] = first
        pack_last[rows, :] = last
    to_west.start()
    to_east.start()

    own_packs = [
        pltpu.make_async_copy(src, dst, local_sem.at[3 + i])
        for i, (src, dst) in enumerate(
            ((pack_first, own_first), (pack_last, own_last), (pack_n, own_n), (pack_s, own_s))
        )
    ]
    give_depth = pltpu.make_async_copy(d_v.at[:, pl.ds(0, ROWS), :], depth_out, out_sem.at[LT + 1])
    give_depth.start()
    for c in own_packs:
        c.start()
    for i, (_, dst) in enumerate(planes):
        pltpu.make_async_copy(dst, dst, plane_sem.at[i]).wait()
    to_smem.wait()
    places = []
    for slot, column_id in enumerate((owned[0, 0, 0], lists_s[0, 0, 1], lists_s[1, 0, 2])):
        info[slot] = jnp.where(column_id >= 0, column_id - x * LT, -1)
        places.append(jnp.clip(column_id - x * LT, 0, LT - 1))

    def hook(i):
        @pl.when(jnp.logical_and(top, i == 2))
        def _():
            own_fold.wait()
            for step in steps:
                fold_arrival(step).wait_recv()
            fold_sibling(half).start()

    ice_tiles(
        places, (ue_v, un_v, mass_v, str_v, mask_v, d_v, u_v, v_v), con, st, rolled, res, hook
    )

    list_1.wait_send()
    list_2.wait_send()
    to_west.wait()
    to_east.wait()
    give_depth.wait()
    for c in own_packs + passed:
        c.wait()
    @pl.when(jnp.logical_not(bottom))
    def _():
        to_south.wait_send()
        to_north.wait_recv()

    @pl.when(jnp.logical_not(top))
    def _():
        to_north.wait_send()
        to_south.wait_recv()

    @pl.when(top)
    def _():
        for step in steps:
            fold_copy(step).wait_send()
        fold_sibling(half).wait_send()
        fold_sibling(1 - half).wait_recv()


def exchange_and_ice(n_lon, n_lat, *operands):
    anywhere = pl.BlockSpec(memory_space=pl.ANY)
    inside = pl.BlockSpec(memory_space=pltpu.VMEM)
    plane = pltpu.VMEM((LT, ROWS, 128), F32)
    column = jax.ShapeDtypeStruct((ROWS, 128), F32)
    rows = jax.ShapeDtypeStruct((24, COLS), F32)

    def body(*refs):
        exchange_kernel(n_lon, n_lat, *refs)

    return pl.pallas_call(
        body,
        name="exchange_and_ice",
        out_shape=(
            column,
            column,
            rows,
            rows,
            column,
            column,
            rows,
            rows,
            jax.ShapeDtypeStruct((2, n_lon // 2, LT + 1, 8, 128), F32),
            jax.ShapeDtypeStruct((LT, 8, ROWS, 128), F32),
            jax.ShapeDtypeStruct((LT, LEV, ROWS, 128), F32),
            jax.ShapeDtypeStruct((LT, ROWS, 128), I32),
            jax.ShapeDtypeStruct((2, ROWS, COLS), F32),
            jax.ShapeDtypeStruct((SLOTS, 2, TILE, TILE), F32),
            jax.ShapeDtypeStruct((SLOTS,), I32),
        ),
        in_specs=[pl.BlockSpec(memory_space=pltpu.HBM)] * 8,
        out_specs=(anywhere,) * 9
        + (inside,)
        + (anywhere,) * 3
        + (inside, pl.BlockSpec(memory_space=pltpu.SMEM)),
        scratch_shapes=[
            pltpu.VMEM((LT, 2, LEV, ROWS + 8, 128), F32),
            pltpu.VMEM((LT, LEV, ROWS, 128), F32),
            pltpu.VMEM((LT, LEV, ROWS, 128), F32),
            pltpu.VMEM((LT, ROWS + 8, 128), I32),
            plane,
            plane,
            plane,
            plane,
            pltpu.VMEM((LT, ROWS, 128), I32),
            pltpu.VMEM((2, LEV, 8, COLS), F32),
            pltpu.VMEM((3, LEV, 8, COLS), F32),
            pltpu.VMEM((2, 8, COLS), I32),
            pltpu.VMEM((2, 8, ROWS, 128), F32),
            pltpu.VMEM((2, ROWS, 128), F32),
            pltpu.VMEM((2, 8, ROWS, 128), F32),
            pltpu.VMEM((8, ROWS + 8, 128), F32),
            pltpu.VMEM((8, ROWS, 128), F32),
            pltpu.VMEM((ROWS, 128), F32),
            pltpu.VMEM((ROWS, 128), F32),
            pltpu.VMEM((24, COLS), F32),
            pltpu.VMEM((24, COLS), F32),
            pltpu.VMEM((LT + 1, 8, 128), F32),
            pltpu.VMEM((8, 128), I32),
            pltpu.VMEM((2, 8, 128), I32),
            pltpu.SMEM((2, 8, 128), I32),
            pltpu.SMEM((1, 1, SLOTS), I32),
            pltpu.VMEM((SLOTS, 6, TILE, TILE), F32),
            pltpu.VMEM((SLOTS, 5, TILE, TILE), F32),
            pltpu.VMEM((SLOTS, 4, TILE, TILE), F32),
            pltpu.SemaphoreType.DMA((4, LT)),
            pltpu.SemaphoreType.DMA((5,)),
            pltpu.SemaphoreType.DMA((6,)),
            pltpu.SemaphoreType.DMA((6,)),
            pltpu.SemaphoreType.DMA((n_lon // 2,)),
            pltpu.SemaphoreType.DMA((n_lon // 2 + 1,)),
            pltpu.SemaphoreType.DMA((7,)),
            pltpu.SemaphoreType.DMA((5,)),
            pltpu.SemaphoreType.DMA((LT + 2,)),
        ],
        compiler_params=pltpu.CompilerParams(
            collective_id=0, has_side_effects=True, vmem_limit_bytes=22 * 2**20
        ),
    )(*operands)


def ocean_kernel(
    n_lon,
    n_lat,
    partner,
    info,
    p_v,
    vm_v,
    d_v,
    ivel,
    he,
    hw,
    hs,
    hn,
    own_first,
    own_last,
    own_n,
    own_s,
    fold,
    res,
    out,
    out_ice,
    o_v,
    hs_v,
    hn_v,
    win,
    west_h,
    east_h,
    south_h,
    north_h,
    out_sem,
    sem,
):
    y = lax.axis_index("lat")
    top = y == n_lat - 1
    bottom = y == 0
    lane, row = iotas()
    lane16 = lax.broadcasted_iota(I32, (16, 128), 1)

    put_ice = pltpu.make_async_copy(ivel, out_ice, sem.at[0])

    def put(j):
        cols = slice(j * 128, j * 128 + 128)
        return pltpu.make_async_copy(o_v.at[j], out.at[:, :, :, cols], out_sem.at[j])

    def patch(slot):
        at = pl.multiple_of(jnp.clip(info[slot], 0, LT - 1) * 128, 128)
        return pltpu.make_async_copy(res.at[slot], out_ice.at[:, :, pl.ds(at, 128)], sem.at[1 + slot])

    put_ice.start()
    hn_v[...] = hn[...]
    hs_v[...] = hs[...]

    @pl.when(top)
    def _():
        base = partner[COLS - 1]
        tile0 = lax.div(base, 128)
        shift = lax.rem(base, 128)
        for m in range(LT + 1):
            t = lax.rem(tile0 + m, n_lon * LT)
            dev = lax.div(t, LT)
            j = lax.rem(t, LT)
            half, chip = lax.rem(dev, 2), lax.div(dev, 2)
            win[m, 0:8, :] = fold[half, chip, j]
            win[m, 8:9, :] = fold[half, chip, LT, pl.ds(j, 1), :]
        back = lax.rem(128 - shift, 128)
        values = []
        for m in range(LT):
            near = pltpu.roll(win[m], back, 1)
            far = pltpu.roll(win[m + 1], back, 1)
            values.append(jnp.where(lane16 < 128 - shift, near, far))
        for bit in (1, 2, 4, 8, 16, 32, 64):
            odd = (lane16 & bit) != 0
            values = [
                jnp.where(odd, pltpu.roll(value, bit, 1), pltpu.roll(value, 128 - bit, 1))
                for value in values
            ]
        for m in range(LT):
            at = (LT - 1 - m) * 128
            hn_v[0:8, at : at + 128] = values[m][0:8, :]
            hn_v[16:24, at : at + 128] = jnp.broadcast_to(values[m][8:9, :], (8, 128))

    @pl.when(bottom)
    def _():
        hs_v[...] = jnp.zeros((24, COLS), F32)

    level = (lane & 3).astype(F32)
    for b in range(NB):
        rows = slice(b * 8, b * 8 + 8)
        pack, own = hw[rows, :], own_first[rows, :]
        both = jnp.minimum(pltpu.roll(pack, 112, 1), pltpu.roll(own, 112, 1))
        far, near = face(both, level, pltpu.roll(pack, 120, 1))
        west_h[rows, :] = pack * near - own * far
        pack, own = he[rows, :], own_last[rows, :]
        both = jnp.minimum(pltpu.roll(pack, 112, 1), pltpu.roll(own, 112, 1))
        far, near = face(both, level, pltpu.roll(own, 120, 1))
        east_h[rows, :] = pack * far - own * near
    level = (row & 3).astype(F32)
    for j in range(LT):
        cols = slice(j * 128, j * 128 + 128)
        far, near = face(jnp.minimum(own_s[16:24, cols], hn_v[16:24, cols]), level, own_s[8:16, cols])
        north_h[:, cols] = hn_v[0:8, cols] * far - own_s[0:8, cols] * near
        far, near = face(jnp.minimum(own_n[16:24, cols], hs_v[16:24, cols]), level, hs_v[8:16, cols])
        south_h[:, cols] = hs_v[0:8, cols] * near - own_n[0:8, cols] * far

    def rhs(j, n, b):
        rows = slice(b * 8, b * 8 + 8)
        value = p_v[j, n, rows, :]
        if j == 0:
            west = west_h[rows, :] if n == 0 else pltpu.roll(west_h[rows, :], 128 - n, 1)
            value = value + jnp.where(lane == 0, west, 0.0)
        if j == LT - 1:
            value = value + jnp.where(lane == 127, pltpu.roll(east_h[rows, :], 127 - n, 1), 0.0)
        cols = slice(j * 128, j * 128 + 128)
        if b == 0:
            rim = jnp.broadcast_to(south_h[n : n + 1, cols], (8, 128))
            value = value + jnp.where(row == 0, rim, 0.0)
        if b == NB - 1:
            rim = jnp.broadcast_to(north_h[n : n + 1, cols], (8, 128))
            value = value + jnp.where(row == 7, rim, 0.0)
        return value

    for j in range(LT):
        if j == 2:
            put_ice.wait()
            for slot in range(SLOTS):

                @pl.when(info[slot] >= 0)
                def _(slot=slot):
                    patch(slot).start()

        for b in range(NB):
            rows = slice(b * 8, b * 8 + 8)
            own = d_v[j, rows, :]
            g = [jnp.where(own > k, vm_v[j, k, rows, :] * 0.25, 0.0) for k in range(LEV)]
            i0 = recip((1.0 + g[0]) + g[1])
            u0 = g[1] * i0
            i1 = recip((1.0 + g[1]) + g[2] - g[1] * u0)
            u1 = g[2] * i1
            i2 = recip((1.0 + g[2]) + g[3] - g[2] * u1)
            u2 = g[3] * i2
            i3 = recip((1.0 + g[3]) - g[3] * u2)
            for t in range(2):
                f = [rhs(j, t * LEV + k, b) for k in range(LEV)]
                r0 = f[0] * i0
                r1 = (f[1] + g[1] * r0) * i1
                r2 = (f[2] + g[2] * r1) * i2
                x3 = (f[3] + g[3] * r2) * i3
                x2 = r2 + u2 * x3
                x1 = r1 + u1 * x2
                x0 = r0 + u0 * x1
                for k, value in enumerate((x0, x1, x2, x3)):
                    o_v[j, t, k, rows, :] = value
        put(j).start()

    for j in range(LT):
        put(j).wait()
    for slot in range(SLOTS):

        @pl.when(info[slot] >= 0)
        def _(slot=slot):
            patch(slot).wait()


def ocean(n_lon, n_lat, *operands):
    anywhere = pl.BlockSpec(memory_space=pl.ANY)
    smem = pl.BlockSpec(memory_space=pltpu.SMEM)
    inside = pl.BlockSpec(memory_space=pltpu.VMEM)
    column = pltpu.VMEM((ROWS, 128), F32)
    rows = pltpu.VMEM((24, COLS), F32)

    def body(*refs):
        ocean_kernel(n_lon, n_lat, *refs)

    return pl.pallas_call(
        body,
        name="ocean",
        out_shape=(
            jax.ShapeDtypeStruct((2, LEV, ROWS, COLS), F32),
            jax.ShapeDtypeStruct((2, ROWS, COLS), F32),
        ),
        in_specs=[smem, smem] + [inside] * (len(operands) - 2),
        out_specs=(anywhere, anywhere),
        scratch_shapes=[
            pltpu.VMEM((LT, 2, LEV, ROWS, 128), F32),
            rows,
            rows,
            pltpu.VMEM((LT + 1, 16, 128), F32),
            column,
            column,
            pltpu.VMEM((8, COLS), F32),
            pltpu.VMEM((8, COLS), F32),
            pltpu.SemaphoreType.DMA((LT,)),
            pltpu.SemaphoreType.DMA((1 + SLOTS,)),
        ],
        compiler_params=pltpu.CompilerParams(vmem_limit_bytes=10 * 2**20),
    )(*operands)


def on_device(state, depth, vmix, partner, ivel, mass, strength, mask, owned):
    n_lon, n_lat = lax.axis_size("lon"), lax.axis_size("lat")
    in_hbm = [
        pltpu.with_memory_space_constraint(value, pltpu.HBM)
        for value in (owned, state, depth, ivel, mass, strength, mask, vmix)
    ]
    *rims, interim, vmix_in, depth_in, ivel_in, res, info = exchange_and_ice(n_lon, n_lat, *in_hbm)
    return ocean(n_lon, n_lat, partner, info, interim, vmix_in, depth_in, ivel_in, *rims, res)


def solution(mesh):
    return jax.shard_map(
        on_device,
        mesh=mesh,
        in_specs=(
            P(None, None, "lat", "lon"),
            P("lat", "lon"),
            P(None, "lat", "lon"),
            P("lon"),
            P(None, "lat", "lon"),
            P("lat", "lon"),
            P("lat", "lon"),
            P("lat", "lon"),
            P("lat", "lon", None),
        ),
        out_specs=(P(None, None, "lat", "lon"), P(None, "lat", "lon")),
        check_vma=False,
    )
```

```python
import jax
import jax.numpy as jnp
from jax import lax
from jax.experimental import pallas as pl
from jax.experimental.pallas import tpu as pltpu
from jax.sharding import PartitionSpec as P

MESH = pl.DeviceIdType.MESH
LEV = 4
TILE = 128
ROWS = 128
COLS = 1024
LT = COLS // TILE
SLOTS = 3
SUBCYCLES = 32
NB = ROWS // 8
F32 = jnp.float32
I32 = jnp.int32


def iotas():
    lane = lax.broadcasted_iota(I32, (8, 128), 1)
    row = lax.broadcasted_iota(I32, (8, 128), 0)
    return lane, row


def recip(value):
    r = pltpu.reciprocal(value, approx=True)
    return r * (2.0 - value * r)


def face(open_depth, level, velocity):
    is_open = open_depth > level
    z = jnp.where(is_open, velocity * 0.25, 0.0)
    e = jnp.where(is_open, 0.125, 0.0)
    far = e - jnp.minimum(z, 0.0)
    return far, far + z


def ice_tiles(places, planes, con, st, rolled, res_ref, hook):
    lane, row = iotas()
    not_first, not_last = lane != 0, lane != 127
    tiles = range(len(places))
    ue_v, un_v, mass_v, str_v, mask_v, depth_v, uo_v, vo_v = planes
    zeros = jnp.zeros((8, 128), F32)

    def at(k):
        return slice(k * 8, k * 8 + 8)

    def north(value):
        return jnp.where(row == 7, 0.0, pltpu.roll(value, 7, 0))

    def south(value):
        return jnp.where(row == 0, 0.0, pltpu.roll(value, 1, 0))

    def keep_east(t, f, k, value):
        pltpu.store(rolled.at[t, f, at(k), :], pltpu.roll(value, 127, 1), mask=not_last)

    def keep_west(t, f, k, value):
        pltpu.store(rolled.at[t, f, at(k), :], pltpu.roll(value, 1, 1), mask=not_first)

    for t in tiles:
        pos = places[t]
        for b in range(NB):
            rows = slice(b * 8, b * 8 + 8)
            spread = pl.ds((b % 2) * 64 + b // 2, 8, stride=8)
            mass, strength = mass_v[pos, rows, :], str_v[pos, rows, :]
            ice = jnp.logical_and(mask_v[pos, rows, :] > 0, depth_v[pos, rows, :] > 0)
            mass = jnp.where(ice, mass, 0.0)
            strength = jnp.where(ice, strength, 0.0)
            inertia = mass * 2.0
            diag = inertia + 1.0
            turn = mass * 0.5
            inv = 1.0 / (diag * diag + turn * turn)
            con[t, 0, spread, :] = inertia
            con[t, 1, spread, :] = diag * inv
            con[t, 2, spread, :] = turn * inv
            con[t, 3, spread, :] = strength * (1.0 / 12.0)
            con[t, 4, spread, :] = uo_v[pos, 0, rows, :] * 0.5
            con[t, 5, spread, :] = vo_v[pos, 0, rows, :] * 0.5
            st[t, 0, spread, :] = ue_v[pos, rows, :] * 0.5
            st[t, 1, spread, :] = un_v[pos, rows, :] * 0.5
            st[t, 2, spread, :] = strength * 0.25
    for t in tiles:
        for k in range(NB):
            for f in range(4):
                rolled[t, f, at(k), :] = zeros
    for t in tiles:
        for k in range(NB):
            p4 = st[t, 2, at(k), :]
            p_south = st[t, 2, at(k - 1), :] if k else south(st[t, 2, at(NB - 1), :])
            p_west = jnp.where(lane == 0, 0.0, pltpu.roll(p4, 1, 1))
            con[t, 4, at(k), :] = con[t, 4, at(k), :] - (p4 - p_west)
            con[t, 5, at(k), :] = con[t, 5, at(k), :] - (p4 - p_south)
            st[t, 3, at(k), :] = p4
            st[t, 4, at(k), :] = zeros
            keep_east(t, 0, k, st[t, 0, at(k), :])
            keep_east(t, 1, k, st[t, 1, at(k), :])

    keep = 1.0 / 1.5

    def stress(t, k):
        u, v = st[t, 0, at(k), :], st[t, 1, at(k), :]
        if k < NB - 1:
            un, vn = st[t, 0, at(k + 1), :], st[t, 1, at(k + 1), :]
        else:
            un, vn = north(st[t, 0, at(0), :]), north(st[t, 1, at(0), :])
        d1 = rolled[t, 0, at(k), :] - u
        d2 = vn - v
        h = (un - u) + (rolled[t, 1, at(k), :] - v)
        div = d1 + d2
        ten = d1 - d2
        p = div + div
        r = ten * 0.5
        q = con[t, 3, at(k), :] * lax.rsqrt((p * p + ten * ten) + (h * h + 0.25))
        sx = st[t, 2, at(k), :] * keep + q * (p + r)
        sy = st[t, 3, at(k), :] * keep + q * (p - r)
        sh = st[t, 4, at(k), :] * keep + q * h
        st[t, 2, at(k), :] = sx
        st[t, 3, at(k), :] = sy
        st[t, 4, at(k), :] = sh
        keep_west(t, 2, k, sx)
        keep_west(t, 3, k, sh)

    def momentum(t, k):
        u, v, sx, sy, sh = [st[t, f, at(k), :] for f in range(5)]
        if k:
            sy_s, sh_s = st[t, 3, at(k - 1), :], st[t, 4, at(k - 1), :]
        else:
            sy_s, sh_s = south(st[t, 3, at(NB - 1), :]), south(st[t, 4, at(NB - 1), :])
        inertia, al, be, kx, ky = [con[t, f, at(k), :] for f in (0, 1, 2, 4, 5)]
        rx = (inertia * u + kx) + ((sx - rolled[t, 2, at(k), :]) + (sh - sh_s))
        ry = (inertia * v + ky) + ((sh - rolled[t, 3, at(k), :]) + (sy - sy_s))
        u = al * rx + be * ry
        v = al * ry - be * rx
        st[t, 0, at(k), :] = u
        st[t, 1, at(k), :] = v
        keep_east(t, 0, k, u)
        keep_east(t, 1, k, v)

    def cycle(_, carry):
        for t in tiles:
            for k in range(NB):
                stress(t, k)
        for t in tiles:
            for k in range(NB):
                momentum(t, k)
        return carry

    def four(i, carry):
        hook(i)
        for _ in range(4):
            cycle(i, carry)
        return carry

    lax.fori_loop(0, SUBCYCLES // 4, four, 0)
    for t in tiles:
        for k in range(NB):
            res_ref[t, 0, pl.ds(k, 8, stride=NB), :] = st[t, 0, at(k), :] * 2.0
            res_ref[t, 1, pl.ds(k, 8, stride=NB), :] = st[t, 1, at(k), :] * 2.0


def exchange_kernel(
    n_lon,
    n_lat,
    owned_hbm,
    state,
    depth,
    ivel,
    mass,
    strength,
    mask,
    vmix,
    he,
    hw,
    hs,
    hn,
    own_first,
    own_last,
    own_n,
    own_s,
    fold,
    interim,
    vmix_out,
    depth_out,
    ivel_out,
    res,
    info,
    c_v,
    u_v,
    v_v,
    d_v,
    ue_v,
    un_v,
    mass_v,
    str_v,
    mask_v,
    blk_first,
    blk_last,
    d_rim,
    c_rolled,
    d_rolled,
    h_west,
    h_north,
    part,
    pack_first,
    pack_last,
    pack_n,
    pack_s,
    pack_f,
    my_list,
    lists,
    lists_s,
    owned,
    con,
    st,
    rolled,
    in_sem,
    plane_sem,
    send_sem,
    recv_sem,
    fsend_sem,
    frecv_sem,
    local_sem,
    rim_sem,
    out_sem,
):
    x = lax.axis_index("lon")
    y = lax.axis_index("lat")
    lane, row = iotas()
    is_last, not_last = lane == 127, lane != 127
    is_first, not_first = lane == 0, lane != 0
    top = y == n_lat - 1
    bottom = y == 0
    half = lax.rem(x, 2)
    chip = lax.div(x, 2)

    def lon(step):
        return {"lon": lax.rem(x + step + n_lon, n_lon), "lat": y}

    def lat(step):
        return {"lon": x, "lat": y + step}

    get_owned = pltpu.make_async_copy(owned_hbm, owned, local_sem.at[0])
    get_owned.start()
    barrier = pltpu.get_barrier_semaphore()

    def greet(device):
        pl.semaphore_signal(barrier, inc=1, device_id=device, device_id_type=MESH)

    for step in (1, -1, 2, -2):
        greet(lon(step))

    fold_extra = range(4, n_lon - 2, 2)

    @pl.when(top)
    def _():
        for step in fold_extra:
            greet(lon(step))

    @pl.when(jnp.logical_not(top))
    def _():
        greet(lat(1))

    @pl.when(jnp.logical_not(bottom))
    def _():
        greet(lat(-1))

    def barrier_wait():
        @pl.when(jnp.logical_and(top, jnp.logical_not(bottom)))
        def _():
            pl.semaphore_wait(barrier, 5 + len(fold_extra))

        @pl.when(jnp.logical_and(bottom, jnp.logical_not(top)))
        def _():
            pl.semaphore_wait(barrier, 5)

        @pl.when(jnp.logical_not(jnp.logical_or(bottom, top)))
        def _():
            pl.semaphore_wait(barrier, 6)

    def fetch(j):
        cols = pl.ds(pl.multiple_of(j * 128, 128), 128)
        rows = pl.ds(0, ROWS)
        return [
            pltpu.make_async_copy(state.at[0:2, :, :, cols], c_v.at[j, :, :, rows, :], in_sem.at[0, j]),
            pltpu.make_async_copy(depth.at[:, cols], d_v.at[j, rows, :], in_sem.at[1, j]),
            pltpu.make_async_copy(state.at[2, :, :, cols], u_v.at[j], in_sem.at[2, j]),
            pltpu.make_async_copy(state.at[3, :, :, cols], v_v.at[j], in_sem.at[3, j]),
        ]

    rims = [
        pltpu.make_async_copy(state.at[0:2, :, pl.ds(0, 8), :], blk_first, rim_sem.at[0]),
        pltpu.make_async_copy(state.at[0:2, :, pl.ds(ROWS - 8, 8), :], blk_last.at[0:2], rim_sem.at[1]),
        pltpu.make_async_copy(state.at[3, :, pl.ds(ROWS - 8, 8), :], blk_last.at[2], rim_sem.at[2]),
        pltpu.make_async_copy(depth.at[pl.ds(0, 8), :], d_rim.at[0], rim_sem.at[3]),
        pltpu.make_async_copy(depth.at[pl.ds(ROWS - 8, 8), :], d_rim.at[1], rim_sem.at[4]),
    ]
    for c in rims:
        c.start()
    for j in range(LT):
        for c in fetch(j):
            c.start()
    planes = [(ivel.at[0], ue_v), (ivel.at[1], un_v), (mass, mass_v), (strength, str_v), (mask, mask_v)]
    for i, (src, dst) in enumerate(planes):
        for j in range(LT):
            pltpu.make_async_copy(
                src.at[:, j * 128 : j * 128 + 128], dst.at[j], plane_sem.at[i]
            ).start()

    passed = [pltpu.make_async_copy(ivel, ivel_out, out_sem.at[LT])] + [
        pltpu.make_async_copy(vmix.at[:, :, j * 128 : j * 128 + 128], vmix_out.at[j], out_sem.at[j])
        for j in range(LT)
    ]
    for c in passed:
        c.start()

    get_owned.wait()
    my_list[...] = jnp.where(
        lane == 0, owned[0, 0, 0], jnp.where(lane == 1, owned[0, 0, 1], owned[0, 0, 2])
    )

    def remote(src, dst, i, device):
        return pltpu.make_async_remote_copy(
            src_ref=src,
            dst_ref=dst,
            send_sem=send_sem.at[i],
            recv_sem=recv_sem.at[i],
            device_id=device,
            device_id_type=MESH,
        )

    list_1 = remote(my_list, lists.at[0], 0, lon(-1))
    list_2 = remote(my_list, lists.at[1], 1, lon(-2))
    to_smem = pltpu.make_async_copy(lists, lists_s, local_sem.at[2])
    to_west = remote(pack_first, he, 2, lon(-1))
    to_east = remote(pack_last, hw, 3, lon(1))
    to_south = remote(pack_n, hn, 4, lat(-1))
    to_north = remote(pack_s, hs, 5, lat(1))

    zeros = jnp.zeros((8, 128), F32)
    beyond = slice(ROWS, ROWS + 8)
    for j in range(LT):
        d_v[j, beyond, :] = jnp.zeros((8, 128), I32)
        for n in range(8):
            c_v[j, n // LEV, n % LEV, beyond, :] = zeros
    for n in range(8):
        h_north[n, 0:8, :] = zeros
        for b in range(NB):
            h_west[0, n, b * 8 : b * 8 + 8, :] = zeros
    for c in rims:
        c.wait()
    for j in range(LT):
        cols = slice(j * 128, j * 128 + 128)
        d_n = d_rim[0, :, cols].astype(F32)[0:1, :]
        d_s = d_rim[1, :, cols].astype(F32)[7:8, :]
        for n in range(8):
            t, k = n // LEV, n % LEV
            pack_n[n : n + 1, cols] = blk_first[t, k, 0:1, cols]
            pack_s[n : n + 1, cols] = blk_last[t, k, 7:8, cols]
            pack_s[8 + n : 9 + n, cols] = blk_last[2, k, 7:8, cols]
        pack_n[8:16, cols] = zeros
        pack_n[16:24, cols] = jnp.broadcast_to(d_n, (8, 128))
        pack_s[16:24, cols] = jnp.broadcast_to(d_s, (8, 128))
        pack_f[j] = pack_s[0:8, cols]
        pack_f[LT, j : j + 1, :] = d_s

    steps = range(1, n_lon // 2)

    def fold_copy(step):
        return pltpu.make_async_remote_copy(
            src_ref=pack_f,
            dst_ref=fold.at[half, chip],
            send_sem=fsend_sem.at[step],
            recv_sem=frecv_sem.at[chip],
            device_id=lon(2 * step),
            device_id_type=MESH,
        )

    def fold_arrival(step):
        source = lax.rem(chip - step + n_lon // 2, n_lon // 2)
        return pltpu.make_async_remote_copy(
            src_ref=pack_f,
            dst_ref=fold.at[half, source],
            send_sem=fsend_sem.at[step],
            recv_sem=frecv_sem.at[source],
            device_id=lon(2 * step),
            device_id_type=MESH,
        )

    def fold_sibling(which):
        return pltpu.make_async_remote_copy(
            src_ref=fold.at[which],
            dst_ref=fold.at[which],
            send_sem=fsend_sem.at[0],
            recv_sem=frecv_sem.at[n_lon // 2],
            device_id=lon(1 - 2 * half),
            device_id_type=MESH,
        )

    own_fold = pltpu.make_async_copy(pack_f, fold.at[half, chip], local_sem.at[1])

    for c in fetch(0):
        c.wait()
    for b in range(NB):
        rows = slice(b * 8, b * 8 + 8)
        pltpu.store(
            d_rolled.at[0, rows, :], pltpu.roll(d_v[0, rows, :].astype(F32), 127, 1), mask=not_last
        )
        for n in range(8):
            value = pltpu.roll(c_v[0, n // LEV, n % LEV, rows, :], 127, 1)
            pltpu.store(c_rolled.at[0, n, rows, :], value, mask=not_last)

    def column(j, carry):
        @pl.when(j < LT - 1)
        def _():
            for c in fetch(j + 1):
                c.wait()

        @pl.when(j == 4)
        def _():
            barrier_wait()
            list_1.start()
            list_2.start()

            @pl.when(jnp.logical_not(bottom))
            def _():
                to_south.start()

            @pl.when(jnp.logical_not(top))
            def _():
                to_north.start()

            @pl.when(top)
            def _():
                own_fold.start()
                for step in steps:
                    fold_copy(step).start()

        @pl.when(j == LT - 1)
        def _():
            list_1.wait_recv()
            list_2.wait_recv()
            to_smem.start()

        cur = lax.rem(j, 2)
        nxt = 1 - cur
        after = jnp.minimum(j + 1, LT - 1)
        inside = jnp.where(j < LT - 1, 1.0, 0.0)

        def roll_next(b):
            rows = slice(b * 8, b * 8 + 8)
            value = pltpu.roll(d_v[after, rows, :].astype(F32) * inside, 127, 1)
            pltpu.store(d_rolled.at[cur, rows, :], value, mask=is_last)
            pltpu.store(d_rolled.at[nxt, rows, :], value, mask=not_last)
            for n in range(8):
                value = pltpu.roll(c_v[after, n // LEV, n % LEV, rows, :], 127, 1)
                pltpu.store(c_rolled.at[cur, n, rows, :], value, mask=is_last)
                pltpu.store(c_rolled.at[nxt, n, rows, :], value, mask=not_last)

        def fluxes(b):
            rows = slice(b * 8, b * 8 + 8)
            ahead = slice(b * 8 + 1, b * 8 + 9)
            store = slice(b * 8 + 8, b * 8 + 16)
            behind = slice(b * 8 + 7, b * 8 + 15)
            own = d_v[j, rows, :].astype(F32)
            open_e = jnp.minimum(own, d_rolled[cur, rows, :])
            open_n = jnp.minimum(own, d_v[j, ahead, :].astype(F32))
            for k in range(LEV):
                e_far, e_near = face(open_e, k, u_v[j, k, rows, :])
                n_far, n_near = face(open_n, k, v_v[j, k, rows, :])
                for t in range(2):
                    n = t * LEV + k
                    c = c_v[j, t, k, rows, :]
                    east = c_rolled[cur, n, rows, :] * e_far - c * e_near
                    east_rolled = pltpu.roll(east, 1, 1)
                    pltpu.store(h_west.at[cur, n, rows, :], east_rolled, mask=not_first)
                    pltpu.store(h_west.at[nxt, n, rows, :], east_rolled, mask=is_first)
                    north = c_v[j, t, k, ahead, :] * n_far - c * n_near
                    h_north[n, store, :] = north
                    part[n, rows, :] = (c + east) + (north - h_north[n, behind, :])

        def finish(b):
            rows = slice(b * 8, b * 8 + 8)
            for n in range(8):
                interim[j, n, rows, :] = part[n, rows, :] - h_west[cur, n, rows, :]

        for b in range(NB + 6):
            if b < NB:
                roll_next(b)
            if 0 <= b - 3 < NB:
                fluxes(b - 3)
            if 0 <= b - 6 < NB:
                finish(b - 6)
        return carry

    lax.fori_loop(0, LT, column, 0)

    for b in range(NB):
        rows = slice(b * 8, b * 8 + 8)
        d_first = jnp.broadcast_to(d_v[0, rows, :].astype(F32)[:, 0:1], (8, 128))
        d_last = jnp.broadcast_to(d_v[LT - 1, rows, :].astype(F32)[:, 127:128], (8, 128))
        first, last = d_first, d_last
        for n in range(8):
            t, k = n // LEV, n % LEV
            value = c_v[0, t, k, rows, :]
            first = jnp.where(lane == n, value if n == 0 else pltpu.roll(value, n, 1), first)
            last = jnp.where(lane == n, pltpu.roll(c_v[LT - 1, t, k, rows, :], n + 1, 1), last)
        for k in range(LEV):
            value = pltpu.roll(u_v[LT - 1, k, rows, :], 9 + k, 1)
            last = jnp.where(lane == 8 + k, value, last)
        last = jnp.where(jnp.logical_and(lane >= 12, lane < 16), pltpu.roll(last, 4, 1), last)
        pack_first[rows, :] = first
        pack_last[rows, :] = last
    to_west.start()
    to_east.start()

    own_packs = [
        pltpu.make_async_copy(src, dst, local_sem.at[3 + i])
        for i, (src, dst) in enumerate(
            ((pack_first, own_first), (pack_last, own_last), (pack_n, own_n), (pack_s, own_s))
        )
    ]
    give_depth = pltpu.make_async_copy(d_v.at[:, pl.ds(0, ROWS), :], depth_out, out_sem.at[LT + 1])
    give_depth.start()
    for c in own_packs:
        c.start()
    for i, (_, dst) in enumerate(planes):
        pltpu.make_async_copy(dst, dst, plane_sem.at[i]).wait()
    to_smem.wait()
    places = []
    for slot, column_id in enumerate((owned[0, 0, 0], lists_s[0, 0, 1], lists_s[1, 0, 2])):
        info[slot] = jnp.where(column_id >= 0, column_id - x * LT, -1)
        places.append(jnp.clip(column_id - x * LT, 0, LT - 1))

    def hook(i):
        @pl.when(jnp.logical_and(top, i == 4))
        def _():
            own_fold.wait()
            for step in steps:
                fold_arrival(step).wait_recv()
            fold_sibling(half).start()

    ice_tiles(
        places, (ue_v, un_v, mass_v, str_v, mask_v, d_v, u_v, v_v), con, st, rolled, res, hook
    )

    list_1.wait_send()
    list_2.wait_send()
    to_west.wait()
    to_east.wait()
    give_depth.wait()
    for c in own_packs + passed:
        c.wait()
    @pl.when(jnp.logical_not(bottom))
    def _():
        to_south.wait_send()
        to_north.wait_recv()

    @pl.when(jnp.logical_not(top))
    def _():
        to_north.wait_send()
        to_south.wait_recv()

    @pl.when(top)
    def _():
        for step in steps:
            fold_copy(step).wait_send()
        fold_sibling(half).wait_send()
        fold_sibling(1 - half).wait_recv()


def exchange_and_ice(n_lon, n_lat, *operands):
    anywhere = pl.BlockSpec(memory_space=pl.ANY)
    inside = pl.BlockSpec(memory_space=pltpu.VMEM)
    plane = pltpu.VMEM((LT, ROWS, 128), F32)
    column = jax.ShapeDtypeStruct((ROWS, 128), F32)
    rows = jax.ShapeDtypeStruct((24, COLS), F32)

    def body(*refs):
        exchange_kernel(n_lon, n_lat, *refs)

    return pl.pallas_call(
        body,
        name="exchange_and_ice",
        out_shape=(
            column,
            column,
            rows,
            rows,
            column,
            column,
            rows,
            rows,
            jax.ShapeDtypeStruct((2, n_lon // 2, LT + 1, 8, 128), F32),
            jax.ShapeDtypeStruct((LT, 8, ROWS, 128), F32),
            jax.ShapeDtypeStruct((LT, LEV, ROWS, 128), F32),
            jax.ShapeDtypeStruct((LT, ROWS, 128), I32),
            jax.ShapeDtypeStruct((2, ROWS, COLS), F32),
            jax.ShapeDtypeStruct((SLOTS, 2, TILE, TILE), F32),
            jax.ShapeDtypeStruct((SLOTS,), I32),
        ),
        in_specs=[pl.BlockSpec(memory_space=pltpu.HBM)] * 8,
        out_specs=(anywhere,) * 9
        + (inside,)
        + (anywhere,) * 3
        + (inside, pl.BlockSpec(memory_space=pltpu.SMEM)),
        scratch_shapes=[
            pltpu.VMEM((LT, 2, LEV, ROWS + 8, 128), F32),
            pltpu.VMEM((LT, LEV, ROWS, 128), F32),
            pltpu.VMEM((LT, LEV, ROWS, 128), F32),
            pltpu.VMEM((LT, ROWS + 8, 128), I32),
            plane,
            plane,
            plane,
            plane,
            pltpu.VMEM((LT, ROWS, 128), I32),
            pltpu.VMEM((2, LEV, 8, COLS), F32),
            pltpu.VMEM((3, LEV, 8, COLS), F32),
            pltpu.VMEM((2, 8, COLS), I32),
            pltpu.VMEM((2, 8, ROWS, 128), F32),
            pltpu.VMEM((2, ROWS, 128), F32),
            pltpu.VMEM((2, 8, ROWS, 128), F32),
            pltpu.VMEM((8, ROWS + 8, 128), F32),
            pltpu.VMEM((8, ROWS, 128), F32),
            pltpu.VMEM((ROWS, 128), F32),
            pltpu.VMEM((ROWS, 128), F32),
            pltpu.VMEM((24, COLS), F32),
            pltpu.VMEM((24, COLS), F32),
            pltpu.VMEM((LT + 1, 8, 128), F32),
            pltpu.VMEM((8, 128), I32),
            pltpu.VMEM((2, 8, 128), I32),
            pltpu.SMEM((2, 8, 128), I32),
            pltpu.SMEM((1, 1, SLOTS), I32),
            pltpu.VMEM((SLOTS, 6, TILE, TILE), F32),
            pltpu.VMEM((SLOTS, 5, TILE, TILE), F32),
            pltpu.VMEM((SLOTS, 4, TILE, TILE), F32),
            pltpu.SemaphoreType.DMA((4, LT)),
            pltpu.SemaphoreType.DMA((5,)),
            pltpu.SemaphoreType.DMA((6,)),
            pltpu.SemaphoreType.DMA((6,)),
            pltpu.SemaphoreType.DMA((n_lon // 2,)),
            pltpu.SemaphoreType.DMA((n_lon // 2 + 1,)),
            pltpu.SemaphoreType.DMA((7,)),
            pltpu.SemaphoreType.DMA((5,)),
            pltpu.SemaphoreType.DMA((LT + 2,)),
        ],
        compiler_params=pltpu.CompilerParams(
            collective_id=0, has_side_effects=True, vmem_limit_bytes=22 * 2**20
        ),
    )(*operands)


def ocean_kernel(
    n_lon,
    n_lat,
    partner,
    info,
    p_v,
    vm_v,
    d_v,
    ivel,
    he,
    hw,
    hs,
    hn,
    own_first,
    own_last,
    own_n,
    own_s,
    fold,
    res,
    out,
    out_ice,
    o_v,
    hs_v,
    hn_v,
    win,
    west_h,
    east_h,
    south_h,
    north_h,
    out_sem,
    sem,
):
    y = lax.axis_index("lat")
    top = y == n_lat - 1
    bottom = y == 0
    lane, row = iotas()
    lane16 = lax.broadcasted_iota(I32, (16, 128), 1)

    put_ice = pltpu.make_async_copy(ivel, out_ice, sem.at[0])

    def put(j):
        cols = slice(j * 128, j * 128 + 128)
        return pltpu.make_async_copy(o_v.at[j], out.at[:, :, :, cols], out_sem.at[j])

    def patch(slot):
        at = pl.multiple_of(jnp.clip(info[slot], 0, LT - 1) * 128, 128)
        return pltpu.make_async_copy(res.at[slot], out_ice.at[:, :, pl.ds(at, 128)], sem.at[1 + slot])

    put_ice.start()
    hn_v[...] = hn[...]
    hs_v[...] = hs[...]

    @pl.when(top)
    def _():
        base = partner[COLS - 1]
        tile0 = lax.div(base, 128)
        shift = lax.rem(base, 128)
        for m in range(LT + 1):
            t = lax.rem(tile0 + m, n_lon * LT)
            dev = lax.div(t, LT)
            j = lax.rem(t, LT)
            half, chip = lax.rem(dev, 2), lax.div(dev, 2)
            win[m, 0:8, :] = fold[half, chip, j]
            win[m, 8:9, :] = fold[half, chip, LT, pl.ds(j, 1), :]
        back = lax.rem(128 - shift, 128)
        values = []
        for m in range(LT):
            near = pltpu.roll(win[m], back, 1)
            far = pltpu.roll(win[m + 1], back, 1)
            values.append(jnp.where(lane16 < 128 - shift, near, far))
        for bit in (1, 2, 4, 8, 16, 32, 64):
            odd = (lane16 & bit) != 0
            values = [
                jnp.where(odd, pltpu.roll(value, bit, 1), pltpu.roll(value, 128 - bit, 1))
                for value in values
            ]
        for m in range(LT):
            at = (LT - 1 - m) * 128
            hn_v[0:8, at : at + 128] = values[m][0:8, :]
            hn_v[16:24, at : at + 128] = jnp.broadcast_to(values[m][8:9, :], (8, 128))

    @pl.when(bottom)
    def _():
        hs_v[...] = jnp.zeros((24, COLS), F32)

    level = (lane & 3).astype(F32)
    for b in range(NB):
        rows = slice(b * 8, b * 8 + 8)
        pack, own = hw[rows, :], own_first[rows, :]
        both = jnp.minimum(pltpu.roll(pack, 112, 1), pltpu.roll(own, 112, 1))
        far, near = face(both, level, pltpu.roll(pack, 120, 1))
        west_h[rows, :] = pack * near - own * far
        pack, own = he[rows, :], own_last[rows, :]
        both = jnp.minimum(pltpu.roll(pack, 112, 1), pltpu.roll(own, 112, 1))
        far, near = face(both, level, pltpu.roll(own, 120, 1))
        east_h[rows, :] = pack * far - own * near
    level = (row & 3).astype(F32)
    for j in range(LT):
        cols = slice(j * 128, j * 128 + 128)
        far, near = face(jnp.minimum(own_s[16:24, cols], hn_v[16:24, cols]), level, own_s[8:16, cols])
        north_h[:, cols] = hn_v[0:8, cols] * far - own_s[0:8, cols] * near
        far, near = face(jnp.minimum(own_n[16:24, cols], hs_v[16:24, cols]), level, hs_v[8:16, cols])
        south_h[:, cols] = hs_v[0:8, cols] * near - own_n[0:8, cols] * far

    def rhs(j, n, b):
        rows = slice(b * 8, b * 8 + 8)
        value = p_v[j, n, rows, :]
        if j == 0:
            west = west_h[rows, :] if n == 0 else pltpu.roll(west_h[rows, :], 128 - n, 1)
            value = value + jnp.where(lane == 0, west, 0.0)
        if j == LT - 1:
            value = value + jnp.where(lane == 127, pltpu.roll(east_h[rows, :], 127 - n, 1), 0.0)
        cols = slice(j * 128, j * 128 + 128)
        if b == 0:
            rim = jnp.broadcast_to(south_h[n : n + 1, cols], (8, 128))
            value = value + jnp.where(row == 0, rim, 0.0)
        if b == NB - 1:
            rim = jnp.broadcast_to(north_h[n : n + 1, cols], (8, 128))
            value = value + jnp.where(row == 7, rim, 0.0)
        return value

    for j in range(LT):
        if j == 2:
            put_ice.wait()
            for slot in range(SLOTS):

                @pl.when(info[slot] >= 0)
                def _(slot=slot):
                    patch(slot).start()

        for b in range(NB):
            rows = slice(b * 8, b * 8 + 8)
            own = d_v[j, rows, :]
            g = [jnp.where(own > k, vm_v[j, k, rows, :] * 0.25, 0.0) for k in range(LEV)]
            i0 = recip((1.0 + g[0]) + g[1])
            u0 = g[1] * i0
            i1 = recip((1.0 + g[1]) + g[2] - g[1] * u0)
            u1 = g[2] * i1
            i2 = recip((1.0 + g[2]) + g[3] - g[2] * u1)
            u2 = g[3] * i2
            i3 = recip((1.0 + g[3]) - g[3] * u2)
            for t in range(2):
                f = [rhs(j, t * LEV + k, b) for k in range(LEV)]
                r0 = f[0] * i0
                r1 = (f[1] + g[1] * r0) * i1
                r2 = (f[2] + g[2] * r1) * i2
                x3 = (f[3] + g[3] * r2) * i3
                x2 = r2 + u2 * x3
                x1 = r1 + u1 * x2
                x0 = r0 + u0 * x1
                for k, value in enumerate((x0, x1, x2, x3)):
                    o_v[j, t, k, rows, :] = value
        put(j).start()

    for j in range(LT):
        put(j).wait()
    for slot in range(SLOTS):

        @pl.when(info[slot] >= 0)
        def _(slot=slot):
            patch(slot).wait()


def ocean(n_lon, n_lat, *operands):
    anywhere = pl.BlockSpec(memory_space=pl.ANY)
    smem = pl.BlockSpec(memory_space=pltpu.SMEM)
    inside = pl.BlockSpec(memory_space=pltpu.VMEM)
    column = pltpu.VMEM((ROWS, 128), F32)
    rows = pltpu.VMEM((24, COLS), F32)

    def body(*refs):
        ocean_kernel(n_lon, n_lat, *refs)

    return pl.pallas_call(
        body,
        name="ocean",
        out_shape=(
            jax.ShapeDtypeStruct((2, LEV, ROWS, COLS), F32),
            jax.ShapeDtypeStruct((2, ROWS, COLS), F32),
        ),
        in_specs=[smem, smem] + [inside] * (len(operands) - 2),
        out_specs=(anywhere, anywhere),
        scratch_shapes=[
            pltpu.VMEM((LT, 2, LEV, ROWS, 128), F32),
            rows,
            rows,
            pltpu.VMEM((LT + 1, 16, 128), F32),
            column,
            column,
            pltpu.VMEM((8, COLS), F32),
            pltpu.VMEM((8, COLS), F32),
            pltpu.SemaphoreType.DMA((LT,)),
            pltpu.SemaphoreType.DMA((1 + SLOTS,)),
        ],
        compiler_params=pltpu.CompilerParams(vmem_limit_bytes=10 * 2**20),
    )(*operands)


def on_device(state, depth, vmix, partner, ivel, mass, strength, mask, owned):
    n_lon, n_lat = lax.axis_size("lon"), lax.axis_size("lat")
    in_hbm = [
        pltpu.with_memory_space_constraint(value, pltpu.HBM)
        for value in (owned, state, depth, ivel, mass, strength, mask, vmix)
    ]
    *rims, interim, vmix_in, depth_in, ivel_in, res, info = exchange_and_ice(n_lon, n_lat, *in_hbm)
    return ocean(n_lon, n_lat, partner, info, interim, vmix_in, depth_in, ivel_in, *rims, res)


def solution(mesh):
    return jax.shard_map(
        on_device,
        mesh=mesh,
        in_specs=(
            P(None, None, "lat", "lon"),
            P("lat", "lon"),
            P(None, "lat", "lon"),
            P("lon"),
            P(None, "lat", "lon"),
            P("lat", "lon"),
            P("lat", "lon"),
            P("lat", "lon"),
            P("lat", "lon", None),
        ),
        out_specs=(P(None, None, "lat", "lon"), P(None, "lat", "lon")),
        check_vma=False,
    )
```

```python
import jax
import jax.numpy as jnp
from jax import lax
from jax.experimental import pallas as pl
from jax.experimental.pallas import tpu as pltpu
from jax.sharding import PartitionSpec as P

MESH = pl.DeviceIdType.MESH
LEV = 4
TILE = 128
ROWS = 128
COLS = 1024
LT = COLS // TILE
SLOTS = 3
SUBCYCLES = 32
NB = ROWS // 8
F32 = jnp.float32
I32 = jnp.int32


def iotas():
    lane = lax.broadcasted_iota(I32, (8, 128), 1)
    row = lax.broadcasted_iota(I32, (8, 128), 0)
    return lane, row


def recip(value):
    r = pltpu.reciprocal(value, approx=True)
    return r * (2.0 - value * r)


def face(open_depth, level, velocity):
    is_open = open_depth > level
    z = jnp.where(is_open, velocity * 0.25, 0.0)
    e = jnp.where(is_open, 0.125, 0.0)
    far = e - jnp.minimum(z, 0.0)
    return far, far + z


def ice_tiles(places, planes, con, st, rolled, res_ref, hook):
    lane, row = iotas()
    not_first, not_last = lane != 0, lane != 127
    tiles = range(len(places))
    ue_v, un_v, mass_v, str_v, mask_v, depth_v, uo_v, vo_v = planes
    zeros = jnp.zeros((8, 128), F32)

    def at(k):
        return slice(k * 8, k * 8 + 8)

    def north(value):
        return jnp.where(row == 7, 0.0, pltpu.roll(value, 7, 0))

    def south(value):
        return jnp.where(row == 0, 0.0, pltpu.roll(value, 1, 0))

    def keep_east(t, f, k, value):
        pltpu.store(rolled.at[t, f, at(k), :], pltpu.roll(value, 127, 1), mask=not_last)

    def keep_west(t, f, k, value):
        pltpu.store(rolled.at[t, f, at(k), :], pltpu.roll(value, 1, 1), mask=not_first)

    for t in tiles:
        pos = places[t]
        for b in range(NB):
            rows = slice(b * 8, b * 8 + 8)
            spread = pl.ds((b % 2) * 64 + b // 2, 8, stride=8)
            mass, strength = mass_v[pos, rows, :], str_v[pos, rows, :]
            ice = jnp.logical_and(mask_v[pos, rows, :] > 0, depth_v[pos, rows, :] > 0)
            mass = jnp.where(ice, mass, 0.0)
            strength = jnp.where(ice, strength, 0.0)
            inertia = mass * 2.0
            diag = inertia + 1.0
            turn = mass * 0.5
            inv = 1.0 / (diag * diag + turn * turn)
            con[t, 0, spread, :] = inertia
            con[t, 1, spread, :] = diag * inv
            con[t, 2, spread, :] = turn * inv
            con[t, 3, spread, :] = strength * (1.0 / 12.0)
            con[t, 4, spread, :] = uo_v[pos, 0, rows, :] * 0.5
            con[t, 5, spread, :] = vo_v[pos, 0, rows, :] * 0.5
            st[t, 0, spread, :] = ue_v[pos, rows, :] * 0.5
            st[t, 1, spread, :] = un_v[pos, rows, :] * 0.5
            st[t, 2, spread, :] = strength * 0.25
    for t in tiles:
        for k in range(NB):
            for f in range(4):
                rolled[t, f, at(k), :] = zeros
    for t in tiles:
        for k in range(NB):
            p4 = st[t, 2, at(k), :]
            p_south = st[t, 2, at(k - 1), :] if k else south(st[t, 2, at(NB - 1), :])
            p_west = jnp.where(lane == 0, 0.0, pltpu.roll(p4, 1, 1))
            con[t, 4, at(k), :] = con[t, 4, at(k), :] - (p4 - p_west)
            con[t, 5, at(k), :] = con[t, 5, at(k), :] - (p4 - p_south)
            st[t, 3, at(k), :] = p4
            st[t, 4, at(k), :] = zeros
            keep_east(t, 0, k, st[t, 0, at(k), :])
            keep_east(t, 1, k, st[t, 1, at(k), :])

    keep = 1.0 / 1.5

    def stress(t, k):
        u, v = st[t, 0, at(k), :], st[t, 1, at(k), :]
        if k < NB - 1:
            un, vn = st[t, 0, at(k + 1), :], st[t, 1, at(k + 1), :]
        else:
            un, vn = north(st[t, 0, at(0), :]), north(st[t, 1, at(0), :])
        d1 = rolled[t, 0, at(k), :] - u
        d2 = vn - v
        h = (un - u) + (rolled[t, 1, at(k), :] - v)
        div = d1 + d2
        ten = d1 - d2
        p = div + div
        r = ten * 0.5
        q = con[t, 3, at(k), :] * lax.rsqrt((p * p + ten * ten) + (h * h + 0.25))
        sx = st[t, 2, at(k), :] * keep + q * (p + r)
        sy = st[t, 3, at(k), :] * keep + q * (p - r)
        sh = st[t, 4, at(k), :] * keep + q * h
        st[t, 2, at(k), :] = sx
        st[t, 3, at(k), :] = sy
        st[t, 4, at(k), :] = sh
        keep_west(t, 2, k, sx)
        keep_west(t, 3, k, sh)

    def momentum(t, k):
        u, v, sx, sy, sh = [st[t, f, at(k), :] for f in range(5)]
        if k:
            sy_s, sh_s = st[t, 3, at(k - 1), :], st[t, 4, at(k - 1), :]
        else:
            sy_s, sh_s = south(st[t, 3, at(NB - 1), :]), south(st[t, 4, at(NB - 1), :])
        inertia, al, be, kx, ky = [con[t, f, at(k), :] for f in (0, 1, 2, 4, 5)]
        rx = (inertia * u + kx) + ((sx - rolled[t, 2, at(k), :]) + (sh - sh_s))
        ry = (inertia * v + ky) + ((sh - rolled[t, 3, at(k), :]) + (sy - sy_s))
        u = al * rx + be * ry
        v = al * ry - be * rx
        st[t, 0, at(k), :] = u
        st[t, 1, at(k), :] = v
        keep_east(t, 0, k, u)
        keep_east(t, 1, k, v)

    def cycle(_, carry):
        for t in tiles:
            for k in range(NB):
                stress(t, k)
        for t in tiles:
            for k in range(NB):
                momentum(t, k)
        return carry

    def four(i, carry):
        hook(i)
        for _ in range(4):
            cycle(i, carry)
        return carry

    lax.fori_loop(0, SUBCYCLES // 4, four, 0)
    for t in tiles:
        for k in range(NB):
            res_ref[t, 0, pl.ds(k, 8, stride=NB), :] = st[t, 0, at(k), :] * 2.0
            res_ref[t, 1, pl.ds(k, 8, stride=NB), :] = st[t, 1, at(k), :] * 2.0


def exchange_kernel(
    n_lon,
    n_lat,
    owned_hbm,
    state,
    depth,
    ivel,
    mass,
    strength,
    mask,
    vmix,
    he,
    hw,
    hs,
    hn,
    own_first,
    own_last,
    own_n,
    own_s,
    fold,
    interim,
    vmix_out,
    depth_out,
    ivel_out,
    res,
    info,
    c_v,
    u_v,
    v_v,
    d_v,
    ue_v,
    un_v,
    mass_v,
    str_v,
    mask_v,
    blk_first,
    blk_last,
    d_rim,
    c_rolled,
    d_rolled,
    h_west,
    h_north,
    part,
    pack_first,
    pack_last,
    pack_n,
    pack_s,
    pack_f,
    my_list,
    lists,
    lists_s,
    owned,
    con,
    st,
    rolled,
    in_sem,
    plane_sem,
    send_sem,
    recv_sem,
    fsend_sem,
    frecv_sem,
    local_sem,
    rim_sem,
    out_sem,
):
    x = lax.axis_index("lon")
    y = lax.axis_index("lat")
    lane, row = iotas()
    is_last, not_last = lane == 127, lane != 127
    is_first, not_first = lane == 0, lane != 0
    top = y == n_lat - 1
    bottom = y == 0
    half = lax.rem(x, 2)
    chip = lax.div(x, 2)

    def lon(step):
        return {"lon": lax.rem(x + step + n_lon, n_lon), "lat": y}

    def lat(step):
        return {"lon": x, "lat": y + step}

    get_owned = pltpu.make_async_copy(owned_hbm, owned, local_sem.at[0])
    get_owned.start()
    barrier = pltpu.get_barrier_semaphore()

    def greet(device):
        pl.semaphore_signal(barrier, inc=1, device_id=device, device_id_type=MESH)

    for step in (1, -1, 2, -2):
        greet(lon(step))

    fold_extra = range(4, n_lon - 2, 2)

    @pl.when(top)
    def _():
        for step in fold_extra:
            greet(lon(step))

    @pl.when(jnp.logical_not(top))
    def _():
        greet(lat(1))

    @pl.when(jnp.logical_not(bottom))
    def _():
        greet(lat(-1))

    def barrier_wait():
        @pl.when(jnp.logical_and(top, jnp.logical_not(bottom)))
        def _():
            pl.semaphore_wait(barrier, 5 + len(fold_extra))

        @pl.when(jnp.logical_and(bottom, jnp.logical_not(top)))
        def _():
            pl.semaphore_wait(barrier, 5)

        @pl.when(jnp.logical_not(jnp.logical_or(bottom, top)))
        def _():
            pl.semaphore_wait(barrier, 6)

    def fetch(j):
        cols = pl.ds(pl.multiple_of(j * 128, 128), 128)
        rows = pl.ds(0, ROWS)
        return [
            pltpu.make_async_copy(state.at[0:2, :, :, cols], c_v.at[j, :, :, rows, :], in_sem.at[0, j]),
            pltpu.make_async_copy(depth.at[:, cols], d_v.at[j, rows, :], in_sem.at[1, j]),
            pltpu.make_async_copy(state.at[2, :, :, cols], u_v.at[j], in_sem.at[2, j]),
            pltpu.make_async_copy(state.at[3, :, :, cols], v_v.at[j], in_sem.at[3, j]),
        ]

    rims = [
        pltpu.make_async_copy(state.at[0:2, :, pl.ds(0, 8), :], blk_first, rim_sem.at[0]),
        pltpu.make_async_copy(state.at[0:2, :, pl.ds(ROWS - 8, 8), :], blk_last.at[0:2], rim_sem.at[1]),
        pltpu.make_async_copy(state.at[3, :, pl.ds(ROWS - 8, 8), :], blk_last.at[2], rim_sem.at[2]),
        pltpu.make_async_copy(depth.at[pl.ds(0, 8), :], d_rim.at[0], rim_sem.at[3]),
        pltpu.make_async_copy(depth.at[pl.ds(ROWS - 8, 8), :], d_rim.at[1], rim_sem.at[4]),
    ]
    for c in rims:
        c.start()
    for j in range(LT):
        for c in fetch(j):
            c.start()
    planes = [(ivel.at[0], ue_v), (ivel.at[1], un_v), (mass, mass_v), (strength, str_v), (mask, mask_v)]
    for i, (src, dst) in enumerate(planes):
        for j in range(LT):
            pltpu.make_async_copy(
                src.at[:, j * 128 : j * 128 + 128], dst.at[j], plane_sem.at[i]
            ).start()

    passed = [pltpu.make_async_copy(ivel, ivel_out, out_sem.at[LT])] + [
        pltpu.make_async_copy(vmix.at[:, :, j * 128 : j * 128 + 128], vmix_out.at[j], out_sem.at[j])
        for j in range(LT)
    ]
    for c in passed:
        c.start()

    get_owned.wait()
    my_list[...] = jnp.where(
        lane == 0, owned[0, 0, 0], jnp.where(lane == 1, owned[0, 0, 1], owned[0, 0, 2])
    )

    def remote(src, dst, i, device):
        return pltpu.make_async_remote_copy(
            src_ref=src,
            dst_ref=dst,
            send_sem=send_sem.at[i],
            recv_sem=recv_sem.at[i],
            device_id=device,
            device_id_type=MESH,
        )

    list_1 = remote(my_list, lists.at[0], 0, lon(-1))
    list_2 = remote(my_list, lists.at[1], 1, lon(-2))
    to_smem = pltpu.make_async_copy(lists, lists_s, local_sem.at[2])
    to_west = remote(pack_first, he, 2, lon(-1))
    to_east = remote(pack_last, hw, 3, lon(1))
    to_south = remote(pack_n, hn, 4, lat(-1))
    to_north = remote(pack_s, hs, 5, lat(1))

    zeros = jnp.zeros((8, 128), F32)
    beyond = slice(ROWS, ROWS + 8)
    for j in range(LT):
        d_v[j, beyond, :] = jnp.zeros((8, 128), I32)
        for n in range(8):
            c_v[j, n // LEV, n % LEV, beyond, :] = zeros
    for n in range(8):
        h_north[n, 0:8, :] = zeros
        for b in range(NB):
            h_west[0, n, b * 8 : b * 8 + 8, :] = zeros
    for c in rims:
        c.wait()
    for j in range(LT):
        cols = slice(j * 128, j * 128 + 128)
        d_n = d_rim[0, :, cols].astype(F32)[0:1, :]
        d_s = d_rim[1, :, cols].astype(F32)[7:8, :]
        for n in range(8):
            t, k = n // LEV, n % LEV
            pack_n[n : n + 1, cols] = blk_first[t, k, 0:1, cols]
            pack_s[n : n + 1, cols] = blk_last[t, k, 7:8, cols]
            pack_s[8 + n : 9 + n, cols] = blk_last[2, k, 7:8, cols]
        pack_n[8:16, cols] = zeros
        pack_n[16:24, cols] = jnp.broadcast_to(d_n, (8, 128))
        pack_s[16:24, cols] = jnp.broadcast_to(d_s, (8, 128))
        pack_f[j] = pack_s[0:8, cols]
        pack_f[LT, j : j + 1, :] = d_s

    steps = range(1, n_lon // 2)

    def fold_copy(step):
        return pltpu.make_async_remote_copy(
            src_ref=pack_f,
            dst_ref=fold.at[half, chip],
            send_sem=fsend_sem.at[step],
            recv_sem=frecv_sem.at[chip],
            device_id=lon(2 * step),
            device_id_type=MESH,
        )

    def fold_arrival(step):
        source = lax.rem(chip - step + n_lon // 2, n_lon // 2)
        return pltpu.make_async_remote_copy(
            src_ref=pack_f,
            dst_ref=fold.at[half, source],
            send_sem=fsend_sem.at[step],
            recv_sem=frecv_sem.at[source],
            device_id=lon(2 * step),
            device_id_type=MESH,
        )

    def fold_sibling(which):
        return pltpu.make_async_remote_copy(
            src_ref=fold.at[which],
            dst_ref=fold.at[which],
            send_sem=fsend_sem.at[0],
            recv_sem=frecv_sem.at[n_lon // 2],
            device_id=lon(1 - 2 * half),
            device_id_type=MESH,
        )

    own_fold = pltpu.make_async_copy(pack_f, fold.at[half, chip], local_sem.at[1])

    for c in fetch(0):
        c.wait()
    for b in range(NB):
        rows = slice(b * 8, b * 8 + 8)
        pltpu.store(
            d_rolled.at[0, rows, :], pltpu.roll(d_v[0, rows, :].astype(F32), 127, 1), mask=not_last
        )
        for n in range(8):
            value = pltpu.roll(c_v[0, n // LEV, n % LEV, rows, :], 127, 1)
            pltpu.store(c_rolled.at[0, n, rows, :], value, mask=not_last)

    def column(j, carry):
        @pl.when(j < LT - 1)
        def _():
            for c in fetch(j + 1):
                c.wait()

        @pl.when(j == 2)
        def _():
            barrier_wait()
            list_1.start()
            list_2.start()

            @pl.when(jnp.logical_not(bottom))
            def _():
                to_south.start()

            @pl.when(jnp.logical_not(top))
            def _():
                to_north.start()

            @pl.when(top)
            def _():
                own_fold.start()
                for step in steps:
                    fold_copy(step).start()

        @pl.when(j == LT - 1)
        def _():
            list_1.wait_recv()
            list_2.wait_recv()
            to_smem.start()

        cur = lax.rem(j, 2)
        nxt = 1 - cur
        after = jnp.minimum(j + 1, LT - 1)
        inside = jnp.where(j < LT - 1, 1.0, 0.0)

        def roll_next(b):
            rows = slice(b * 8, b * 8 + 8)
            value = pltpu.roll(d_v[after, rows, :].astype(F32) * inside, 127, 1)
            pltpu.store(d_rolled.at[cur, rows, :], value, mask=is_last)
            pltpu.store(d_rolled.at[nxt, rows, :], value, mask=not_last)
            for n in range(8):
                value = pltpu.roll(c_v[after, n // LEV, n % LEV, rows, :], 127, 1)
                pltpu.store(c_rolled.at[cur, n, rows, :], value, mask=is_last)
                pltpu.store(c_rolled.at[nxt, n, rows, :], value, mask=not_last)

        def fluxes(b):
            rows = slice(b * 8, b * 8 + 8)
            ahead = slice(b * 8 + 1, b * 8 + 9)
            store = slice(b * 8 + 8, b * 8 + 16)
            behind = slice(b * 8 + 7, b * 8 + 15)
            own = d_v[j, rows, :].astype(F32)
            open_e = jnp.minimum(own, d_rolled[cur, rows, :])
            open_n = jnp.minimum(own, d_v[j, ahead, :].astype(F32))
            for k in range(LEV):
                e_far, e_near = face(open_e, k, u_v[j, k, rows, :])
                n_far, n_near = face(open_n, k, v_v[j, k, rows, :])
                for t in range(2):
                    n = t * LEV + k
                    c = c_v[j, t, k, rows, :]
                    east = c_rolled[cur, n, rows, :] * e_far - c * e_near
                    east_rolled = pltpu.roll(east, 1, 1)
                    pltpu.store(h_west.at[cur, n, rows, :], east_rolled, mask=not_first)
                    pltpu.store(h_west.at[nxt, n, rows, :], east_rolled, mask=is_first)
                    north = c_v[j, t, k, ahead, :] * n_far - c * n_near
                    h_north[n, store, :] = north
                    part[n, rows, :] = (c + east) + (north - h_north[n, behind, :])

        def finish(b):
            rows = slice(b * 8, b * 8 + 8)
            for n in range(8):
                interim[j, n, rows, :] = part[n, rows, :] - h_west[cur, n, rows, :]

        for b in range(NB + 6):
            if b < NB:
                roll_next(b)
            if 0 <= b - 3 < NB:
                fluxes(b - 3)
            if 0 <= b - 6 < NB:
                finish(b - 6)
        return carry

    lax.fori_loop(0, LT, column, 0)

    for b in range(NB):
        rows = slice(b * 8, b * 8 + 8)
        d_first = jnp.broadcast_to(d_v[0, rows, :].astype(F32)[:, 0:1], (8, 128))
        d_last = jnp.broadcast_to(d_v[LT - 1, rows, :].astype(F32)[:, 127:128], (8, 128))
        first, last = d_first, d_last
        for n in range(8):
            t, k = n // LEV, n % LEV
            value = c_v[0, t, k, rows, :]
            first = jnp.where(lane == n, value if n == 0 else pltpu.roll(value, n, 1), first)
            last = jnp.where(lane == n, pltpu.roll(c_v[LT - 1, t, k, rows, :], n + 1, 1), last)
        for k in range(LEV):
            value = pltpu.roll(u_v[LT - 1, k, rows, :], 9 + k, 1)
            last = jnp.where(lane == 8 + k, value, last)
        last = jnp.where(jnp.logical_and(lane >= 12, lane < 16), pltpu.roll(last, 4, 1), last)
        pack_first[rows, :] = first
        pack_last[rows, :] = last
    to_west.start()
    to_east.start()

    own_packs = [
        pltpu.make_async_copy(src, dst, local_sem.at[3 + i])
        for i, (src, dst) in enumerate(
            ((pack_first, own_first), (pack_last, own_last), (pack_n, own_n), (pack_s, own_s))
        )
    ]
    give_depth = pltpu.make_async_copy(d_v.at[:, pl.ds(0, ROWS), :], depth_out, out_sem.at[LT + 1])
    give_depth.start()
    for c in own_packs:
        c.start()
    for i, (_, dst) in enumerate(planes):
        pltpu.make_async_copy(dst, dst, plane_sem.at[i]).wait()
    to_smem.wait()
    places = []
    for slot, column_id in enumerate((owned[0, 0, 0], lists_s[0, 0, 1], lists_s[1, 0, 2])):
        info[slot] = jnp.where(column_id >= 0, column_id - x * LT, -1)
        places.append(jnp.clip(column_id - x * LT, 0, LT - 1))

    def hook(i):
        @pl.when(jnp.logical_and(top, i == 4))
        def _():
            own_fold.wait()
            for step in steps:
                fold_arrival(step).wait_recv()
            fold_sibling(half).start()

    ice_tiles(
        places, (ue_v, un_v, mass_v, str_v, mask_v, d_v, u_v, v_v), con, st, rolled, res, hook
    )

    list_1.wait_send()
    list_2.wait_send()
    to_west.wait()
    to_east.wait()
    give_depth.wait()
    for c in own_packs + passed:
        c.wait()
    @pl.when(jnp.logical_not(bottom))
    def _():
        to_south.wait_send()
        to_north.wait_recv()

    @pl.when(jnp.logical_not(top))
    def _():
        to_north.wait_send()
        to_south.wait_recv()

    @pl.when(top)
    def _():
        for step in steps:
            fold_copy(step).wait_send()
        fold_sibling(half).wait_send()
        fold_sibling(1 - half).wait_recv()


def exchange_and_ice(n_lon, n_lat, *operands):
    anywhere = pl.BlockSpec(memory_space=pl.ANY)
    inside = pl.BlockSpec(memory_space=pltpu.VMEM)
    plane = pltpu.VMEM((LT, ROWS, 128), F32)
    column = jax.ShapeDtypeStruct((ROWS, 128), F32)
    rows = jax.ShapeDtypeStruct((24, COLS), F32)

    def body(*refs):
        exchange_kernel(n_lon, n_lat, *refs)

    return pl.pallas_call(
        body,
        name="exchange_and_ice",
        out_shape=(
            column,
            column,
            rows,
            rows,
            column,
            column,
            rows,
            rows,
            jax.ShapeDtypeStruct((2, n_lon // 2, LT + 1, 8, 128), F32),
            jax.ShapeDtypeStruct((LT, 8, ROWS, 128), F32),
            jax.ShapeDtypeStruct((LT, LEV, ROWS, 128), F32),
            jax.ShapeDtypeStruct((LT, ROWS, 128), I32),
            jax.ShapeDtypeStruct((2, ROWS, COLS), F32),
            jax.ShapeDtypeStruct((SLOTS, 2, TILE, TILE), F32),
            jax.ShapeDtypeStruct((SLOTS,), I32),
        ),
        in_specs=[pl.BlockSpec(memory_space=pltpu.HBM)] * 8,
        out_specs=(anywhere,) * 9
        + (inside,)
        + (anywhere,) * 3
        + (inside, pl.BlockSpec(memory_space=pltpu.SMEM)),
        scratch_shapes=[
            pltpu.VMEM((LT, 2, LEV, ROWS + 8, 128), F32),
            pltpu.VMEM((LT, LEV, ROWS, 128), F32),
            pltpu.VMEM((LT, LEV, ROWS, 128), F32),
            pltpu.VMEM((LT, ROWS + 8, 128), I32),
            plane,
            plane,
            plane,
            plane,
            pltpu.VMEM((LT, ROWS, 128), I32),
            pltpu.VMEM((2, LEV, 8, COLS), F32),
            pltpu.VMEM((3, LEV, 8, COLS), F32),
            pltpu.VMEM((2, 8, COLS), I32),
            pltpu.VMEM((2, 8, ROWS, 128), F32),
            pltpu.VMEM((2, ROWS, 128), F32),
            pltpu.VMEM((2, 8, ROWS, 128), F32),
            pltpu.VMEM((8, ROWS + 8, 128), F32),
            pltpu.VMEM((8, ROWS, 128), F32),
            pltpu.VMEM((ROWS, 128), F32),
            pltpu.VMEM((ROWS, 128), F32),
            pltpu.VMEM((24, COLS), F32),
            pltpu.VMEM((24, COLS), F32),
            pltpu.VMEM((LT + 1, 8, 128), F32),
            pltpu.VMEM((8, 128), I32),
            pltpu.VMEM((2, 8, 128), I32),
            pltpu.SMEM((2, 8, 128), I32),
            pltpu.SMEM((1, 1, SLOTS), I32),
            pltpu.VMEM((SLOTS, 6, TILE, TILE), F32),
            pltpu.VMEM((SLOTS, 5, TILE, TILE), F32),
            pltpu.VMEM((SLOTS, 4, TILE, TILE), F32),
            pltpu.SemaphoreType.DMA((4, LT)),
            pltpu.SemaphoreType.DMA((5,)),
            pltpu.SemaphoreType.DMA((6,)),
            pltpu.SemaphoreType.DMA((6,)),
            pltpu.SemaphoreType.DMA((n_lon // 2,)),
            pltpu.SemaphoreType.DMA((n_lon // 2 + 1,)),
            pltpu.SemaphoreType.DMA((7,)),
            pltpu.SemaphoreType.DMA((5,)),
            pltpu.SemaphoreType.DMA((LT + 2,)),
        ],
        compiler_params=pltpu.CompilerParams(
            collective_id=0, has_side_effects=True, vmem_limit_bytes=22 * 2**20
        ),
    )(*operands)


def ocean_kernel(
    n_lon,
    n_lat,
    partner,
    info,
    p_v,
    vm_v,
    d_v,
    ivel,
    he,
    hw,
    hs,
    hn,
    own_first,
    own_last,
    own_n,
    own_s,
    fold,
    res,
    out,
    out_ice,
    o_v,
    hs_v,
    hn_v,
    win,
    west_h,
    east_h,
    south_h,
    north_h,
    out_sem,
    sem,
):
    y = lax.axis_index("lat")
    top = y == n_lat - 1
    bottom = y == 0
    lane, row = iotas()
    lane16 = lax.broadcasted_iota(I32, (16, 128), 1)

    put_ice = pltpu.make_async_copy(ivel, out_ice, sem.at[0])

    def put(j):
        cols = slice(j * 128, j * 128 + 128)
        return pltpu.make_async_copy(o_v.at[j], out.at[:, :, :, cols], out_sem.at[j])

    def patch(slot):
        at = pl.multiple_of(jnp.clip(info[slot], 0, LT - 1) * 128, 128)
        return pltpu.make_async_copy(res.at[slot], out_ice.at[:, :, pl.ds(at, 128)], sem.at[1 + slot])

    put_ice.start()
    hn_v[...] = hn[...]
    hs_v[...] = hs[...]

    @pl.when(top)
    def _():
        base = partner[COLS - 1]
        tile0 = lax.div(base, 128)
        shift = lax.rem(base, 128)
        for m in range(LT + 1):
            t = lax.rem(tile0 + m, n_lon * LT)
            dev = lax.div(t, LT)
            j = lax.rem(t, LT)
            half, chip = lax.rem(dev, 2), lax.div(dev, 2)
            win[m, 0:8, :] = fold[half, chip, j]
            win[m, 8:9, :] = fold[half, chip, LT, pl.ds(j, 1), :]
        back = lax.rem(128 - shift, 128)
        values = []
        for m in range(LT):
            near = pltpu.roll(win[m], back, 1)
            far = pltpu.roll(win[m + 1], back, 1)
            values.append(jnp.where(lane16 < 128 - shift, near, far))
        for bit in (1, 2, 4, 8, 16, 32, 64):
            odd = (lane16 & bit) != 0
            values = [
                jnp.where(odd, pltpu.roll(value, bit, 1), pltpu.roll(value, 128 - bit, 1))
                for value in values
            ]
        for m in range(LT):
            at = (LT - 1 - m) * 128
            hn_v[0:8, at : at + 128] = values[m][0:8, :]
            hn_v[16:24, at : at + 128] = jnp.broadcast_to(values[m][8:9, :], (8, 128))

    @pl.when(bottom)
    def _():
        hs_v[...] = jnp.zeros((24, COLS), F32)

    level = (lane & 3).astype(F32)
    for b in range(NB):
        rows = slice(b * 8, b * 8 + 8)
        pack, own = hw[rows, :], own_first[rows, :]
        both = jnp.minimum(pltpu.roll(pack, 112, 1), pltpu.roll(own, 112, 1))
        far, near = face(both, level, pltpu.roll(pack, 120, 1))
        west_h[rows, :] = pack * near - own * far
        pack, own = he[rows, :], own_last[rows, :]
        both = jnp.minimum(pltpu.roll(pack, 112, 1), pltpu.roll(own, 112, 1))
        far, near = face(both, level, pltpu.roll(own, 120, 1))
        east_h[rows, :] = pack * far - own * near
    level = (row & 3).astype(F32)
    for j in range(LT):
        cols = slice(j * 128, j * 128 + 128)
        far, near = face(jnp.minimum(own_s[16:24, cols], hn_v[16:24, cols]), level, own_s[8:16, cols])
        north_h[:, cols] = hn_v[0:8, cols] * far - own_s[0:8, cols] * near
        far, near = face(jnp.minimum(own_n[16:24, cols], hs_v[16:24, cols]), level, hs_v[8:16, cols])
        south_h[:, cols] = hs_v[0:8, cols] * near - own_n[0:8, cols] * far

    def rhs(j, n, b):
        rows = slice(b * 8, b * 8 + 8)
        value = p_v[j, n, rows, :]
        if j == 0:
            west = west_h[rows, :] if n == 0 else pltpu.roll(west_h[rows, :], 128 - n, 1)
            value = value + jnp.where(lane == 0, west, 0.0)
        if j == LT - 1:
            value = value + jnp.where(lane == 127, pltpu.roll(east_h[rows, :], 127 - n, 1), 0.0)
        cols = slice(j * 128, j * 128 + 128)
        if b == 0:
            rim = jnp.broadcast_to(south_h[n : n + 1, cols], (8, 128))
            value = value + jnp.where(row == 0, rim, 0.0)
        if b == NB - 1:
            rim = jnp.broadcast_to(north_h[n : n + 1, cols], (8, 128))
            value = value + jnp.where(row == 7, rim, 0.0)
        return value

    for j in range(LT):
        if j == 2:
            put_ice.wait()
            for slot in range(SLOTS):

                @pl.when(info[slot] >= 0)
                def _(slot=slot):
                    patch(slot).start()

        for b in range(NB):
            rows = slice(b * 8, b * 8 + 8)
            own = d_v[j, rows, :]
            g = [jnp.where(own > k, vm_v[j, k, rows, :] * 0.25, 0.0) for k in range(LEV)]
            i0 = recip((1.0 + g[0]) + g[1])
            u0 = g[1] * i0
            i1 = recip((1.0 + g[1]) + g[2] - g[1] * u0)
            u1 = g[2] * i1
            i2 = recip((1.0 + g[2]) + g[3] - g[2] * u1)
            u2 = g[3] * i2
            i3 = recip((1.0 + g[3]) - g[3] * u2)
            for t in range(2):
                f = [rhs(j, t * LEV + k, b) for k in range(LEV)]
                r0 = f[0] * i0
                r1 = (f[1] + g[1] * r0) * i1
                r2 = (f[2] + g[2] * r1) * i2
                x3 = (f[3] + g[3] * r2) * i3
                x2 = r2 + u2 * x3
                x1 = r1 + u1 * x2
                x0 = r0 + u0 * x1
                for k, value in enumerate((x0, x1, x2, x3)):
                    o_v[j, t, k, rows, :] = value
        put(j).start()

    for j in range(LT):
        put(j).wait()
    for slot in range(SLOTS):

        @pl.when(info[slot] >= 0)
        def _(slot=slot):
            patch(slot).wait()


def ocean(n_lon, n_lat, *operands):
    anywhere = pl.BlockSpec(memory_space=pl.ANY)
    smem = pl.BlockSpec(memory_space=pltpu.SMEM)
    inside = pl.BlockSpec(memory_space=pltpu.VMEM)
    column = pltpu.VMEM((ROWS, 128), F32)
    rows = pltpu.VMEM((24, COLS), F32)

    def body(*refs):
        ocean_kernel(n_lon, n_lat, *refs)

    return pl.pallas_call(
        body,
        name="ocean",
        out_shape=(
            jax.ShapeDtypeStruct((2, LEV, ROWS, COLS), F32),
            jax.ShapeDtypeStruct((2, ROWS, COLS), F32),
        ),
        in_specs=[smem, smem] + [inside] * (len(operands) - 2),
        out_specs=(anywhere, anywhere),
        scratch_shapes=[
            pltpu.VMEM((LT, 2, LEV, ROWS, 128), F32),
            rows,
            rows,
            pltpu.VMEM((LT + 1, 16, 128), F32),
            column,
            column,
            pltpu.VMEM((8, COLS), F32),
            pltpu.VMEM((8, COLS), F32),
            pltpu.SemaphoreType.DMA((LT,)),
            pltpu.SemaphoreType.DMA((1 + SLOTS,)),
        ],
        compiler_params=pltpu.CompilerParams(vmem_limit_bytes=10 * 2**20),
    )(*operands)


def on_device(state, depth, vmix, partner, ivel, mass, strength, mask, owned):
    n_lon, n_lat = lax.axis_size("lon"), lax.axis_size("lat")
    in_hbm = [
        pltpu.with_memory_space_constraint(value, pltpu.HBM)
        for value in (owned, state, depth, ivel, mass, strength, mask, vmix)
    ]
    *rims, interim, vmix_in, depth_in, ivel_in, res, info = exchange_and_ice(n_lon, n_lat, *in_hbm)
    return ocean(n_lon, n_lat, partner, info, interim, vmix_in, depth_in, ivel_in, *rims, res)


def solution(mesh):
    return jax.shard_map(
        on_device,
        mesh=mesh,
        in_specs=(
            P(None, None, "lat", "lon"),
            P("lat", "lon"),
            P(None, "lat", "lon"),
            P("lon"),
            P(None, "lat", "lon"),
            P("lat", "lon"),
            P("lat", "lon"),
            P("lat", "lon"),
            P("lat", "lon", None),
        ),
        out_specs=(P(None, None, "lat", "lon"), P(None, "lat", "lon")),
        check_vma=False,
    )
```

```python
import jax
import jax.numpy as jnp
from jax import lax
from jax.experimental import pallas as pl
from jax.experimental.pallas import tpu as pltpu
from jax.sharding import PartitionSpec as P

MESH = pl.DeviceIdType.MESH
LEV = 4
TILE = 128
ROWS = 128
COLS = 1024
LT = COLS // TILE
SLOTS = 3
SUBCYCLES = 32
NB = ROWS // 8
F32 = jnp.float32
I32 = jnp.int32


def iotas():
    lane = lax.broadcasted_iota(I32, (8, 128), 1)
    row = lax.broadcasted_iota(I32, (8, 128), 0)
    return lane, row


def recip(value):
    r = pltpu.reciprocal(value, approx=True)
    return r * (2.0 - value * r)


def face(open_depth, level, velocity):
    is_open = open_depth > level
    z = jnp.where(is_open, velocity * 0.25, 0.0)
    e = jnp.where(is_open, 0.125, 0.0)
    far = e - jnp.minimum(z, 0.0)
    return far, far + z


def ice_tiles(places, planes, con, st, rolled, res_ref, hook):
    lane, row = iotas()
    not_first, not_last = lane != 0, lane != 127
    tiles = range(len(places))
    ue_v, un_v, mass_v, str_v, mask_v, depth_v, uo_v, vo_v = planes
    zeros = jnp.zeros((8, 128), F32)

    def at(k):
        return slice(k * 8, k * 8 + 8)

    def north(value):
        return jnp.where(row == 7, 0.0, pltpu.roll(value, 7, 0))

    def south(value):
        return jnp.where(row == 0, 0.0, pltpu.roll(value, 1, 0))

    def keep_east(t, f, k, value):
        pltpu.store(rolled.at[t, f, at(k), :], pltpu.roll(value, 127, 1), mask=not_last)

    def keep_west(t, f, k, value):
        pltpu.store(rolled.at[t, f, at(k), :], pltpu.roll(value, 1, 1), mask=not_first)

    for t in tiles:
        pos = places[t]
        for b in range(NB):
            rows = slice(b * 8, b * 8 + 8)
            spread = pl.ds((b % 2) * 64 + b // 2, 8, stride=8)
            mass, strength = mass_v[pos, rows, :], str_v[pos, rows, :]
            ice = jnp.logical_and(mask_v[pos, rows, :] > 0, depth_v[pos, rows, :] > 0)
            mass = jnp.where(ice, mass, 0.0)
            strength = jnp.where(ice, strength, 0.0)
            inertia = mass * 2.0
            diag = inertia + 1.0
            turn = mass * 0.5
            inv = 1.0 / (diag * diag + turn * turn)
            con[t, 0, spread, :] = inertia
            con[t, 1, spread, :] = diag * inv
            con[t, 2, spread, :] = turn * inv
            con[t, 3, spread, :] = strength * (1.0 / 12.0)
            con[t, 4, spread, :] = uo_v[pos, 0, rows, :] * 0.5
            con[t, 5, spread, :] = vo_v[pos, 0, rows, :] * 0.5
            st[t, 0, spread, :] = ue_v[pos, rows, :] * 0.5
            st[t, 1, spread, :] = un_v[pos, rows, :] * 0.5
            st[t, 2, spread, :] = strength * 0.25
    for t in tiles:
        for k in range(NB):
            for f in range(4):
                rolled[t, f, at(k), :] = zeros
    for t in tiles:
        for k in range(NB):
            p4 = st[t, 2, at(k), :]
            p_south = st[t, 2, at(k - 1), :] if k else south(st[t, 2, at(NB - 1), :])
            p_west = jnp.where(lane == 0, 0.0, pltpu.roll(p4, 1, 1))
            con[t, 4, at(k), :] = con[t, 4, at(k), :] - (p4 - p_west)
            con[t, 5, at(k), :] = con[t, 5, at(k), :] - (p4 - p_south)
            st[t, 3, at(k), :] = p4
            st[t, 4, at(k), :] = zeros
            keep_east(t, 0, k, st[t, 0, at(k), :])
            keep_east(t, 1, k, st[t, 1, at(k), :])

    keep = 1.0 / 1.5

    def stress(t, k):
        u, v = st[t, 0, at(k), :], st[t, 1, at(k), :]
        if k < NB - 1:
            un, vn = st[t, 0, at(k + 1), :], st[t, 1, at(k + 1), :]
        else:
            un, vn = north(st[t, 0, at(0), :]), north(st[t, 1, at(0), :])
        d1 = rolled[t, 0, at(k), :] - u
        d2 = vn - v
        h = (un - u) + (rolled[t, 1, at(k), :] - v)
        div = d1 + d2
        ten = d1 - d2
        p = div + div
        r = ten * 0.5
        q = con[t, 3, at(k), :] * lax.rsqrt((p * p + ten * ten) + (h * h + 0.25))
        sx = st[t, 2, at(k), :] * keep + q * (p + r)
        sy = st[t, 3, at(k), :] * keep + q * (p - r)
        sh = st[t, 4, at(k), :] * keep + q * h
        st[t, 2, at(k), :] = sx
        st[t, 3, at(k), :] = sy
        st[t, 4, at(k), :] = sh
        keep_west(t, 2, k, sx)
        keep_west(t, 3, k, sh)

    def momentum(t, k):
        u, v, sx, sy, sh = [st[t, f, at(k), :] for f in range(5)]
        if k:
            sy_s, sh_s = st[t, 3, at(k - 1), :], st[t, 4, at(k - 1), :]
        else:
            sy_s, sh_s = south(st[t, 3, at(NB - 1), :]), south(st[t, 4, at(NB - 1), :])
        inertia, al, be, kx, ky = [con[t, f, at(k), :] for f in (0, 1, 2, 4, 5)]
        rx = (inertia * u + kx) + ((sx - rolled[t, 2, at(k), :]) + (sh - sh_s))
        ry = (inertia * v + ky) + ((sh - rolled[t, 3, at(k), :]) + (sy - sy_s))
        u = al * rx + be * ry
        v = al * ry - be * rx
        st[t, 0, at(k), :] = u
        st[t, 1, at(k), :] = v
        keep_east(t, 0, k, u)
        keep_east(t, 1, k, v)

    def cycle(_, carry):
        for t in tiles:
            for k in range(NB):
                stress(t, k)
        for t in tiles:
            for k in range(NB):
                momentum(t, k)
        return carry

    def four(i, carry):
        hook(i)
        for _ in range(4):
            cycle(i, carry)
        return carry

    lax.fori_loop(0, SUBCYCLES // 4, four, 0)
    for t in tiles:
        for k in range(NB):
            res_ref[t, 0, pl.ds(k, 8, stride=NB), :] = st[t, 0, at(k), :] * 2.0
            res_ref[t, 1, pl.ds(k, 8, stride=NB), :] = st[t, 1, at(k), :] * 2.0


def exchange_kernel(
    n_lon,
    n_lat,
    owned_hbm,
    state,
    depth,
    ivel,
    mass,
    strength,
    mask,
    vmix,
    he,
    hw,
    hs,
    hn,
    own_first,
    own_last,
    own_n,
    own_s,
    fold,
    interim,
    vmix_out,
    depth_out,
    ivel_out,
    res,
    info,
    c_v,
    u_v,
    v_v,
    d_v,
    ue_v,
    un_v,
    mass_v,
    str_v,
    mask_v,
    blk_first,
    blk_last,
    d_rim,
    c_rolled,
    d_rolled,
    h_west,
    h_north,
    part,
    pack_first,
    pack_last,
    pack_n,
    pack_s,
    pack_f,
    my_list,
    lists,
    lists_s,
    owned,
    con,
    st,
    rolled,
    in_sem,
    plane_sem,
    send_sem,
    recv_sem,
    fsend_sem,
    frecv_sem,
    local_sem,
    rim_sem,
    out_sem,
):
    x = lax.axis_index("lon")
    y = lax.axis_index("lat")
    lane, row = iotas()
    is_last, not_last = lane == 127, lane != 127
    is_first, not_first = lane == 0, lane != 0
    top = y == n_lat - 1
    bottom = y == 0
    half = lax.rem(x, 2)
    chip = lax.div(x, 2)

    def lon(step):
        return {"lon": lax.rem(x + step + n_lon, n_lon), "lat": y}

    def lat(step):
        return {"lon": x, "lat": y + step}

    get_owned = pltpu.make_async_copy(owned_hbm, owned, local_sem.at[0])
    get_owned.start()
    barrier = pltpu.get_barrier_semaphore()

    def greet(device):
        pl.semaphore_signal(barrier, inc=1, device_id=device, device_id_type=MESH)

    for step in (1, -1, 2, -2):
        greet(lon(step))

    fold_extra = range(4, n_lon - 2, 2)

    @pl.when(top)
    def _():
        for step in fold_extra:
            greet(lon(step))

    @pl.when(jnp.logical_not(top))
    def _():
        greet(lat(1))

    @pl.when(jnp.logical_not(bottom))
    def _():
        greet(lat(-1))

    def barrier_wait():
        @pl.when(jnp.logical_and(top, jnp.logical_not(bottom)))
        def _():
            pl.semaphore_wait(barrier, 5 + len(fold_extra))

        @pl.when(jnp.logical_and(bottom, jnp.logical_not(top)))
        def _():
            pl.semaphore_wait(barrier, 5)

        @pl.when(jnp.logical_not(jnp.logical_or(bottom, top)))
        def _():
            pl.semaphore_wait(barrier, 6)

    def fetch(j):
        cols = pl.ds(pl.multiple_of(j * 128, 128), 128)
        rows = pl.ds(0, ROWS)
        return [
            pltpu.make_async_copy(state.at[0:2, :, :, cols], c_v.at[j, :, :, rows, :], in_sem.at[0, j]),
            pltpu.make_async_copy(depth.at[:, cols], d_v.at[j, rows, :], in_sem.at[1, j]),
            pltpu.make_async_copy(state.at[2, :, :, cols], u_v.at[j], in_sem.at[2, j]),
            pltpu.make_async_copy(state.at[3, :, :, cols], v_v.at[j], in_sem.at[3, j]),
        ]

    rims = [
        pltpu.make_async_copy(state.at[0:2, :, pl.ds(0, 8), :], blk_first, rim_sem.at[0]),
        pltpu.make_async_copy(state.at[0:2, :, pl.ds(ROWS - 8, 8), :], blk_last.at[0:2], rim_sem.at[1]),
        pltpu.make_async_copy(state.at[3, :, pl.ds(ROWS - 8, 8), :], blk_last.at[2], rim_sem.at[2]),
        pltpu.make_async_copy(depth.at[pl.ds(0, 8), :], d_rim.at[0], rim_sem.at[3]),
        pltpu.make_async_copy(depth.at[pl.ds(ROWS - 8, 8), :], d_rim.at[1], rim_sem.at[4]),
    ]
    for c in rims:
        c.start()
    for j in range(LT):
        for c in fetch(j):
            c.start()
    planes = [(ivel.at[0], ue_v), (ivel.at[1], un_v), (mass, mass_v), (strength, str_v), (mask, mask_v)]
    for i, (src, dst) in enumerate(planes):
        for j in range(LT):
            pltpu.make_async_copy(
                src.at[:, j * 128 : j * 128 + 128], dst.at[j], plane_sem.at[i]
            ).start()

    passed = [pltpu.make_async_copy(ivel, ivel_out, out_sem.at[LT])] + [
        pltpu.make_async_copy(vmix.at[:, :, j * 128 : j * 128 + 128], vmix_out.at[j], out_sem.at[j])
        for j in range(LT)
    ]
    for c in passed:
        c.start()

    get_owned.wait()
    my_list[...] = jnp.where(
        lane == 0, owned[0, 0, 0], jnp.where(lane == 1, owned[0, 0, 1], owned[0, 0, 2])
    )

    def remote(src, dst, i, device):
        return pltpu.make_async_remote_copy(
            src_ref=src,
            dst_ref=dst,
            send_sem=send_sem.at[i],
            recv_sem=recv_sem.at[i],
            device_id=device,
            device_id_type=MESH,
        )

    list_1 = remote(my_list, lists.at[0], 0, lon(-1))
    list_2 = remote(my_list, lists.at[1], 1, lon(-2))
    to_smem = pltpu.make_async_copy(lists, lists_s, local_sem.at[2])
    to_west = remote(pack_first, he, 2, lon(-1))
    to_east = remote(pack_last, hw, 3, lon(1))
    to_south = remote(pack_n, hn, 4, lat(-1))
    to_north = remote(pack_s, hs, 5, lat(1))

    zeros = jnp.zeros((8, 128), F32)
    beyond = slice(ROWS, ROWS + 8)
    for j in range(LT):
        d_v[j, beyond, :] = jnp.zeros((8, 128), I32)
        for n in range(8):
            c_v[j, n // LEV, n % LEV, beyond, :] = zeros
    for n in range(8):
        h_north[n, 0:8, :] = zeros
        for b in range(NB):
            h_west[0, n, b * 8 : b * 8 + 8, :] = zeros
    for c in rims:
        c.wait()
    for j in range(LT):
        cols = slice(j * 128, j * 128 + 128)
        d_n = d_rim[0, :, cols].astype(F32)[0:1, :]
        d_s = d_rim[1, :, cols].astype(F32)[7:8, :]
        for n in range(8):
            t, k = n // LEV, n % LEV
            pack_n[n : n + 1, cols] = blk_first[t, k, 0:1, cols]
            pack_s[n : n + 1, cols] = blk_last[t, k, 7:8, cols]
            pack_s[8 + n : 9 + n, cols] = blk_last[2, k, 7:8, cols]
        pack_n[8:16, cols] = zeros
        pack_n[16:24, cols] = jnp.broadcast_to(d_n, (8, 128))
        pack_s[16:24, cols] = jnp.broadcast_to(d_s, (8, 128))
        pack_f[j] = pack_s[0:8, cols]
        pack_f[LT, j : j + 1, :] = d_s

    steps = range(1, n_lon // 2)

    def fold_copy(step):
        return pltpu.make_async_remote_copy(
            src_ref=pack_f,
            dst_ref=fold.at[half, chip],
            send_sem=fsend_sem.at[step],
            recv_sem=frecv_sem.at[chip],
            device_id=lon(2 * step),
            device_id_type=MESH,
        )

    def fold_arrival(step):
        source = lax.rem(chip - step + n_lon // 2, n_lon // 2)
        return pltpu.make_async_remote_copy(
            src_ref=pack_f,
            dst_ref=fold.at[half, source],
            send_sem=fsend_sem.at[step],
            recv_sem=frecv_sem.at[source],
            device_id=lon(2 * step),
            device_id_type=MESH,
        )

    def fold_sibling(which):
        return pltpu.make_async_remote_copy(
            src_ref=fold.at[which],
            dst_ref=fold.at[which],
            send_sem=fsend_sem.at[0],
            recv_sem=frecv_sem.at[n_lon // 2],
            device_id=lon(1 - 2 * half),
            device_id_type=MESH,
        )

    own_fold = pltpu.make_async_copy(pack_f, fold.at[half, chip], local_sem.at[1])

    for c in fetch(0):
        c.wait()
    for b in range(NB):
        rows = slice(b * 8, b * 8 + 8)
        pltpu.store(
            d_rolled.at[0, rows, :], pltpu.roll(d_v[0, rows, :].astype(F32), 127, 1), mask=not_last
        )
        for n in range(8):
            value = pltpu.roll(c_v[0, n // LEV, n % LEV, rows, :], 127, 1)
            pltpu.store(c_rolled.at[0, n, rows, :], value, mask=not_last)

    def column(j, carry):
        @pl.when(j < LT - 1)
        def _():
            for c in fetch(j + 1):
                c.wait()

        @pl.when(j == 1)
        def _():
            barrier_wait()
            list_1.start()
            list_2.start()

            @pl.when(jnp.logical_not(bottom))
            def _():
                to_south.start()

            @pl.when(jnp.logical_not(top))
            def _():
                to_north.start()

            @pl.when(top)
            def _():
                own_fold.start()
                for step in steps:
                    fold_copy(step).start()

        @pl.when(j == LT - 1)
        def _():
            list_1.wait_recv()
            list_2.wait_recv()
            to_smem.start()

        cur = lax.rem(j, 2)
        nxt = 1 - cur
        after = jnp.minimum(j + 1, LT - 1)
        inside = jnp.where(j < LT - 1, 1.0, 0.0)

        def roll_next(b):
            rows = slice(b * 8, b * 8 + 8)
            value = pltpu.roll(d_v[after, rows, :].astype(F32) * inside, 127, 1)
            pltpu.store(d_rolled.at[cur, rows, :], value, mask=is_last)
            pltpu.store(d_rolled.at[nxt, rows, :], value, mask=not_last)
            for n in range(8):
                value = pltpu.roll(c_v[after, n // LEV, n % LEV, rows, :], 127, 1)
                pltpu.store(c_rolled.at[cur, n, rows, :], value, mask=is_last)
                pltpu.store(c_rolled.at[nxt, n, rows, :], value, mask=not_last)

        def fluxes(b):
            rows = slice(b * 8, b * 8 + 8)
            ahead = slice(b * 8 + 1, b * 8 + 9)
            store = slice(b * 8 + 8, b * 8 + 16)
            behind = slice(b * 8 + 7, b * 8 + 15)
            own = d_v[j, rows, :].astype(F32)
            open_e = jnp.minimum(own, d_rolled[cur, rows, :])
            open_n = jnp.minimum(own, d_v[j, ahead, :].astype(F32))
            for k in range(LEV):
                e_far, e_near = face(open_e, k, u_v[j, k, rows, :])
                n_far, n_near = face(open_n, k, v_v[j, k, rows, :])
                for t in range(2):
                    n = t * LEV + k
                    c = c_v[j, t, k, rows, :]
                    east = c_rolled[cur, n, rows, :] * e_far - c * e_near
                    east_rolled = pltpu.roll(east, 1, 1)
                    pltpu.store(h_west.at[cur, n, rows, :], east_rolled, mask=not_first)
                    pltpu.store(h_west.at[nxt, n, rows, :], east_rolled, mask=is_first)
                    north = c_v[j, t, k, ahead, :] * n_far - c * n_near
                    h_north[n, store, :] = north
                    part[n, rows, :] = (c + east) + (north - h_north[n, behind, :])

        def finish(b):
            rows = slice(b * 8, b * 8 + 8)
            for n in range(8):
                interim[j, n, rows, :] = part[n, rows, :] - h_west[cur, n, rows, :]

        for b in range(NB + 6):
            if b < NB:
                roll_next(b)
            if 0 <= b - 3 < NB:
                fluxes(b - 3)
            if 0 <= b - 6 < NB:
                finish(b - 6)
        return carry

    lax.fori_loop(0, LT, column, 0)

    for b in range(NB):
        rows = slice(b * 8, b * 8 + 8)
        d_first = jnp.broadcast_to(d_v[0, rows, :].astype(F32)[:, 0:1], (8, 128))
        d_last = jnp.broadcast_to(d_v[LT - 1, rows, :].astype(F32)[:, 127:128], (8, 128))
        first, last = d_first, d_last
        for n in range(8):
            t, k = n // LEV, n % LEV
            value = c_v[0, t, k, rows, :]
            first = jnp.where(lane == n, value if n == 0 else pltpu.roll(value, n, 1), first)
            last = jnp.where(lane == n, pltpu.roll(c_v[LT - 1, t, k, rows, :], n + 1, 1), last)
        for k in range(LEV):
            value = pltpu.roll(u_v[LT - 1, k, rows, :], 9 + k, 1)
            last = jnp.where(lane == 8 + k, value, last)
        last = jnp.where(jnp.logical_and(lane >= 12, lane < 16), pltpu.roll(last, 4, 1), last)
        pack_first[rows, :] = first
        pack_last[rows, :] = last
    to_west.start()
    to_east.start()

    own_packs = [
        pltpu.make_async_copy(src, dst, local_sem.at[3 + i])
        for i, (src, dst) in enumerate(
            ((pack_first, own_first), (pack_last, own_last), (pack_n, own_n), (pack_s, own_s))
        )
    ]
    give_depth = pltpu.make_async_copy(d_v.at[:, pl.ds(0, ROWS), :], depth_out, out_sem.at[LT + 1])
    give_depth.start()
    for c in own_packs:
        c.start()
    for i, (_, dst) in enumerate(planes):
        pltpu.make_async_copy(dst, dst, plane_sem.at[i]).wait()
    to_smem.wait()
    places = []
    for slot, column_id in enumerate((owned[0, 0, 0], lists_s[0, 0, 1], lists_s[1, 0, 2])):
        info[slot] = jnp.where(column_id >= 0, column_id - x * LT, -1)
        places.append(jnp.clip(column_id - x * LT, 0, LT - 1))

    def hook(i):
        @pl.when(jnp.logical_and(top, i == 4))
        def _():
            own_fold.wait()
            for step in steps:
                fold_arrival(step).wait_recv()
            fold_sibling(half).start()

    ice_tiles(
        places, (ue_v, un_v, mass_v, str_v, mask_v, d_v, u_v, v_v), con, st, rolled, res, hook
    )

    list_1.wait_send()
    list_2.wait_send()
    to_west.wait()
    to_east.wait()
    give_depth.wait()
    for c in own_packs + passed:
        c.wait()
    @pl.when(jnp.logical_not(bottom))
    def _():
        to_south.wait_send()
        to_north.wait_recv()

    @pl.when(jnp.logical_not(top))
    def _():
        to_north.wait_send()
        to_south.wait_recv()

    @pl.when(top)
    def _():
        for step in steps:
            fold_copy(step).wait_send()
        fold_sibling(half).wait_send()
        fold_sibling(1 - half).wait_recv()


def exchange_and_ice(n_lon, n_lat, *operands):
    anywhere = pl.BlockSpec(memory_space=pl.ANY)
    inside = pl.BlockSpec(memory_space=pltpu.VMEM)
    plane = pltpu.VMEM((LT, ROWS, 128), F32)
    column = jax.ShapeDtypeStruct((ROWS, 128), F32)
    rows = jax.ShapeDtypeStruct((24, COLS), F32)

    def body(*refs):
        exchange_kernel(n_lon, n_lat, *refs)

    return pl.pallas_call(
        body,
        name="exchange_and_ice",
        out_shape=(
            column,
            column,
            rows,
            rows,
            column,
            column,
            rows,
            rows,
            jax.ShapeDtypeStruct((2, n_lon // 2, LT + 1, 8, 128), F32),
            jax.ShapeDtypeStruct((LT, 8, ROWS, 128), F32),
            jax.ShapeDtypeStruct((LT, LEV, ROWS, 128), F32),
            jax.ShapeDtypeStruct((LT, ROWS, 128), I32),
            jax.ShapeDtypeStruct((2, ROWS, COLS), F32),
            jax.ShapeDtypeStruct((SLOTS, 2, TILE, TILE), F32),
            jax.ShapeDtypeStruct((SLOTS,), I32),
        ),
        in_specs=[pl.BlockSpec(memory_space=pltpu.HBM)] * 8,
        out_specs=(anywhere,) * 9
        + (inside,)
        + (anywhere,) * 3
        + (inside, pl.BlockSpec(memory_space=pltpu.SMEM)),
        scratch_shapes=[
            pltpu.VMEM((LT, 2, LEV, ROWS + 8, 128), F32),
            pltpu.VMEM((LT, LEV, ROWS, 128), F32),
            pltpu.VMEM((LT, LEV, ROWS, 128), F32),
            pltpu.VMEM((LT, ROWS + 8, 128), I32),
            plane,
            plane,
            plane,
            plane,
            pltpu.VMEM((LT, ROWS, 128), I32),
            pltpu.VMEM((2, LEV, 8, COLS), F32),
            pltpu.VMEM((3, LEV, 8, COLS), F32),
            pltpu.VMEM((2, 8, COLS), I32),
            pltpu.VMEM((2, 8, ROWS, 128), F32),
            pltpu.VMEM((2, ROWS, 128), F32),
            pltpu.VMEM((2, 8, ROWS, 128), F32),
            pltpu.VMEM((8, ROWS + 8, 128), F32),
            pltpu.VMEM((8, ROWS, 128), F32),
            pltpu.VMEM((ROWS, 128), F32),
            pltpu.VMEM((ROWS, 128), F32),
            pltpu.VMEM((24, COLS), F32),
            pltpu.VMEM((24, COLS), F32),
            pltpu.VMEM((LT + 1, 8, 128), F32),
            pltpu.VMEM((8, 128), I32),
            pltpu.VMEM((2, 8, 128), I32),
            pltpu.SMEM((2, 8, 128), I32),
            pltpu.SMEM((1, 1, SLOTS), I32),
            pltpu.VMEM((SLOTS, 6, TILE, TILE), F32),
            pltpu.VMEM((SLOTS, 5, TILE, TILE), F32),
            pltpu.VMEM((SLOTS, 4, TILE, TILE), F32),
            pltpu.SemaphoreType.DMA((4, LT)),
            pltpu.SemaphoreType.DMA((5,)),
            pltpu.SemaphoreType.DMA((6,)),
            pltpu.SemaphoreType.DMA((6,)),
            pltpu.SemaphoreType.DMA((n_lon // 2,)),
            pltpu.SemaphoreType.DMA((n_lon // 2 + 1,)),
            pltpu.SemaphoreType.DMA((7,)),
            pltpu.SemaphoreType.DMA((5,)),
            pltpu.SemaphoreType.DMA((LT + 2,)),
        ],
        compiler_params=pltpu.CompilerParams(
            collective_id=0, has_side_effects=True, vmem_limit_bytes=22 * 2**20
        ),
    )(*operands)


def ocean_kernel(
    n_lon,
    n_lat,
    partner,
    info,
    p_v,
    vm_v,
    d_v,
    ivel,
    he,
    hw,
    hs,
    hn,
    own_first,
    own_last,
    own_n,
    own_s,
    fold,
    res,
    out,
    out_ice,
    o_v,
    hs_v,
    hn_v,
    win,
    west_h,
    east_h,
    south_h,
    north_h,
    out_sem,
    sem,
):
    y = lax.axis_index("lat")
    top = y == n_lat - 1
    bottom = y == 0
    lane, row = iotas()
    lane16 = lax.broadcasted_iota(I32, (16, 128), 1)

    put_ice = pltpu.make_async_copy(ivel, out_ice, sem.at[0])

    def put(j):
        cols = slice(j * 128, j * 128 + 128)
        return pltpu.make_async_copy(o_v.at[j], out.at[:, :, :, cols], out_sem.at[j])

    def patch(slot):
        at = pl.multiple_of(jnp.clip(info[slot], 0, LT - 1) * 128, 128)
        return pltpu.make_async_copy(res.at[slot], out_ice.at[:, :, pl.ds(at, 128)], sem.at[1 + slot])

    put_ice.start()
    hn_v[...] = hn[...]
    hs_v[...] = hs[...]

    @pl.when(top)
    def _():
        base = partner[COLS - 1]
        tile0 = lax.div(base, 128)
        shift = lax.rem(base, 128)
        for m in range(LT + 1):
            t = lax.rem(tile0 + m, n_lon * LT)
            dev = lax.div(t, LT)
            j = lax.rem(t, LT)
            half, chip = lax.rem(dev, 2), lax.div(dev, 2)
            win[m, 0:8, :] = fold[half, chip, j]
            win[m, 8:9, :] = fold[half, chip, LT, pl.ds(j, 1), :]
        back = lax.rem(128 - shift, 128)
        values = []
        for m in range(LT):
            near = pltpu.roll(win[m], back, 1)
            far = pltpu.roll(win[m + 1], back, 1)
            values.append(jnp.where(lane16 < 128 - shift, near, far))
        for bit in (1, 2, 4, 8, 16, 32, 64):
            odd = (lane16 & bit) != 0
            values = [
                jnp.where(odd, pltpu.roll(value, bit, 1), pltpu.roll(value, 128 - bit, 1))
                for value in values
            ]
        for m in range(LT):
            at = (LT - 1 - m) * 128
            hn_v[0:8, at : at + 128] = values[m][0:8, :]
            hn_v[16:24, at : at + 128] = jnp.broadcast_to(values[m][8:9, :], (8, 128))

    @pl.when(bottom)
    def _():
        hs_v[...] = jnp.zeros((24, COLS), F32)

    level = (lane & 3).astype(F32)
    for b in range(NB):
        rows = slice(b * 8, b * 8 + 8)
        pack, own = hw[rows, :], own_first[rows, :]
        both = jnp.minimum(pltpu.roll(pack, 112, 1), pltpu.roll(own, 112, 1))
        far, near = face(both, level, pltpu.roll(pack, 120, 1))
        west_h[rows, :] = pack * near - own * far
        pack, own = he[rows, :], own_last[rows, :]
        both = jnp.minimum(pltpu.roll(pack, 112, 1), pltpu.roll(own, 112, 1))
        far, near = face(both, level, pltpu.roll(own, 120, 1))
        east_h[rows, :] = pack * far - own * near
    level = (row & 3).astype(F32)
    for j in range(LT):
        cols = slice(j * 128, j * 128 + 128)
        far, near = face(jnp.minimum(own_s[16:24, cols], hn_v[16:24, cols]), level, own_s[8:16, cols])
        north_h[:, cols] = hn_v[0:8, cols] * far - own_s[0:8, cols] * near
        far, near = face(jnp.minimum(own_n[16:24, cols], hs_v[16:24, cols]), level, hs_v[8:16, cols])
        south_h[:, cols] = hs_v[0:8, cols] * near - own_n[0:8, cols] * far

    def rhs(j, n, b):
        rows = slice(b * 8, b * 8 + 8)
        value = p_v[j, n, rows, :]
        if j == 0:
            west = west_h[rows, :] if n == 0 else pltpu.roll(west_h[rows, :], 128 - n, 1)
            value = value + jnp.where(lane == 0, west, 0.0)
        if j == LT - 1:
            value = value + jnp.where(lane == 127, pltpu.roll(east_h[rows, :], 127 - n, 1), 0.0)
        cols = slice(j * 128, j * 128 + 128)
        if b == 0:
            rim = jnp.broadcast_to(south_h[n : n + 1, cols], (8, 128))
            value = value + jnp.where(row == 0, rim, 0.0)
        if b == NB - 1:
            rim = jnp.broadcast_to(north_h[n : n + 1, cols], (8, 128))
            value = value + jnp.where(row == 7, rim, 0.0)
        return value

    for j in range(LT):
        if j == 2:
            put_ice.wait()
            for slot in range(SLOTS):

                @pl.when(info[slot] >= 0)
                def _(slot=slot):
                    patch(slot).start()

        for b in range(NB):
            rows = slice(b * 8, b * 8 + 8)
            own = d_v[j, rows, :]
            g = [jnp.where(own > k, vm_v[j, k, rows, :] * 0.25, 0.0) for k in range(LEV)]
            i0 = recip((1.0 + g[0]) + g[1])
            u0 = g[1] * i0
            i1 = recip((1.0 + g[1]) + g[2] - g[1] * u0)
            u1 = g[2] * i1
            i2 = recip((1.0 + g[2]) + g[3] - g[2] * u1)
            u2 = g[3] * i2
            i3 = recip((1.0 + g[3]) - g[3] * u2)
            for t in range(2):
                f = [rhs(j, t * LEV + k, b) for k in range(LEV)]
                r0 = f[0] * i0
                r1 = (f[1] + g[1] * r0) * i1
                r2 = (f[2] + g[2] * r1) * i2
                x3 = (f[3] + g[3] * r2) * i3
                x2 = r2 + u2 * x3
                x1 = r1 + u1 * x2
                x0 = r0 + u0 * x1
                for k, value in enumerate((x0, x1, x2, x3)):
                    o_v[j, t, k, rows, :] = value
        put(j).start()

    for j in range(LT):
        put(j).wait()
    for slot in range(SLOTS):

        @pl.when(info[slot] >= 0)
        def _(slot=slot):
            patch(slot).wait()


def ocean(n_lon, n_lat, *operands):
    anywhere = pl.BlockSpec(memory_space=pl.ANY)
    smem = pl.BlockSpec(memory_space=pltpu.SMEM)
    inside = pl.BlockSpec(memory_space=pltpu.VMEM)
    column = pltpu.VMEM((ROWS, 128), F32)
    rows = pltpu.VMEM((24, COLS), F32)

    def body(*refs):
        ocean_kernel(n_lon, n_lat, *refs)

    return pl.pallas_call(
        body,
        name="ocean",
        out_shape=(
            jax.ShapeDtypeStruct((2, LEV, ROWS, COLS), F32),
            jax.ShapeDtypeStruct((2, ROWS, COLS), F32),
        ),
        in_specs=[smem, smem] + [inside] * (len(operands) - 2),
        out_specs=(anywhere, anywhere),
        scratch_shapes=[
            pltpu.VMEM((LT, 2, LEV, ROWS, 128), F32),
            rows,
            rows,
            pltpu.VMEM((LT + 1, 16, 128), F32),
            column,
            column,
            pltpu.VMEM((8, COLS), F32),
            pltpu.VMEM((8, COLS), F32),
            pltpu.SemaphoreType.DMA((LT,)),
            pltpu.SemaphoreType.DMA((1 + SLOTS,)),
        ],
        compiler_params=pltpu.CompilerParams(vmem_limit_bytes=10 * 2**20),
    )(*operands)


def on_device(state, depth, vmix, partner, ivel, mass, strength, mask, owned):
    n_lon, n_lat = lax.axis_size("lon"), lax.axis_size("lat")
    in_hbm = [
        pltpu.with_memory_space_constraint(value, pltpu.HBM)
        for value in (owned, state, depth, ivel, mass, strength, mask, vmix)
    ]
    *rims, interim, vmix_in, depth_in, ivel_in, res, info = exchange_and_ice(n_lon, n_lat, *in_hbm)
    return ocean(n_lon, n_lat, partner, info, interim, vmix_in, depth_in, ivel_in, *rims, res)


def solution(mesh):
    return jax.shard_map(
        on_device,
        mesh=mesh,
        in_specs=(
            P(None, None, "lat", "lon"),
            P("lat", "lon"),
            P(None, "lat", "lon"),
            P("lon"),
            P(None, "lat", "lon"),
            P("lat", "lon"),
            P("lat", "lon"),
            P("lat", "lon"),
            P("lat", "lon", None),
        ),
        out_specs=(P(None, None, "lat", "lon"), P(None, "lat", "lon")),
        check_vma=False,
    )
```
